128 devices in a mesh: lat: 32 (over z, x_lo, y), grp: 4 (over x_hi, core).
Axes of the slice: x: 4 (x_hi: 2, x_lo: 2; x = x_hi * 2 + x_lo), y: 4, z: 4, core: 2. Of those that a mesh axis runs over, the one named last changes fastest.
Arguments:
- tokens: bfloat16 [384, 256, 1024], P('grp', 'lat'), may hold values from -6 to 6
- cotangent: bfloat16 [384, 256, 1024], P('grp', 'lat'), may hold values from -6 to 6
- gain: float32 [384], P('grp'), may hold values from 0.5 to 1.5
- shift: float32 [384], P('grp'), may hold values from -3 to 3
- w_in: float32 [4, 2, 96, 96], P('grp'), may hold values from -0.4375 to 0.4375
- b_in: float32 [4, 2, 96], P('grp'), may hold values from -0.3 to 0.3
- w_out: float32 [4, 2, 96, 96], P('grp'), may hold values from -0.4375 to 0.4375
- b_out: float32 [4, 2, 96], P('grp'), may hold values from -0.12 to 0.12
Outputs:
- mixed: bfloat16 [384, 256, 1024], P('grp', 'lat')
- grad_tokens: bfloat16 [384, 256, 1024], P('grp', 'lat')
- grad_weights: float32 [4, 36864], P('grp', 'lat')
The draws below stay inside these ranges and needn't reach their ends.
All inputs are finite; a program needn't handle non-finite values.
Results may differ from the reference program's by a relative error of at most 0.012.
Values sent between devices are 32-bit elements; how exact they have to be, the bound alone decides.
No kernel may reach another device: no remote copies, remote signals or barrier semaphores. Data moves between devices by JAX's collectives and lax.ppermute only.
A program may use at most 128 MiB of HBM per device.

```python
import math
import jax
import jax.numpy as jnp
from jax import lax

BLOCK_SIZE = 96
LON = 1024
LAT_ROWS = 256
MODES = 512
BLOCKS = 4
WIDTH = 384


def block_levels(rng, dims, shards, low, high):
    factor_of = 1.0
    for axis_at, shards_of in shards:
        draws = jax.random.uniform(jax.random.fold_in(jax.random.fold_in(rng, 6), axis_at), (shards_of,), jnp.float32, low / len(shards), high / len(shards))
        factor_of = factor_of * jnp.repeat(jnp.exp(draws), dims[axis_at] // shards_of).reshape((-1,) + (1,) * (len(dims) - 1 - axis_at))
    return factor_of


def centred(own_key, dims, scale, limit, cuts=(), held_as=jnp.bfloat16):
    level = block_levels(own_key, dims, cuts, -0.22, 0.18) if cuts else 1.0
    values = jax.random.normal(own_key, dims, jnp.float32) * scale * level
    return jnp.minimum(jnp.maximum(values, -limit), limit).astype(held_as)


def setup_inputs(seed: int = 0) -> dict:
    streams_of = jax.random.split(jax.random.key(seed), 9)
    return {
        "tokens": centred(streams_of[0], (WIDTH, LAT_ROWS, LON), 1.0, 6.0, ((0, 4), (1, 32))),
        "cotangent": centred(streams_of[1], (WIDTH, LAT_ROWS, LON), 1.0, 6.0, ((0, 4), (1, 32))),
        "gain": jnp.clip(1.0 + 0.1 * jax.random.normal(streams_of[2], (WIDTH,), jnp.float32), 0.5, 1.5),
        "shift": centred(streams_of[3], (WIDTH,), 0.5, 3.0, ((0, 4),), jnp.float32),
        "w_in": centred(streams_of[4], (BLOCKS, 2, BLOCK_SIZE, BLOCK_SIZE), (2 * BLOCK_SIZE) ** -0.5, 0.4375, ((0, 4),), jnp.float32),
        "b_in": centred(streams_of[5], (BLOCKS, 2, BLOCK_SIZE), 0.05, 0.3, ((0, 4),), jnp.float32),
        "w_out": centred(streams_of[6], (BLOCKS, 2, BLOCK_SIZE, BLOCK_SIZE), (2 * BLOCK_SIZE) ** -0.5, 0.4375, ((0, 4),), jnp.float32),
        "b_out": centred(streams_of[7], (BLOCKS, 2, BLOCK_SIZE), 0.02, 0.12, ((0, 4),), jnp.float32),
    }


highest = lax.Precision.HIGHEST
shrink_level = 0.01
norm_eps = 1e-05

def complex_mix(left_real, left_imag, w_real, w_imag):
    form = 'ihk,io->ohk'
    out_real = jnp.einsum(form, left_real, w_real, precision=highest) - jnp.einsum(form, left_imag, w_imag, precision=highest)
    out_imag = jnp.einsum(form, left_imag, w_real, precision=highest) + jnp.einsum(form, left_real, w_imag, precision=highest)
    return (out_real, out_imag)

def shrink(value):
    return jnp.sign(value) * jnp.maximum(jnp.abs(value) - shrink_level, 0.0)

def spectral_filter(field, in_real, in_imag, out_real, out_imag, bias_in, bias_out):
    half = jnp.fft.rfft(field, axis=2, norm='ortho')[:, :, :MODES]
    spectrum = jnp.fft.fft(half, axis=1, norm='ortho')
    pre_real, pre_imag = complex_mix(jnp.real(spectrum), jnp.imag(spectrum), in_real, in_imag)
    act_real = jax.nn.relu(pre_real + bias_in[0][:, None, None])
    act_imag = jax.nn.relu(pre_imag + bias_in[1][:, None, None])
    post_real, post_imag = complex_mix(act_real, act_imag, out_real, out_imag)
    shrunk_real = shrink(post_real + bias_out[0][:, None, None])
    shrunk_imag = shrink(post_imag + bias_out[1][:, None, None])
    back = jnp.fft.ifft(lax.complex(shrunk_real, shrunk_imag), axis=1, norm='ortho')
    return jnp.fft.irfft(back, n=LON, axis=2, norm='ortho')

def per_block(items):
    field, grad_part, block_in, bias_in, block_out, bias_out = items

    def apply_filter(value, in_real, in_imag, out_real, out_imag):
        return spectral_filter(value, in_real, in_imag, out_real, out_imag, bias_in, bias_out)
    filtered, pullback = jax.vjp(apply_filter, field, block_in[0], block_in[1], block_out[0], block_out[1])
    d_field, g_in_real, g_in_imag, g_out_real, g_out_imag = pullback(grad_part)
    grads = jnp.stack([g_in_real, g_in_imag, g_out_real, g_out_imag]).reshape(-1)
    return (filtered, d_field, grads)

def reference(tokens, cotangent, gain, shift, w_in, b_in, w_out, b_out):
    tok_val = tokens.astype(jnp.float32)
    grad_val = cotangent.astype(jnp.float32)
    token_mean = lax.optimization_barrier(jnp.mean(tok_val, axis=0))
    square_mean = lax.optimization_barrier(jnp.mean(tok_val * tok_val, axis=0))
    inv_std = lax.rsqrt(square_mean - token_mean * token_mean + norm_eps)
    normed = (tok_val - token_mean) * inv_std
    normal_out = normed * gain[:, None, None] + shift[:, None, None]

    def shaped(value):
        return value.reshape(BLOCKS, BLOCK_SIZE, LAT_ROWS, LON)
    filtered, d_filter, grads = lax.map(per_block, (shaped(normal_out), shaped(grad_val), w_in, b_in, w_out, b_out))
    filtered = filtered.reshape(WIDTH, LAT_ROWS, LON)
    d_filter = d_filter.reshape(WIDTH, LAT_ROWS, LON)
    mixed = (filtered + normal_out + tok_val).astype(jnp.bfloat16)
    d_normal = grad_val + d_filter
    dnorm = d_normal * gain[:, None, None]
    back_one = lax.optimization_barrier(jnp.mean(dnorm, axis=0))
    back_two = lax.optimization_barrier(jnp.mean(dnorm * normed, axis=0))
    grad_tokens = (grad_val + inv_std * (dnorm - back_one - normed * back_two)).astype(jnp.bfloat16)
    grad_weights = grads * (1.0 / math.sqrt(LAT_ROWS * MODES))
    return (mixed, grad_tokens, grad_weights)
```

```python
import functools
import math

import jax
import jax.numpy as jnp
import ml_dtypes
import numpy as np
from jax import lax
from jax.experimental import pallas as pl
from jax.experimental.pallas import tpu as pltpu
from jax.sharding import PartitionSpec as P

shrink_level = 0.01
norm_eps = 1e-05
f32 = jnp.float32
bf16 = jnp.bfloat16

CH = 96
RW = 8
LON = 1024
HALF = 512
PEERS = 32
LANES = RW * CH
QB = 4
KB = 128
STEPS = 4
TILES = LANES // 128
WIRE_SHAPE = jax.ShapeDtypeStruct((PEERS, TILES, 32, 128), jnp.float32)


def host_split(table):
    high = table.astype(ml_dtypes.bfloat16)
    low = (table - high.astype(np.float64)).astype(ml_dtypes.bfloat16)
    return np.stack([high, low])


def lon_table():
    parts = []
    n = np.arange(HALF)
    for parity in range(2):
        m = 2 * np.arange(256) + parity
        theta = 2.0 * np.pi * ((m[:, None] * n[None, :]) % LON) / LON
        table = np.stack([np.cos(theta), -np.sin(theta)], axis=1).reshape(HALF, HALF)
        parts.append(host_split(table / 32.0))
    return np.stack(parts)


def lat_table():
    parts = []
    row = np.arange(RW)[:, None]
    peer = np.arange(16)[None, :]
    place = (8 * peer + row).reshape(-1)
    for parity in range(2):
        k = 2 * np.arange(KB) + parity
        theta = 2.0 * np.pi * ((k[:, None] * place[None, :]) % 256) / 256
        c, s = np.cos(theta), np.sin(theta)
        table = np.concatenate(
            [np.concatenate([c, s], axis=1), np.concatenate([-s, c], axis=1)], axis=0
        )
        parts.append(host_split(table / 16.0))
    return np.stack(parts)


def split(value):
    high = value.astype(bf16)
    low = (value - high.astype(f32)).astype(bf16)
    return high, low


def dot(left, right, dims=((1,), (0,))):
    return lax.dot_general(left, right, (dims, ((), ())), preferred_element_type=f32)


NT = ((1,), (1,))
TN = ((0,), (0,))


def dot3(left, right, dims=((1,), (0,))):
    return (
        dot(left[0], right[0], dims) + dot(left[0], right[1], dims) + dot(left[1], right[0], dims)
    )


def fill_halves(rows_ref, halves_ref, gain_ref):
    for r in range(RW):
        own = jnp.concatenate(
            [rows_ref[tile, pl.ds(r, CH, stride=RW), :] for tile in range(8)], axis=1
        )
        if gain_ref is not None:
            own = own * gain_ref[...]
        first, second = own[:, :HALF], own[:, HALF:]
        at = pl.ds(r * CH, CH)
        for parity, value in enumerate((first + second, first - second)):
            high, low = split(value)
            halves_ref[parity, 0, at, :] = high
            halves_ref[parity, 1, at, :] = low


def put_tiles(out_ref, value):
    for tile in range(TILES):
        out_ref[:, tile] = value[:, tile * 128 : tile * 128 + 128].reshape(16, 32, 128)


def lon_grad_kernel(x_ref, tab_ref, out_ref, rows_ref, halves_ref):
    parity = pl.program_id(0)

    @pl.when(parity == 0)
    def _():
        for tile in range(8):
            value = x_ref[:, :, tile * 128 : tile * 128 + 128].astype(f32) * 2.0
            rows_ref[tile] = value.reshape(LANES, 128)
        fill_halves(rows_ref, halves_ref, None)

    table = (tab_ref[0, 0], tab_ref[0, 1])
    put_tiles(out_ref, dot3(table, (halves_ref[parity, 0], halves_ref[parity, 1]), NT))

    @pl.when(parity == 0)
    def _():
        out_ref[0, :, 0:2, :] = out_ref[0, :, 0:2, :] * 0.5


def lon_field_kernel(x_ref, stat_ref, gain_ref, shift_ref, tab_ref, out_ref, rows_ref, halves_ref):
    parity = pl.program_id(0)

    @pl.when(parity == 0)
    def _():
        for tile in range(8):
            lanes = slice(tile * 128, tile * 128 + 128)
            value = x_ref[:, :, lanes].astype(f32)
            value = (value - stat_ref[0, :, lanes][None]) * stat_ref[1, :, lanes][None]
            rows_ref[tile] = value.reshape(LANES, 128)
        fill_halves(rows_ref, halves_ref, gain_ref)

    table = (tab_ref[0, 0], tab_ref[0, 1])
    put_tiles(out_ref, dot3(table, (halves_ref[parity, 0], halves_ref[parity, 1]), NT))

    @pl.when(parity == 0)
    def _():
        for tile in range(TILES):
            out_ref[0, tile, 0:1, :] = out_ref[0, tile, 0:1, :] + shift_ref[tile] * 32.0


def lon_forward_call(kernel, name, small_specs):
    return pl.pallas_call(
        kernel,
        name=name,
        grid=(2,),
        in_specs=[pl.BlockSpec((CH, RW, LON), lambda i: (0, 0, 0))]
        + small_specs
        + [pl.BlockSpec((1, 2, HALF, HALF), lambda i: (i, 0, 0, 0))],
        out_specs=pl.BlockSpec((16, TILES, 32, 128), lambda i: (i, 0, 0, 0)),
        out_shape=WIRE_SHAPE,
        scratch_shapes=[
            pltpu.VMEM((8, LANES, 128), f32),
            pltpu.VMEM((2, 2, LANES, HALF), bf16),
        ],
        compiler_params=pltpu.CompilerParams(vmem_limit_bytes=40 * 2**20),
        cost_estimate=pl.CostEstimate(
            flops=6 * LANES * LON * LON, bytes_accessed=7 * 2**20, transcendentals=0
        ),
    )


def unpack_rows(block_ref, halves_ref):
    lane = lax.broadcasted_iota(jnp.int32, (16, 128), 1)
    for q in range(QB):
        for part in range(2):
            own = [
                block_ref[pl.ds(tile * 8 + 2 * q + part, PEERS, stride=TILES * 8), :]
                for tile in range(TILES)
            ]
            first, second = [v[0:16] for v in own], [v[16:32] for v in own]
            sums = [a + b for a, b in zip(first, second)]
            differences = [a - b for a, b in zip(first, second)]
            for parity, value in enumerate((sums, differences)):
                for r in range(RW):
                    tile, skip = divmod(r * CH, 128)
                    piece = value[tile]
                    if skip:
                        piece = pltpu.roll(piece, 128 - skip, 1)
                    if skip + CH > 128:
                        after = pltpu.roll(value[tile + 1], 128 - skip, 1)
                        piece = jnp.where(lane < 128 - skip, piece, after)
                    high, low = split(piece)
                    at = (pl.ds((part * RW + r) * 16, 16), pl.ds(q * 128, 128))
                    halves_ref[(parity, 0) + at] = high
                    halves_ref[(parity, 1) + at] = low


def pack_rows(even, odd, block_ref):
    lane = lax.broadcasted_iota(jnp.int32, (16, 128), 1)
    for q in range(QB):
        for part in range(2):
            e = [even[(part * RW + r) * 16 : (part * RW + r + 1) * 16, q * 128 : q * 128 + 128] for r in range(RW)]
            o = [odd[(part * RW + r) * 16 : (part * RW + r + 1) * 16, q * 128 : q * 128 + 128] for r in range(RW)]
            for side in range(2):
                y = [a + b if side == 0 else a - b for a, b in zip(e, o)]
                for tile in range(TILES):
                    out = None
                    for r in range(RW):
                        low = r * CH - tile * 128
                        if low >= 128 or low + CH <= 0:
                            continue
                        piece = y[r] if low == 0 else pltpu.roll(y[r], low % 128, 1)
                        if out is None:
                            out = piece
                        else:
                            out = jnp.where(lane < low, out, piece)
                    start = (side * 16 * TILES + tile) * 8 + 2 * q + part
                    block_ref[pl.ds(start, 16, stride=TILES * 8), :] = out


def by_frequency(even, odd):
    rows = []
    for q in range(QB):
        for value in (even, odd):
            lanes = slice(q * 128, q * 128 + 128)
            rows.append(jnp.concatenate([value[0:KB, lanes], value[KB : 2 * KB, lanes]], axis=1))
    return jnp.concatenate(rows, axis=0)


def by_part(rows):
    out = []
    for parity in range(2):
        parts = []
        for part in range(2):
            lanes = slice(part * 128, part * 128 + 128)
            parts.append(
                jnp.concatenate(
                    [rows[(2 * q + parity) * KB : (2 * q + parity + 1) * KB, lanes] for q in range(QB)],
                    axis=1,
                )
            )
        out.append(jnp.concatenate(parts, axis=0))
    return out


def lat_forward(block_ref, tab_ref, halves_ref):
    unpack_rows(block_ref, halves_ref)
    out = [
        dot3(
            (tab_ref[parity, 0], tab_ref[parity, 1]),
            (halves_ref[parity, 0], halves_ref[parity, 1]),
        )
        for parity in range(2)
    ]
    return by_frequency(out[0], out[1])


def lat_inverse(rows, tab_ref, block_ref):
    even, odd = by_part(rows)
    pack_rows(dot(tab_ref[0, 0], even, TN), dot(tab_ref[1, 0], odd, TN), block_ref)


def fill_weight(w_ref, out_ref):
    full = jnp.zeros((256, 256), f32)
    out_ref[...] = full
    real, imag = w_ref[0, 0], w_ref[0, 1]
    out_ref[0:CH, 0:CH] = real
    out_ref[0:CH, 128 : 128 + CH] = imag
    out_ref[128 : 128 + CH, 0:CH] = -imag
    out_ref[128 : 128 + CH, 128 : 128 + CH] = real


def fill_bias(b_ref, out_ref):
    out_ref[...] = jnp.zeros((8, 256), f32)
    out_ref[0:1, 0:CH] = b_ref[0, 0:1, :]
    out_ref[0:1, 128 : 128 + CH] = b_ref[0, 1:2, :]


def grad_modes_kernel(block_ref, tab_ref, out_ref, halves_ref):
    out_ref[...] = lat_forward(block_ref.reshape(PEERS * TILES * 8, 128), tab_ref, halves_ref)


def field_modes_kernel(
    block_ref, tab_ref, w_in_ref, b_in_ref, w_out_ref, b_out_ref,
    back_ref, spec_ref, act_ref, mask_ref,
    halves_ref, full_ref, weight_ref, bias_ref,
):
    @pl.when(pl.program_id(0) == 0)
    def _():
        for at, (w_ref, b_ref) in enumerate(((w_in_ref, b_in_ref), (w_out_ref, b_out_ref))):
            fill_weight(w_ref, full_ref)
            weight_ref[at, 0], weight_ref[at, 1] = split(full_ref[...])
            fill_bias(b_ref, bias_ref.at[at])

    spec = split(lat_forward(block_ref.reshape(PEERS * TILES * 8, 128), tab_ref, halves_ref))
    spec_ref[...] = spec[0]
    act = dot3(spec, (weight_ref[0, 0], weight_ref[0, 1])) + bias_ref[0, 0:1, :]
    act = split(jnp.maximum(act, 0.0))
    act_ref[...] = act[0]
    post = dot3(act, (weight_ref[1, 0], weight_ref[1, 1])) + bias_ref[1, 0:1, :]
    mask_ref[...] = jnp.where(jnp.abs(post) > shrink_level, 1.0, 0.0).astype(bf16)
    shrunk = post - jnp.clip(post, -shrink_level, shrink_level)
    lat_inverse(shrunk.astype(bf16), tab_ref, back_ref.reshape(PEERS * TILES * 8, 128))


def pull_modes_kernel(
    grad_ref, spec_ref, act_ref, mask_ref, tab_ref, w_in_ref, w_out_ref,
    back_ref, g_ref,
    full_ref, weight_ref, sum_ref,
):
    step = pl.program_id(0)

    @pl.when(step == 0)
    def _():
        for at, w_ref in enumerate((w_in_ref, w_out_ref)):
            fill_weight(w_ref, full_ref)
            weight_ref[at] = full_ref[...].astype(bf16)
        sum_ref[...] = jnp.zeros_like(sum_ref)

    spec, act = spec_ref[...], act_ref[...]
    d_post = jnp.where(mask_ref[...] > 0.5, grad_ref[...].astype(bf16), jnp.zeros((), bf16))
    sum_ref[1] += dot(act, d_post, TN)
    d_act = dot(d_post, weight_ref[1], NT)
    d_pre = jnp.where(act > 0, d_act.astype(bf16), jnp.zeros((), bf16))
    sum_ref[0] += dot(spec, d_pre, TN)
    d_spec = dot(d_pre, weight_ref[0], NT)
    lat_inverse(d_spec.astype(bf16), tab_ref, back_ref.reshape(PEERS * TILES * 8, 128))

    @pl.when(step == STEPS - 1)
    def _():
        scale = 1.0 / math.sqrt(131072.0)
        for at in range(2):
            total = sum_ref[at]
            rr, ri = total[0:CH, 0:CH], total[0:CH, 128 : 128 + CH]
            ir, ii = total[128 : 128 + CH, 0:CH], total[128 : 128 + CH, 128 : 128 + CH]
            g_ref[2 * at] = (rr + ii) * scale
            g_ref[2 * at + 1] = (ri - ir) * scale


WIRE = pl.BlockSpec((PEERS, TILES, 8, 128), lambda i: (0, 0, i, 0))
LAT_TAB = pl.BlockSpec((2, 2, 256, 256), lambda i: (0, 0, 0, 0))
MODES = pl.BlockSpec((1024, 256), lambda i: (i, 0))
WEIGHT = pl.BlockSpec((1, 2, CH, CH), lambda i: (0, 0, 0, 0))
BIAS = pl.BlockSpec((1, 2, CH), lambda i: (0, 0, 0))


def modes_shape(dtype):
    return jax.ShapeDtypeStruct((4096, 256), dtype)


def grad_modes(block, table):
    return pl.pallas_call(
        grad_modes_kernel,
        name="grad_modes",
        grid=(STEPS,),
        in_specs=[WIRE, LAT_TAB],
        out_specs=MODES,
        out_shape=modes_shape(f32),
        scratch_shapes=[pltpu.VMEM((2, 2, 256, QB * 128), bf16)],
        compiler_params=pltpu.CompilerParams(vmem_limit_bytes=40 * 2**20),
        cost_estimate=pl.CostEstimate(
            flops=6 * 2**31, bytes_accessed=8 * 2**20, transcendentals=0
        ),
    )(block, table)


def field_modes(block, table, w_in, b_in, w_out, b_out):
    return pl.pallas_call(
        field_modes_kernel,
        name="field_modes",
        grid=(STEPS,),
        in_specs=[WIRE, LAT_TAB, WEIGHT, BIAS, WEIGHT, BIAS],
        out_specs=[WIRE, MODES, MODES, MODES],
        out_shape=[WIRE_SHAPE, modes_shape(bf16), modes_shape(bf16), modes_shape(bf16)],
        scratch_shapes=[
            pltpu.VMEM((2, 2, 256, QB * 128), bf16),
            pltpu.VMEM((256, 256), f32),
            pltpu.VMEM((2, 2, 256, 256), bf16),
            pltpu.VMEM((2, 8, 256), f32),
        ],
        compiler_params=pltpu.CompilerParams(vmem_limit_bytes=48 * 2**20),
        cost_estimate=pl.CostEstimate(
            flops=12 * 2**31, bytes_accessed=14 * 2**20, transcendentals=0
        ),
    )(block, table, w_in, b_in, w_out, b_out)


def pull_modes(grad, spec, act, mask, table, w_in, w_out):
    return pl.pallas_call(
        pull_modes_kernel,
        name="pull_modes",
        grid=(STEPS,),
        in_specs=[MODES, MODES, MODES, MODES, LAT_TAB, WEIGHT, WEIGHT],
        out_specs=[WIRE, pl.BlockSpec((4, CH, CH), lambda i: (0, 0, 0))],
        out_shape=[WIRE_SHAPE, jax.ShapeDtypeStruct((4, CH, CH), f32)],
        scratch_shapes=[
            pltpu.VMEM((256, 256), f32),
            pltpu.VMEM((2, 256, 256), bf16),
            pltpu.VMEM((2, 256, 256), f32),
        ],
        compiler_params=pltpu.CompilerParams(vmem_limit_bytes=48 * 2**20),
        cost_estimate=pl.CostEstimate(
            flops=8 * 2**31, bytes_accessed=14 * 2**20, transcendentals=0
        ),
    )(grad, spec, act, mask, table, w_in, w_out)


def lon_inverse(block_ref, tab_ref, rows_ref, weighted):
    sides = []
    for parity in range(2):
        value = jnp.concatenate(
            [
                block_ref[pl.ds(parity * 16, 16), tile].reshape(HALF, 128)
                for tile in range(TILES)
            ],
            axis=1,
        )
        if weighted:
            value = value * 2.0
            if parity == 0:
                row = lax.broadcasted_iota(jnp.int32, (HALF, 1), 0)
                value = value * jnp.where(row == 0, 0.5, 1.0)
        sides.append(dot(value.astype(bf16), tab_ref[parity, 0], TN))
    first, second = sides[0] + sides[1], sides[0] - sides[1]
    for r in range(RW):
        at, rows = pl.ds(r, CH, stride=RW), slice(r * CH, (r + 1) * CH)
        for tile in range(4):
            lanes = slice(tile * 128, tile * 128 + 128)
            rows_ref[tile, at, :] = first[rows, lanes]
            rows_ref[4 + tile, at, :] = second[rows, lanes]


def mixed_kernel(block_ref, tab_ref, tok_ref, stat_ref, gain_ref, shift_ref, out_ref, rows_ref):
    lon_inverse(block_ref, tab_ref, rows_ref, True)
    for tile in range(8):
        lanes = slice(tile * 128, tile * 128 + 128)
        tok = tok_ref[:, :, lanes].astype(f32)
        normed = (tok - stat_ref[0, :, lanes][None]) * stat_ref[1, :, lanes][None]
        normal = normed * gain_ref[...] + shift_ref[...]
        filtered = rows_ref[tile].reshape(CH, RW, 128)
        out_ref[:, :, lanes] = (filtered + normal + tok).astype(bf16)


def pulled_kernel(block_ref, tab_ref, tok_ref, cot_ref, stat_ref, gain_ref, out_ref, sum_ref, rows_ref):
    lon_inverse(block_ref, tab_ref, rows_ref, False)
    for tile in range(8):
        lanes = slice(tile * 128, tile * 128 + 128)
        tok = tok_ref[:, :, lanes].astype(f32)
        normed = (tok - stat_ref[0, :, lanes][None]) * stat_ref[1, :, lanes][None]
        pulled = rows_ref[tile].reshape(CH, RW, 128)
        dnorm = (pulled + cot_ref[:, :, lanes].astype(f32)) * gain_ref[...]
        out_ref[:, :, lanes] = dnorm
        sum_ref[0, :, lanes] = jnp.sum(dnorm, axis=0)
        sum_ref[1, :, lanes] = jnp.sum(dnorm * normed, axis=0)


def whole_call(kernel, name, out_shape):
    return pl.pallas_call(
        kernel,
        name=name,
        out_shape=out_shape,
        scratch_shapes=[pltpu.VMEM((8, LANES, 128), f32)],
        compiler_params=pltpu.CompilerParams(vmem_limit_bytes=48 * 2**20),
        cost_estimate=pl.CostEstimate(
            flops=4 * LANES * LON * LON, bytes_accessed=10 * 2**20, transcendentals=0
        ),
    )


def exchange(value):
    return lax.all_to_all(value, "lat", split_axis=0, concat_axis=0, tiled=True)


def sum_groups(value):
    return jnp.sum(lax.all_gather(value, "grp"), axis=0)


def per_device(tokens, cotangent, gain, shift, w_in, b_in, w_out, b_out):
    all_chans = CH * lax.axis_size("grp")
    lon_tab, lat_tab = jnp.asarray(lon_table()), jnp.asarray(lat_table())
    tok_val = tokens.astype(f32)
    sums = sum_groups(jnp.stack([jnp.sum(tok_val, axis=0), jnp.sum(tok_val * tok_val, axis=0)]))
    token_mean = sums[0] / all_chans
    inv_std = lax.rsqrt(sums[1] / all_chans - token_mean * token_mean + norm_eps)
    stats = jnp.stack([token_mean, inv_std])
    gain_col = gain.reshape(CH, 1)
    gain_cube = jnp.broadcast_to(gain.reshape(CH, 1, 1), (CH, 1, 128))
    shift_cube = jnp.broadcast_to(shift.reshape(CH, 1, 1), (CH, 1, 128))

    spec_grad = lon_forward_call(lon_grad_kernel, "lon_grad", [])(cotangent, lon_tab)
    modes_grad = exchange(spec_grad)
    small = [
        pl.BlockSpec((2, RW, LON), lambda i: (0, 0, 0)),
        pl.BlockSpec((CH, 1), lambda i: (0, 0)),
        pl.BlockSpec((TILES, 1, 128), lambda i: (0, 0, 0)),
    ]
    spec_field = lon_forward_call(lon_field_kernel, "lon_field", small)(
        tokens, stats, gain_col, jnp.tile(shift, RW).reshape(TILES, 1, 128), lon_tab
    )
    modes_field = exchange(spec_field)
    grad_rows = grad_modes(modes_grad, lat_tab)
    back_field, spec, act, mask = field_modes(modes_field, lat_tab, w_in, b_in, w_out, b_out)
    rows_field = exchange(back_field)
    back_grad, grads = pull_modes(grad_rows, spec, act, mask, lat_tab, w_in, w_out)
    rows_grad = exchange(back_grad)
    mixed = whole_call(mixed_kernel, "mixed", jax.ShapeDtypeStruct((CH, RW, LON), bf16))(
        rows_field, lon_tab, tokens, stats, gain_cube, shift_cube
    )
    dnorm, back = whole_call(
        pulled_kernel,
        "pulled",
        [jax.ShapeDtypeStruct((CH, RW, LON), f32), jax.ShapeDtypeStruct((2, RW, LON), f32)],
    )(rows_grad, lon_tab, tokens, cotangent, stats, gain_cube)
    back = sum_groups(back) / all_chans
    normed = (tok_val - token_mean) * inv_std
    grad_tokens = cotangent.astype(f32) + inv_std * (dnorm - back[0] - normed * back[1])
    shares = exchange(grads.reshape(PEERS, 1152))
    grad_weights = jnp.sum(shares, axis=0).reshape(1, 1152)
    return (mixed, grad_tokens.astype(bf16), grad_weights)


def solution(mesh):
    in_specs = (
        P("grp", "lat", None),
        P("grp", "lat", None),
        P("grp"),
        P("grp"),
        P("grp", None, None, None),
        P("grp", None, None),
        P("grp", None, None, None),
        P("grp", None, None),
    )
    out_specs = (P("grp", "lat", None), P("grp", "lat", None), P("grp", "lat"))
    return jax.shard_map(
        per_device, mesh=mesh, in_specs=in_specs, out_specs=out_specs, check_vma=False
    )
```

```python
import functools
import math

import jax
import jax.numpy as jnp
import ml_dtypes
import numpy as np
from jax import lax
from jax.experimental import pallas as pl
from jax.experimental.pallas import tpu as pltpu
from jax.sharding import PartitionSpec as P

shrink_level = 0.01
norm_eps = 1e-05
f32 = jnp.float32
bf16 = jnp.bfloat16

CH = 96
RW = 8
LON = 1024
HALF = 512
PEERS = 32
LANES = RW * CH
QB = 4
KB = 128
STEPS = 4
TILES = LANES // 128
WIRE_SHAPE = jax.ShapeDtypeStruct((PEERS, TILES, 32, 128), jnp.float32)


def host_split(table):
    high = table.astype(ml_dtypes.bfloat16)
    low = (table - high.astype(np.float64)).astype(ml_dtypes.bfloat16)
    return np.stack([high, low])


def lon_table():
    parts = []
    n = np.arange(HALF)
    for parity in range(2):
        m = 2 * np.arange(256) + parity
        theta = 2.0 * np.pi * ((m[:, None] * n[None, :]) % LON) / LON
        table = np.stack([np.cos(theta), -np.sin(theta)], axis=1).reshape(HALF, HALF)
        parts.append(host_split(table / 32.0))
    return np.stack(parts)


def lat_table():
    parts = []
    row = np.arange(RW)[:, None]
    peer = np.arange(16)[None, :]
    place = (8 * peer + row).reshape(-1)
    for parity in range(2):
        k = 2 * np.arange(KB) + parity
        theta = 2.0 * np.pi * ((k[:, None] * place[None, :]) % 256) / 256
        c, s = np.cos(theta), np.sin(theta)
        table = np.concatenate(
            [np.concatenate([c, s], axis=1), np.concatenate([-s, c], axis=1)], axis=0
        )
        parts.append(host_split(table / 16.0))
    return np.stack(parts)


def split(value):
    high = value.astype(bf16)
    low = (value - high.astype(f32)).astype(bf16)
    return high, low


def dot(left, right, dims=((1,), (0,))):
    return lax.dot_general(left, right, (dims, ((), ())), preferred_element_type=f32)


NT = ((1,), (1,))
TN = ((0,), (0,))


def dot3(left, right, dims=((1,), (0,))):
    return (
        dot(left[0], right[0], dims) + dot(left[0], right[1], dims) + dot(left[1], right[0], dims)
    )


def fill_halves(rows_ref, halves_ref):
    for r in range(RW):
        own = jnp.concatenate(
            [rows_ref[tile, pl.ds(r, CH, stride=RW), :] for tile in range(8)], axis=1
        )
        first, second = own[:, :HALF], own[:, HALF:]
        at = pl.ds(r * CH, CH)
        for parity, value in enumerate((first + second, first - second)):
            high, low = split(value)
            halves_ref[parity, 0, at, :] = high
            halves_ref[parity, 1, at, :] = low


def lon_grad_kernel(x_ref, tab_ref, out_ref, rows_ref, halves_ref):
    parity = pl.program_id(0)

    @pl.when(parity == 0)
    def _():
        for tile in range(8):
            value = x_ref[:, :, tile * 128 : tile * 128 + 128].astype(f32) * 2.0
            rows_ref[tile] = value.reshape(LANES, 128)
        fill_halves(rows_ref, halves_ref)

    table = (tab_ref[0, 0], tab_ref[0, 1])
    value = dot3(table, (halves_ref[parity, 0], halves_ref[parity, 1]), NT)
    for tile in range(TILES):
        out_ref[:, tile] = value[:, tile * 128 : tile * 128 + 128].reshape(16, 32, 128)

    @pl.when(parity == 0)
    def _():
        out_ref[0, :, 0:2, :] = out_ref[0, :, 0:2, :] * 0.5


def row_lanes(values):
    wide = jnp.concatenate([values, jnp.zeros((1, 128 - CH), f32)], axis=1)
    wide = jnp.broadcast_to(wide, (8, 128))
    lane = lax.broadcasted_iota(jnp.int32, (8, 128), 1)
    tiles = []
    for tile in range(TILES):
        out = None
        for r in range(RW):
            low = r * CH - tile * 128
            if low >= 128 or low + CH <= 0:
                continue
            piece = wide if low == 0 else pltpu.roll(wide, low % 128, 1)
            out = piece if out is None else jnp.where(lane < low, out, piece)
        tiles.append(out[0:1])
    return tiles


CHUNKS = 4


def lon_field_kernel(
    x_ref, sums_ref, gain_ref, shift_ref, tab_ref,
    out_ref, stat_ref,
    rows_ref, halves_ref, wire_ref, sems,
):
    first = sums_ref[0, 0] + sums_ref[1, 0] + sums_ref[2, 0] + sums_ref[3, 0]
    second = sums_ref[0, 1] + sums_ref[1, 1] + sums_ref[2, 1] + sums_ref[3, 1]
    count = 4.0 * CH
    mean = first / count
    inv_std = lax.rsqrt(second / count - mean * mean + norm_eps)
    stat_ref[0], stat_ref[1] = mean, inv_std
    for tile in range(8):
        lanes = slice(tile * 128, tile * 128 + 128)
        value = x_ref[:, :, lanes].astype(f32)
        value = (value - mean[:, lanes][None]) * inv_std[:, lanes][None]
        rows_ref[tile] = value.reshape(LANES, 128)
    fill_halves(rows_ref, halves_ref)
    gain, shift = row_lanes(gain_ref[...]), row_lanes(shift_ref[...])
    peers = PEERS // CHUNKS
    copies = []
    for chunk in range(CHUNKS):
        parity, place = divmod(chunk, CHUNKS // 2)
        rows = slice(place * 256, place * 256 + 256)
        table = (tab_ref[parity, 0, rows], tab_ref[parity, 1, rows])
        value = dot3(table, (halves_ref[parity, 0], halves_ref[parity, 1]), NT)
        own = pl.ds(chunk * peers, peers)
        for tile in range(TILES):
            piece = value[:, tile * 128 : tile * 128 + 128] * gain[tile]
            wire_ref[own, tile] = piece.reshape(peers, 32, 128)
        if chunk == 0:
            for tile in range(TILES):
                wire_ref[0, tile, 0:1, :] = wire_ref[0, tile, 0:1, :] + shift[tile] * 32.0
        copy = pltpu.make_async_copy(wire_ref.at[own], out_ref.at[own], sems.at[chunk])
        copy.start()
        copies.append(copy)
    for copy in copies:
        copy.wait()


def lon_grad(cotangent, table):
    return pl.pallas_call(
        lon_grad_kernel,
        name="lon_grad",
        grid=(2,),
        in_specs=[
            pl.BlockSpec((CH, RW, LON), lambda i: (0, 0, 0)),
            pl.BlockSpec((1, 2, HALF, HALF), lambda i: (i, 0, 0, 0)),
        ],
        out_specs=pl.BlockSpec((16, TILES, 32, 128), lambda i: (i, 0, 0, 0)),
        out_shape=WIRE_SHAPE,
        scratch_shapes=[
            pltpu.VMEM((8, LANES, 128), f32),
            pltpu.VMEM((2, 2, LANES, HALF), bf16),
        ],
        compiler_params=pltpu.CompilerParams(vmem_limit_bytes=56 * 2**20),
        cost_estimate=pl.CostEstimate(
            flops=6 * LANES * LON * LON, bytes_accessed=7 * 2**20, transcendentals=0
        ),
    )(cotangent, table)


def lon_field(tokens, sums, gain, shift, table):
    vmem = pl.BlockSpec(memory_space=pltpu.VMEM)
    return pl.pallas_call(
        lon_field_kernel,
        name="lon_field",
        in_specs=[vmem] * 5,
        out_specs=[pl.BlockSpec(memory_space=pltpu.HBM), vmem],
        out_shape=[WIRE_SHAPE, jax.ShapeDtypeStruct((2, RW, LON), f32)],
        scratch_shapes=[
            pltpu.VMEM((8, LANES, 128), f32),
            pltpu.VMEM((2, 2, LANES, HALF), bf16),
            pltpu.VMEM((PEERS, TILES, 32, 128), f32),
            pltpu.SemaphoreType.DMA((CHUNKS,)),
        ],
        compiler_params=pltpu.CompilerParams(vmem_limit_bytes=24 * 2**20),
        cost_estimate=pl.CostEstimate(
            flops=6 * LANES * LON * LON, bytes_accessed=7 * 2**20, transcendentals=0
        ),
    )(tokens, sums, gain, shift, table)


def unpack_rows(block_ref, halves_ref):
    lane = lax.broadcasted_iota(jnp.int32, (16, 128), 1)
    for q in range(QB):
        for part in range(2):
            own = [
                block_ref[pl.ds(tile * 8 + 2 * q + part, PEERS, stride=TILES * 8), :]
                for tile in range(TILES)
            ]
            first, second = [v[0:16] for v in own], [v[16:32] for v in own]
            sums = [a + b for a, b in zip(first, second)]
            differences = [a - b for a, b in zip(first, second)]
            for parity, value in enumerate((sums, differences)):
                for r in range(RW):
                    tile, skip = divmod(r * CH, 128)
                    piece = value[tile]
                    if skip:
                        piece = pltpu.roll(piece, 128 - skip, 1)
                    if skip + CH > 128:
                        after = pltpu.roll(value[tile + 1], 128 - skip, 1)
                        piece = jnp.where(lane < 128 - skip, piece, after)
                    high, low = split(piece)
                    at = (pl.ds((part * RW + r) * 16, 16), pl.ds(q * 128, 128))
                    halves_ref[(parity, 0) + at] = high
                    halves_ref[(parity, 1) + at] = low


def pack_rows(even, odd, block_ref, peer_rows, tile_rows, first_row):
    lane = lax.broadcasted_iota(jnp.int32, (16, 128), 1)
    for q in range(QB):
        for part in range(2):
            e = [even[(part * RW + r) * 16 : (part * RW + r + 1) * 16, q * 128 : q * 128 + 128] for r in range(RW)]
            o = [odd[(part * RW + r) * 16 : (part * RW + r + 1) * 16, q * 128 : q * 128 + 128] for r in range(RW)]
            for side in range(2):
                y = [a + b if side == 0 else a - b for a, b in zip(e, o)]
                for tile in range(TILES):
                    out = None
                    for r in range(RW):
                        low = r * CH - tile * 128
                        if low >= 128 or low + CH <= 0:
                            continue
                        piece = y[r] if low == 0 else pltpu.roll(y[r], low % 128, 1)
                        if out is None:
                            out = piece
                        else:
                            out = jnp.where(lane < low, out, piece)
                    start = side * 16 * peer_rows + tile * tile_rows + 2 * q + part + first_row
                    block_ref[pl.ds(start, 16, stride=peer_rows), :] = out


def by_frequency(even, odd):
    rows = []
    for q in range(QB):
        for value in (even, odd):
            lanes = slice(q * 128, q * 128 + 128)
            rows.append(jnp.concatenate([value[0:KB, lanes], value[KB : 2 * KB, lanes]], axis=1))
    return jnp.concatenate(rows, axis=0)


def by_part(rows):
    out = []
    for parity in range(2):
        parts = []
        for part in range(2):
            lanes = slice(part * 128, part * 128 + 128)
            parts.append(
                jnp.concatenate(
                    [rows[(2 * q + parity) * KB : (2 * q + parity + 1) * KB, lanes] for q in range(QB)],
                    axis=1,
                )
            )
        out.append(jnp.concatenate(parts, axis=0))
    return out


def lat_forward(block_ref, tab_ref, halves_ref):
    unpack_rows(block_ref, halves_ref)
    out = [
        dot3(
            (tab_ref[parity, 0], tab_ref[parity, 1]),
            (halves_ref[parity, 0], halves_ref[parity, 1]),
        )
        for parity in range(2)
    ]
    return by_frequency(out[0], out[1])


def lat_inverse(rows, tab_ref, block_ref, peer_rows=TILES * 8, tile_rows=8, first_row=0):
    high, low = by_part(rows[0]), by_part(rows[1])
    even, odd = [
        dot3((tab_ref[parity, 0], tab_ref[parity, 1]), (high[parity], low[parity]), TN)
        for parity in range(2)
    ]
    pack_rows(even, odd, block_ref, peer_rows, tile_rows, first_row)


def fill_weight(w_ref, out_ref):
    full = jnp.zeros((256, 256), f32)
    out_ref[...] = full
    real, imag = w_ref[0, 0], w_ref[0, 1]
    out_ref[0:CH, 0:CH] = real
    out_ref[0:CH, 128 : 128 + CH] = imag
    out_ref[128 : 128 + CH, 0:CH] = -imag
    out_ref[128 : 128 + CH, 128 : 128 + CH] = real


def fill_bias(b_ref, out_ref):
    out_ref[...] = jnp.zeros((8, 256), f32)
    out_ref[0:1, 0:CH] = b_ref[0, 0:1, :]
    out_ref[0:1, 128 : 128 + CH] = b_ref[0, 1:2, :]


def grad_modes_kernel(block_ref, tab_ref, out_ref, halves_ref):
    out_ref[...] = lat_forward(block_ref.reshape(PEERS * TILES * 8, 128), tab_ref, halves_ref)


def field_modes_kernel(
    block_ref, tab_ref, w_in_ref, b_in_ref, w_out_ref, b_out_ref,
    back_ref, spec_ref, spec_low_ref, act_ref, act_low_ref, mask_ref,
    halves_ref, full_ref, weight_ref, bias_ref,
):
    @pl.when(pl.program_id(0) == 0)
    def _():
        for at, (w_ref, b_ref) in enumerate(((w_in_ref, b_in_ref), (w_out_ref, b_out_ref))):
            fill_weight(w_ref, full_ref)
            weight_ref[at, 0], weight_ref[at, 1] = split(full_ref[...])
            fill_bias(b_ref, bias_ref.at[at])

    spec = split(lat_forward(block_ref.reshape(PEERS * TILES * 8, 128), tab_ref, halves_ref))
    spec_ref[...], spec_low_ref[...] = spec
    act = dot3(spec, (weight_ref[0, 0], weight_ref[0, 1])) + bias_ref[0, 0:1, :]
    act = split(jnp.maximum(act, 0.0))
    act_ref[...], act_low_ref[...] = act
    post = dot3(act, (weight_ref[1, 0], weight_ref[1, 1])) + bias_ref[1, 0:1, :]
    mask_ref[...] = jnp.where(jnp.abs(post) > shrink_level, 1.0, 0.0).astype(bf16)
    shrunk = post - jnp.clip(post, -shrink_level, shrink_level)
    lat_inverse(split(shrunk), tab_ref, back_ref.reshape(PEERS * TILES * 8, 128))


def pull_modes_kernel(
    grad_ref, spec_ref, spec_low_ref, act_ref, act_low_ref, mask_ref, tab_ref, w_in_ref, w_out_ref,
    back_ref,
    full_ref, weight_ref, sum_ref,
):
    step = pl.program_id(0)

    @pl.when(step == 0)
    def _():
        for at, w_ref in enumerate((w_in_ref, w_out_ref)):
            fill_weight(w_ref, full_ref)
            weight_ref[at, 0], weight_ref[at, 1] = split(full_ref[...])
        sum_ref[...] = jnp.zeros_like(sum_ref)
        back_ref[:, PULL_ROWS - 16 :, :] = jnp.zeros((PEERS, 16, 128), f32)

    spec, act = (spec_ref[...], spec_low_ref[...]), (act_ref[...], act_low_ref[...])
    d_post = split(jnp.where(mask_ref[...].astype(f32) > 0.5, grad_ref[...], 0.0))
    sum_ref[1] += dot3(act, d_post, TN)
    d_act = dot3(d_post, (weight_ref[1, 0], weight_ref[1, 1]), NT)
    d_pre = split(jnp.where(act[0].astype(f32) > 0.0, d_act, 0.0))
    sum_ref[0] += dot3(spec, d_pre, TN)
    d_spec = dot3(d_pre, (weight_ref[0, 0], weight_ref[0, 1]), NT)
    flat_ref = back_ref.reshape(PEERS * PULL_ROWS, 128)
    lat_inverse(split(d_spec), tab_ref, flat_ref, PULL_ROWS, 32, step * 8)

    @pl.when(step == STEPS - 1)
    def _():
        scale = 1.0 / math.sqrt(131072.0)
        for at in range(2):
            total = sum_ref[at] * scale
            rr, ri = total[0:CH, 0:CH], total[0:CH, 128 : 128 + CH]
            ir, ii = total[128 : 128 + CH, 0:CH], total[128 : 128 + CH, 128 : 128 + CH]
            for part, value in enumerate((rr + ii, ri - ir)):
                for k in range(8):
                    peer = (2 * at + part) * 8 + k
                    back_ref[peer, PULL_ROWS - 16 : PULL_ROWS - 4, 0:CH] = value[12 * k : 12 * k + 12]


PULL_ROWS = TILES * 32 + 16
WIRE = pl.BlockSpec((PEERS, TILES, 8, 128), lambda i: (0, 0, i, 0))
LAT_TAB = pl.BlockSpec((2, 2, 256, 256), lambda i: (0, 0, 0, 0))
MODES = pl.BlockSpec((1024, 256), lambda i: (i, 0))
WEIGHT = pl.BlockSpec((1, 2, CH, CH), lambda i: (0, 0, 0, 0))
BIAS = pl.BlockSpec((1, 2, CH), lambda i: (0, 0, 0))


def modes_shape(dtype):
    return jax.ShapeDtypeStruct((4096, 256), dtype)


def grad_modes(block, table):
    return pl.pallas_call(
        grad_modes_kernel,
        name="grad_modes",
        grid=(STEPS,),
        in_specs=[WIRE, LAT_TAB],
        out_specs=MODES,
        out_shape=modes_shape(f32),
        scratch_shapes=[pltpu.VMEM((2, 2, 256, QB * 128), bf16)],
        compiler_params=pltpu.CompilerParams(vmem_limit_bytes=56 * 2**20),
        cost_estimate=pl.CostEstimate(
            flops=6 * 2**31, bytes_accessed=8 * 2**20, transcendentals=0
        ),
    )(block, table)


def field_modes(block, table, w_in, b_in, w_out, b_out):
    return pl.pallas_call(
        field_modes_kernel,
        name="field_modes",
        grid=(STEPS,),
        in_specs=[WIRE, LAT_TAB, WEIGHT, BIAS, WEIGHT, BIAS],
        out_specs=[WIRE] + [MODES] * 5,
        out_shape=[WIRE_SHAPE] + [modes_shape(bf16)] * 5,
        scratch_shapes=[
            pltpu.VMEM((2, 2, 256, QB * 128), bf16),
            pltpu.VMEM((256, 256), f32),
            pltpu.VMEM((2, 2, 256, 256), bf16),
            pltpu.VMEM((2, 8, 256), f32),
        ],
        compiler_params=pltpu.CompilerParams(vmem_limit_bytes=56 * 2**20),
        cost_estimate=pl.CostEstimate(
            flops=12 * 2**31, bytes_accessed=14 * 2**20, transcendentals=0
        ),
    )(block, table, w_in, b_in, w_out, b_out)


def pull_modes(grad, saved, table, w_in, w_out):
    return pl.pallas_call(
        pull_modes_kernel,
        name="pull_modes",
        grid=(STEPS,),
        in_specs=[MODES] * 6 + [LAT_TAB, WEIGHT, WEIGHT],
        out_specs=pl.BlockSpec((PEERS, PULL_ROWS, 128), lambda i: (0, 0, 0)),
        out_shape=jax.ShapeDtypeStruct((PEERS, PULL_ROWS, 128), f32),
        scratch_shapes=[
            pltpu.VMEM((256, 256), f32),
            pltpu.VMEM((2, 2, 256, 256), bf16),
            pltpu.VMEM((2, 256, 256), f32),
        ],
        compiler_params=pltpu.CompilerParams(vmem_limit_bytes=56 * 2**20),
        cost_estimate=pl.CostEstimate(
            flops=8 * 2**31, bytes_accessed=14 * 2**20, transcendentals=0
        ),
    )(grad, *saved, table, w_in, w_out)


def lon_inverse(take, tab_ref, rows_ref, weighted):
    sides = []
    for parity in range(2):
        value = jnp.concatenate(
            [
                take(slice(parity * 16, parity * 16 + 16), tile).reshape(HALF, 128)
                for tile in range(TILES)
            ],
            axis=1,
        )
        if weighted:
            value = value * 2.0
            if parity == 0:
                row = lax.broadcasted_iota(jnp.int32, (HALF, 1), 0)
                value = value * jnp.where(row == 0, 0.5, 1.0)
        sides.append(dot(value.astype(bf16), tab_ref[parity], TN))
    first, second = sides[0] + sides[1], sides[0] - sides[1]
    for r in range(RW):
        at, rows = pl.ds(r, CH, stride=RW), slice(r * CH, (r + 1) * CH)
        for tile in range(4):
            lanes = slice(tile * 128, tile * 128 + 128)
            rows_ref[tile, at, :] = first[rows, lanes]
            rows_ref[4 + tile, at, :] = second[rows, lanes]


def mixed_kernel(block_ref, tab_ref, tok_ref, stat_ref, gain_ref, shift_ref, out_ref, rows_ref):
    lon_inverse(lambda peers, tile: block_ref[peers, tile], tab_ref, rows_ref, True)
    for tile in range(8):
        lanes = slice(tile * 128, tile * 128 + 128)
        tok = tok_ref[:, :, lanes].astype(f32)
        normed = (tok - stat_ref[0, :, lanes][None]) * stat_ref[1, :, lanes][None]
        normal = normed * gain_ref[...] + shift_ref[...]
        filtered = rows_ref[tile].reshape(CH, RW, 128)
        out_ref[:, :, lanes] = (filtered + normal + tok).astype(bf16)


def pulled_kernel(
    block_ref, tab_ref, tok_ref, cot_ref, stat_ref, gain_ref,
    out_ref, sum_ref, weight_ref,
    rows_ref,
):
    def take(peers, tile):
        return block_ref[peers, tile * 32 : tile * 32 + 32, :]

    lon_inverse(take, tab_ref, rows_ref, False)
    for tile in range(8):
        lanes = slice(tile * 128, tile * 128 + 128)
        tok = tok_ref[:, :, lanes].astype(f32)
        inv_std = stat_ref[1, :, lanes]
        normed = (tok - stat_ref[0, :, lanes][None]) * inv_std[None]
        pulled = rows_ref[tile].reshape(CH, RW, 128)
        cot = cot_ref[:, :, lanes].astype(f32)
        dnorm = (pulled + cot) * gain_ref[...]
        out_ref[:, :, lanes] = cot + inv_std[None] * dnorm
        sum_ref[0, :, lanes] = jnp.sum(dnorm, axis=0)
        sum_ref[1, :, lanes] = jnp.sum(dnorm * normed, axis=0)
    share = jnp.sum(block_ref[:, PULL_ROWS - 16 :, :], axis=0)
    for i in range(12):
        weight_ref[0:1, i * CH : i * CH + CH] = share[i : i + 1, 0:CH]


def finish_kernel(part_ref, tok_ref, sums_ref, stat_ref, out_ref):
    count = 4.0 * CH
    mean, inv_std = stat_ref[0], stat_ref[1]
    one = (sums_ref[0, 0] + sums_ref[1, 0] + sums_ref[2, 0] + sums_ref[3, 0]) / count
    two = (sums_ref[0, 1] + sums_ref[1, 1] + sums_ref[2, 1] + sums_ref[3, 1]) / count
    normed = (tok_ref[...].astype(f32) - mean[None]) * inv_std[None]
    out_ref[...] = (part_ref[...] - (inv_std * one)[None] - normed * (inv_std * two)[None]).astype(bf16)


def finish(part, tokens, sums, stats):
    block = pl.BlockSpec((CH // 4, RW, LON), lambda i: (i, 0, 0))
    return pl.pallas_call(
        finish_kernel,
        name="finish",
        grid=(4,),
        in_specs=[
            block,
            block,
            pl.BlockSpec((4, 2, RW, LON), lambda i: (0, 0, 0, 0)),
            pl.BlockSpec((2, RW, LON), lambda i: (0, 0, 0)),
        ],
        out_specs=block,
        out_shape=jax.ShapeDtypeStruct((CH, RW, LON), bf16),
        compiler_params=pltpu.CompilerParams(vmem_limit_bytes=24 * 2**20),
        cost_estimate=pl.CostEstimate(
            flops=8 * CH * RW * LON, bytes_accessed=6 * 2**20, transcendentals=0
        ),
    )(part, tokens, sums, stats)


def whole_call(kernel, name, out_shape):
    return pl.pallas_call(
        kernel,
        name=name,
        out_shape=out_shape,
        scratch_shapes=[pltpu.VMEM((8, LANES, 128), f32)],
        compiler_params=pltpu.CompilerParams(vmem_limit_bytes=28 * 2**20),
        cost_estimate=pl.CostEstimate(
            flops=4 * LANES * LON * LON, bytes_accessed=10 * 2**20, transcendentals=0
        ),
    )


def exchange(value):
    return lax.all_to_all(value, "lat", split_axis=0, concat_axis=0, tiled=True)


def after(value, first):
    mark = lax.slice(first, (0,) * first.ndim, (1,) * first.ndim)
    return lax.optimization_barrier((value, mark))[0]


def per_device(tokens, cotangent, gain, shift, w_in, b_in, w_out, b_out):
    lon_host = lon_table()
    lon_tab, lon_high = jnp.asarray(lon_host), jnp.asarray(lon_host[:, 0])
    lat_tab = jnp.asarray(lat_table())
    tok_val = tokens.astype(f32)
    sums = jnp.stack([jnp.sum(tok_val, axis=0), jnp.sum(tok_val * tok_val, axis=0)])
    sums = lax.all_gather(sums, "grp")
    spec_field, stats = lon_field(
        tokens, sums, gain.reshape(1, CH), shift.reshape(1, CH), lon_tab
    )
    gain_cube = jnp.broadcast_to(gain.reshape(CH, 1, 1), (CH, 1, 128))
    shift_cube = jnp.broadcast_to(shift.reshape(CH, 1, 1), (CH, 1, 128))

    modes_field = exchange(spec_field)
    spec_grad = lon_grad(after(cotangent, stats), lon_tab)
    modes_grad = exchange(after(spec_grad, modes_field))
    back_field, *saved = field_modes(modes_field, lat_tab, w_in, b_in, w_out, b_out)
    rows_field = exchange(after(back_field, modes_grad))
    grad_rows = grad_modes(modes_grad, lat_tab)
    back_grad = pull_modes(grad_rows, saved, lat_tab, w_in, w_out)
    rows_grad = exchange(after(back_grad, rows_field))
    mixed = whole_call(mixed_kernel, "mixed", jax.ShapeDtypeStruct((CH, RW, LON), bf16))(
        rows_field, lon_high, tokens, stats, gain_cube, shift_cube
    )
    part, back, grad_weights = whole_call(
        pulled_kernel,
        "pulled",
        [
            jax.ShapeDtypeStruct((CH, RW, LON), f32),
            jax.ShapeDtypeStruct((2, RW, LON), f32),
            jax.ShapeDtypeStruct((1, 1152), f32),
        ],
    )(rows_grad, lon_high, tokens, cotangent, stats, gain_cube)
    grad_tokens = finish(part, tokens, lax.all_gather(back, "grp"), stats)
    return (mixed, grad_tokens, grad_weights)


def solution(mesh):
    in_specs = (
        P("grp", "lat", None),
        P("grp", "lat", None),
        P("grp"),
        P("grp"),
        P("grp", None, None, None),
        P("grp", None, None),
        P("grp", None, None, None),
        P("grp", None, None),
    )
    out_specs = (P("grp", "lat", None), P("grp", "lat", None), P("grp", "lat"))
    return jax.shard_map(
        per_device, mesh=mesh, in_specs=in_specs, out_specs=out_specs, check_vma=False
    )
```

```python
import functools
import math

import jax
import jax.numpy as jnp
import ml_dtypes
import numpy as np
from jax import lax
from jax.experimental import pallas as pl
from jax.experimental.pallas import tpu as pltpu
from jax.sharding import PartitionSpec as P

shrink_level = 0.01
norm_eps = 1e-05
f32 = jnp.float32
bf16 = jnp.bfloat16

CH = 96
RW = 8
LON = 1024
HALF = 512
PEERS = 32
LANES = RW * CH
QB = 4
KB = 128
STEPS = 4
TILES = LANES // 128
WIRE_SHAPE = jax.ShapeDtypeStruct((PEERS, TILES, 32, 128), jnp.float32)


def host_split(table):
    high = table.astype(ml_dtypes.bfloat16)
    low = (table - high.astype(np.float64)).astype(ml_dtypes.bfloat16)
    return np.stack([high, low])


def lon_table():
    parts = []
    n = np.arange(HALF)
    for parity in range(2):
        m = 2 * np.arange(256) + parity
        theta = 2.0 * np.pi * ((m[:, None] * n[None, :]) % LON) / LON
        table = np.stack([np.cos(theta), -np.sin(theta)], axis=1).reshape(HALF, HALF)
        parts.append(host_split(table / 32.0))
    return np.stack(parts)


def lat_table():
    parts = []
    row = np.arange(RW)[:, None]
    peer = np.arange(16)[None, :]
    place = (8 * peer + row).reshape(-1)
    for parity in range(2):
        k = 2 * np.arange(KB) + parity
        theta = 2.0 * np.pi * ((k[:, None] * place[None, :]) % 256) / 256
        c, s = np.cos(theta), np.sin(theta)
        table = np.concatenate(
            [np.concatenate([c, s], axis=1), np.concatenate([-s, c], axis=1)], axis=0
        )
        parts.append(host_split(table / 16.0))
    return np.stack(parts)


def spread_table():
    table = np.zeros((LANES, RW * 128), ml_dtypes.bfloat16)
    channel, row = np.divmod(np.arange(LANES), RW)
    table[np.arange(LANES), row * 128 + channel] = 1
    return table


def split(value):
    high = value.astype(bf16)
    low = (value - high.astype(f32)).astype(bf16)
    return high, low


def dot(left, right, dims=((1,), (0,))):
    return lax.dot_general(left, right, (dims, ((), ())), preferred_element_type=f32)


NT = ((1,), (1,))
TN = ((0,), (0,))


def dot3(left, right, dims=((1,), (0,))):
    return (
        dot(left[0], right[0], dims) + dot(left[0], right[1], dims) + dot(left[1], right[0], dims)
    )


CHUNKS = 4
GROUP = CH // CHUNKS


def bring(pairs, sems):
    copies = [pltpu.make_async_copy(src, dst, sems.at[i]) for i, (src, dst) in enumerate(pairs)]
    for copy in copies:
        copy.start()
    return copies


def lon_transform(prepare, finish_rows, x_ref, tab_hbm, out_hbm, scratch):
    tab_ref, halves_ref, wire_ref, tab_sems, sems = scratch
    tab_copies = bring([(tab_hbm.at[p], tab_ref.at[p]) for p in range(2)], tab_sems)
    for tile in range(4):
        pair = []
        for lanes in (slice(tile * 128, tile * 128 + 128), slice(HALF + tile * 128, HALF + tile * 128 + 128)):
            pair.append(prepare(x_ref[:, :, lanes].astype(f32), lanes).reshape(LANES, 128))
        for parity, value in enumerate((pair[0] + pair[1], pair[0] - pair[1])):
            high, low = split(value)
            halves_ref[parity, 0, :, tile * 128 : tile * 128 + 128] = high
            halves_ref[parity, 1, :, tile * 128 : tile * 128 + 128] = low
    peers = PEERS // 2
    copies = []
    for parity in range(2):
        tab_copies[parity].wait()
        both = dot(tab_ref[parity].reshape(2 * HALF, HALF), halves_ref[parity, 0], NT)
        value = both[:HALF] + both[HALF:] + dot(tab_ref[parity, 0], halves_ref[parity, 1], NT)
        own = pl.ds(parity * peers, peers)
        for tile in range(TILES):
            piece = finish_rows(value[:, tile * 128 : tile * 128 + 128], tile)
            wire_ref[own, tile] = piece.reshape(peers, 32, 128)
        if parity == 0:
            finish_rows(None, wire_ref)
        copy = pltpu.make_async_copy(wire_ref.at[own], out_hbm.at[own], sems.at[parity])
        copy.start()
        copies.append(copy)
    for copy in copies:
        copy.wait()


def lon_grad_kernel(x_ref, tab_hbm, sums_hbm, out_hbm, mark_ref, *scratch):
    mark_ref[...] = jnp.zeros((8, 128), f32)

    def finish_rows(value, at):
        if value is not None:
            return value
        at[0, :, 0:2, :] = at[0, :, 0:2, :] * 0.5

    lon_transform(lambda value, lanes: value * 2.0, finish_rows, x_ref, tab_hbm, out_hbm, scratch)


def total(terms, at):
    return terms[0][at] + terms[1][at] + terms[2][at] + terms[3][at]


def lon_field_kernel(
    x_ref, tab_hbm, gain_ref, shift_ref, one_ref, two_ref, three_ref, four_ref,
    mark_hbm,
    out_hbm, stat_ref,
    *scratch,
):
    terms = (one_ref, two_ref, three_ref, four_ref)
    count = 4.0 * CH
    mean = total(terms, 0) / count
    inv_std = lax.rsqrt(total(terms, 1) / count - mean * mean + norm_eps)
    stat_ref[0], stat_ref[1] = mean, inv_std

    def prepare(value, lanes):
        return (value - mean[:, lanes][None]) * inv_std[:, lanes][None]

    def finish_rows(value, at):
        if value is not None:
            return value * gain_ref[at]
        for tile in range(TILES):
            at[0, tile, 0:1, :] = at[0, tile, 0:1, :] + shift_ref[tile] * 32.0

    lon_transform(prepare, finish_rows, x_ref, tab_hbm, out_hbm, scratch)


VMEM = pl.BlockSpec(memory_space=pltpu.VMEM)
HBM = pl.BlockSpec(memory_space=pltpu.HBM)
STATS_SHAPE = jax.ShapeDtypeStruct((2, RW, LON), f32)


def lon_call(kernel, name, more, unread):
    return pl.pallas_call(
        kernel,
        name=name,
        in_specs=[VMEM, HBM] + [VMEM] * (more + unread),
        out_specs=[HBM, VMEM],
        out_shape=[WIRE_SHAPE, STATS_SHAPE]
        if more
        else [pltpu.HBM(WIRE_SHAPE.shape, f32), jax.ShapeDtypeStruct((8, 128), f32)],
        scratch_shapes=[
            pltpu.VMEM((2, 2, HALF, HALF), bf16),
            pltpu.VMEM((2, 2, LANES, HALF), bf16),
            pltpu.VMEM((PEERS, TILES, 32, 128), f32),
            pltpu.SemaphoreType.DMA((2,)),
            pltpu.SemaphoreType.DMA((2,)),
        ],
        compiler_params=pltpu.CompilerParams(vmem_limit_bytes=24 * 2**20),
        cost_estimate=pl.CostEstimate(
            flops=6 * LANES * LON * LON, bytes_accessed=7 * 2**20, transcendentals=0
        ),
    )


def unpack_rows(block_ref, spread_ref, rows_ref, halves_ref, terms):
    left = jnp.concatenate([block_ref[:, t].reshape(PEERS * 8, 128) for t in range(TILES)], axis=1)
    value = None
    for _ in range(terms):
        part = left.astype(bf16)
        left = left - part.astype(f32)
        moved = dot(part, spread_ref[...])
        value = moved if value is None else value + moved
    for r in range(RW):
        rows_ref[r, 0 : PEERS * 8] = value[:, r * 128 : r * 128 + 128]
    for q in range(QB):
        for part in range(2):
            for r in range(RW):
                first = rows_ref[r, pl.ds(2 * q + part, 16, stride=8), :]
                second = rows_ref[r, pl.ds(128 + 2 * q + part, 16, stride=8), :]
                for parity, value in enumerate((first + second, first - second)):
                    high, low = split(value)
                    at = (pl.ds((part * RW + r) * 16, 16), pl.ds(q * 128, 128))
                    halves_ref[(parity, 0) + at] = high
                    halves_ref[(parity, 1) + at] = low


def pack_rows(even, odd, spread_ref, rows_ref):
    for q in range(QB):
        lanes = slice(q * 128, q * 128 + 128)
        for part in range(2):
            for r in range(RW):
                at = slice((part * RW + r) * 16, (part * RW + r + 1) * 16)
                first, second = even[at, lanes], odd[at, lanes]
                rows_ref[r, pl.ds(2 * q + part, 16, stride=8), :] = first + second
                rows_ref[r, pl.ds(128 + 2 * q + part, 16, stride=8), :] = first - second
    high, low = split(jnp.concatenate([rows_ref[r, 0 : PEERS * 8] for r in range(RW)], axis=1))
    return dot(high, spread_ref[...], NT) + dot(low, spread_ref[...], NT)


def by_frequency(even, odd):
    rows = []
    for q in range(QB):
        for value in (even, odd):
            lanes = slice(q * 128, q * 128 + 128)
            rows.append(jnp.concatenate([value[0:KB, lanes], value[KB : 2 * KB, lanes]], axis=1))
    return jnp.concatenate(rows, axis=0)


def by_part(rows):
    out = []
    for parity in range(2):
        parts = []
        for part in range(2):
            lanes = slice(part * 128, part * 128 + 128)
            parts.append(
                jnp.concatenate(
                    [rows[(2 * q + parity) * KB : (2 * q + parity + 1) * KB, lanes] for q in range(QB)],
                    axis=1,
                )
            )
        out.append(jnp.concatenate(parts, axis=0))
    return out


def lat_forward(block_ref, tab_ref, spread_ref, rows_ref, halves_ref, terms):
    unpack_rows(block_ref, spread_ref, rows_ref, halves_ref, terms)
    out = [
        dot3(
            (tab_ref[parity, 0], tab_ref[parity, 1]),
            (halves_ref[parity, 0], halves_ref[parity, 1]),
        )
        for parity in range(2)
    ]
    return by_frequency(out[0], out[1])


def lat_inverse(rows, tab_ref, spread_ref, rows_ref):
    high, low = by_part(rows[0]), by_part(rows[1])
    even, odd = [
        dot3((tab_ref[parity, 0], tab_ref[parity, 1]), (high[parity], low[parity]), TN)
        for parity in range(2)
    ]
    wire = pack_rows(even, odd, spread_ref, rows_ref)
    return [wire[:, t * 128 : t * 128 + 128].reshape(PEERS, 8, 128) for t in range(TILES)]


def fill_weight(w_ref, out_ref):
    full = jnp.zeros((256, 256), f32)
    out_ref[...] = full
    real, imag = w_ref[0, 0], w_ref[0, 1]
    out_ref[0:CH, 0:CH] = real
    out_ref[0:CH, 128 : 128 + CH] = imag
    out_ref[128 : 128 + CH, 0:CH] = -imag
    out_ref[128 : 128 + CH, 128 : 128 + CH] = real


def fill_bias(b_ref, out_ref):
    out_ref[...] = jnp.zeros((8, 256), f32)
    out_ref[0:1, 0:CH] = b_ref[0, 0:1, :]
    out_ref[0:1, 128 : 128 + CH] = b_ref[0, 1:2, :]


def grad_modes_kernel(block_ref, tab_ref, spread_ref, out_ref, rows_ref, halves_ref):
    out_ref[...] = lat_forward(block_ref, tab_ref, spread_ref, rows_ref, halves_ref, 2)


def field_modes_kernel(
    block_ref, tab_ref, spread_ref, w_in_ref, b_in_ref, w_out_ref, b_out_ref,
    back_ref, spec_ref, spec_low_ref, act_ref, act_low_ref, mask_ref,
    rows_ref, halves_ref, full_ref, weight_ref, bias_ref,
):
    @pl.when(pl.program_id(0) == 0)
    def _():
        for at, (w_ref, b_ref) in enumerate(((w_in_ref, b_in_ref), (w_out_ref, b_out_ref))):
            fill_weight(w_ref, full_ref)
            weight_ref[at, 0], weight_ref[at, 1] = split(full_ref[...])
            fill_bias(b_ref, bias_ref.at[at])

    spec = split(lat_forward(block_ref, tab_ref, spread_ref, rows_ref, halves_ref, 3))
    spec_ref[...], spec_low_ref[...] = spec
    act = dot3(spec, (weight_ref[0, 0], weight_ref[0, 1])) + bias_ref[0, 0:1, :]
    act = split(jnp.maximum(act, 0.0))
    act_ref[...], act_low_ref[...] = act
    post = dot3(act, (weight_ref[1, 0], weight_ref[1, 1])) + bias_ref[1, 0:1, :]
    mask_ref[...] = jnp.where(jnp.abs(post) > shrink_level, 1.0, 0.0).astype(bf16)
    shrunk = post - jnp.clip(post, -shrink_level, shrink_level)
    for tile, piece in enumerate(lat_inverse(split(shrunk), tab_ref, spread_ref, rows_ref)):
        back_ref[:, tile] = piece


def pull_modes_kernel(
    grad_ref, spec_ref, spec_low_ref, act_ref, act_low_ref, mask_ref, tab_ref, spread_ref,
    w_in_ref, w_out_ref, cubes_hbm,
    back_ref,
    rows_ref, full_ref, weight_ref, sum_ref,
):
    step = pl.program_id(0)

    @pl.when(step == 0)
    def _():
        for at, w_ref in enumerate((w_in_ref, w_out_ref)):
            fill_weight(w_ref, full_ref)
            weight_ref[at, 0], weight_ref[at, 1] = split(full_ref[...])
        sum_ref[...] = jnp.zeros_like(sum_ref)
        back_ref[:, PULL_ROWS - 16 :, :] = jnp.zeros((PEERS, 16, 128), f32)

    spec, act = (spec_ref[...], spec_low_ref[...]), (act_ref[...], act_low_ref[...])
    d_post = split(jnp.where(mask_ref[...].astype(f32) > 0.5, grad_ref[...], 0.0))
    sum_ref[1] += dot3(act, d_post, TN)
    d_act = dot3(d_post, (weight_ref[1, 0], weight_ref[1, 1]), NT)
    d_pre = split(jnp.where(act[0].astype(f32) > 0.0, d_act, 0.0))
    sum_ref[0] += dot3(spec, d_pre, TN)
    d_spec = dot3(d_pre, (weight_ref[0, 0], weight_ref[0, 1]), NT)
    for tile, piece in enumerate(lat_inverse(split(d_spec), tab_ref, spread_ref, rows_ref)):
        back_ref[:, pl.ds(pl.multiple_of(tile * 32 + step * 8, 8), 8), :] = piece

    @pl.when(step == STEPS - 1)
    def _():
        scale = 1.0 / math.sqrt(131072.0)
        for at in range(2):
            total = sum_ref[at] * scale
            rr, ri = total[0:CH, 0:CH], total[0:CH, 128 : 128 + CH]
            ir, ii = total[128 : 128 + CH, 0:CH], total[128 : 128 + CH, 128 : 128 + CH]
            for part, value in enumerate((rr + ii, ri - ir)):
                for k in range(8):
                    peer = (2 * at + part) * 8 + k
                    back_ref[peer, PULL_ROWS - 16 : PULL_ROWS - 4, 0:CH] = value[12 * k : 12 * k + 12]


PULL_ROWS = TILES * 32 + 16
WIRE = pl.BlockSpec((PEERS, TILES, 8, 128), lambda i: (0, 0, i, 0))
LAT_TAB = pl.BlockSpec((2, 2, 256, 256), lambda i: (0, 0, 0, 0))
MODES = pl.BlockSpec((1024, 256), lambda i: (i, 0))
SPREAD = pl.BlockSpec((LANES, RW * 128), lambda i: (0, 0))
ROWS = pltpu.VMEM((RW, PEERS * 8 + 8, 128), f32)
WEIGHT = pl.BlockSpec((1, 2, CH, CH), lambda i: (0, 0, 0, 0))
BIAS = pl.BlockSpec((1, 2, CH), lambda i: (0, 0, 0))


def modes_shape(dtype):
    return jax.ShapeDtypeStruct((4096, 256), dtype)


def grad_modes(block, table, spread):
    return pl.pallas_call(
        grad_modes_kernel,
        name="grad_modes",
        grid=(STEPS,),
        in_specs=[WIRE, LAT_TAB, SPREAD],
        out_specs=MODES,
        out_shape=modes_shape(f32),
        scratch_shapes=[ROWS, pltpu.VMEM((2, 2, 256, QB * 128), bf16)],
        compiler_params=pltpu.CompilerParams(vmem_limit_bytes=36 * 2**20),
        cost_estimate=pl.CostEstimate(
            flops=6 * 2**31, bytes_accessed=8 * 2**20, transcendentals=0
        ),
    )(block, table, spread)


def field_modes(block, table, spread, w_in, b_in, w_out, b_out):
    return pl.pallas_call(
        field_modes_kernel,
        name="field_modes",
        grid=(STEPS,),
        in_specs=[WIRE, LAT_TAB, SPREAD, WEIGHT, BIAS, WEIGHT, BIAS],
        out_specs=[WIRE] + [MODES] * 5,
        out_shape=[WIRE_SHAPE] + [modes_shape(bf16)] * 5,
        scratch_shapes=[
            ROWS,
            pltpu.VMEM((2, 2, 256, QB * 128), bf16),
            pltpu.VMEM((256, 256), f32),
            pltpu.VMEM((2, 2, 256, 256), bf16),
            pltpu.VMEM((2, 8, 256), f32),
        ],
        compiler_params=pltpu.CompilerParams(vmem_limit_bytes=36 * 2**20),
        cost_estimate=pl.CostEstimate(
            flops=12 * 2**31, bytes_accessed=14 * 2**20, transcendentals=0
        ),
    )(block, table, spread, w_in, b_in, w_out, b_out)


def pull_modes(grad, saved, table, spread, w_in, w_out, cubes):
    return pl.pallas_call(
        pull_modes_kernel,
        name="pull_modes",
        grid=(STEPS,),
        in_specs=[MODES] * 6 + [LAT_TAB, SPREAD, WEIGHT, WEIGHT, HBM],
        out_specs=pl.BlockSpec((PEERS, PULL_ROWS, 128), lambda i: (0, 0, 0)),
        out_shape=jax.ShapeDtypeStruct((PEERS, PULL_ROWS, 128), f32),
        scratch_shapes=[
            ROWS,
            pltpu.VMEM((256, 256), f32),
            pltpu.VMEM((2, 2, 256, 256), bf16),
            pltpu.VMEM((2, 256, 256), f32),
        ],
        compiler_params=pltpu.CompilerParams(vmem_limit_bytes=36 * 2**20),
        cost_estimate=pl.CostEstimate(
            flops=8 * 2**31, bytes_accessed=14 * 2**20, transcendentals=0
        ),
    )(grad, *saved, table, spread, w_in, w_out, cubes)


def lon_inverse(take, tab_ref, weighted):
    sides = []
    for parity in range(2):
        value = jnp.concatenate(
            [
                take(slice(parity * 16, parity * 16 + 16), tile).reshape(HALF, 128)
                for tile in range(TILES)
            ],
            axis=1,
        )
        if weighted:
            value = value * 2.0
            if parity == 0:
                row = lax.broadcasted_iota(jnp.int32, (HALF, 1), 0)
                value = value * jnp.where(row == 0, 0.5, 1.0)
        sides.append(dot(value.astype(bf16), tab_ref[parity], TN))
    sums, differences = sides[0] + sides[1], sides[0] - sides[1]
    return [v[:, t * 128 : t * 128 + 128] for v in (sums, differences) for t in range(4)]


def mixed_kernel(
    block_ref, tab_hbm, tok_hbm, stat_ref, cubes_ref, back_hbm,
    out_hbm,
    tab_ref, tok_ref, mix_ref, sems, out_sems,
):
    copies = bring(((tab_hbm, tab_ref), (tok_hbm, tok_ref)), sems)
    copies[0].wait()
    tiles = lon_inverse(lambda peers, tile: block_ref[peers, tile], tab_ref, True)
    copies[1].wait()
    out_copies = []
    for g in range(CHUNKS):
        own = pl.ds(g * GROUP, GROUP)
        gain, shift = cubes_ref[0, own], cubes_ref[1, own]
        for tile in range(8):
            lanes = slice(tile * 128, tile * 128 + 128)
            tok = tok_ref[own, :, lanes].astype(f32)
            normed = (tok - stat_ref[0, :, lanes][None]) * stat_ref[1, :, lanes][None]
            filtered = tiles[tile][g * GROUP * RW : (g + 1) * GROUP * RW].reshape(GROUP, RW, 128)
            mix_ref[own, :, lanes] = (filtered + (normed * gain + shift) + tok).astype(bf16)
        copy = pltpu.make_async_copy(mix_ref.at[own], out_hbm.at[own], out_sems.at[g])
        copy.start()
        out_copies.append(copy)
    for copy in out_copies:
        copy.wait()


def pulled_kernel(
    block_ref, tab_hbm, tok_hbm, cot_hbm, stat_ref, cubes_ref,
    out_ref, sum_ref, weight_ref,
    tab_ref, tok_ref, cot_ref, sems,
):
    copies = bring(((tab_hbm, tab_ref), (tok_hbm, tok_ref), (cot_hbm, cot_ref)), sems)

    def take(peers, tile):
        return block_ref[peers, tile * 32 : tile * 32 + 32, :]

    copies[0].wait()
    tiles = lon_inverse(take, tab_ref, False)
    share = jnp.sum(block_ref[:, PULL_ROWS - 16 :, :], axis=0)
    for i in range(12):
        weight_ref[0:1, i * CH : i * CH + CH] = share[i : i + 1, 0:CH]
    copies[1].wait()
    copies[2].wait()
    for tile in range(8):
        lanes = slice(tile * 128, tile * 128 + 128)
        tok = tok_ref[:, :, lanes].astype(f32)
        inv_std = stat_ref[1, :, lanes]
        normed = (tok - stat_ref[0, :, lanes][None]) * inv_std[None]
        pulled = tiles[tile].reshape(CH, RW, 128)
        cot = cot_ref[:, :, lanes].astype(f32)
        dnorm = (pulled + cot) * cubes_ref[0]
        out_ref[:, :, lanes] = cot + inv_std[None] * dnorm
        sum_ref[0, :, lanes] = jnp.sum(dnorm, axis=0)
        sum_ref[1, :, lanes] = jnp.sum(dnorm * normed, axis=0)


def inverse_call(kernel, name, in_specs, out_specs, out_shape, scratch):
    return pl.pallas_call(
        kernel,
        name=name,
        in_specs=in_specs,
        out_specs=out_specs,
        out_shape=out_shape,
        scratch_shapes=[
            pltpu.VMEM((2, HALF, HALF), bf16),
            pltpu.VMEM((CH, RW, LON), bf16),
            pltpu.VMEM((CH, RW, LON), bf16),
        ]
        + scratch,
        compiler_params=pltpu.CompilerParams(vmem_limit_bytes=28 * 2**20),
        cost_estimate=pl.CostEstimate(
            flops=4 * LANES * LON * LON, bytes_accessed=10 * 2**20, transcendentals=0
        ),
    )


def finish_kernel(part_ref, tok_ref, stat_ref, one_ref, two_ref, three_ref, four_ref, out_ref):
    terms = (one_ref, two_ref, three_ref, four_ref)
    count = 4.0 * CH
    mean, inv_std = stat_ref[0], stat_ref[1]
    one, two = total(terms, 0) / count, total(terms, 1) / count
    normed = (tok_ref[...].astype(f32) - mean[None]) * inv_std[None]
    out_ref[...] = (part_ref[...] - (inv_std * one)[None] - normed * (inv_std * two)[None]).astype(bf16)


def finish(part, tokens, stats, terms):
    block = pl.BlockSpec((CH // 4, RW, LON), lambda i: (i, 0, 0))
    return pl.pallas_call(
        finish_kernel,
        name="finish",
        grid=(4,),
        in_specs=[block, block] + [pl.BlockSpec((2, RW, LON), lambda i: (0, 0, 0))] * 5,
        out_specs=block,
        out_shape=jax.ShapeDtypeStruct((CH, RW, LON), bf16),
        compiler_params=pltpu.CompilerParams(vmem_limit_bytes=24 * 2**20),
        cost_estimate=pl.CostEstimate(
            flops=8 * CH * RW * LON, bytes_accessed=6 * 2**20, transcendentals=0
        ),
    )(part, tokens, stats, *terms)


def exchange(value):
    return lax.all_to_all(value, "lat", split_axis=0, concat_axis=0, tiled=True)


def group_terms(value):
    return [value] + [
        lax.ppermute(value, "grp", [(j, j ^ step) for j in range(4)]) for step in (1, 2, 3)
    ]


def per_device(tokens, cotangent, gain, shift, w_in, b_in, w_out, b_out):
    lon_host = lon_table()
    lon_tab, lon_high = jnp.asarray(lon_host), jnp.asarray(lon_host[:, 0])
    lon_tab = pltpu.with_memory_space_constraint(lon_tab, pltpu.HBM)
    lat_tab, spread = jnp.asarray(lat_table()), jnp.asarray(spread_table())
    tok_val = tokens.astype(f32)
    sums = jnp.stack([jnp.sum(tok_val, axis=0), jnp.sum(tok_val * tok_val, axis=0)])
    terms = group_terms(sums)
    spec_grad, grad_mark = lon_call(lon_grad_kernel, "lon_grad", 0, 1)(cotangent, lon_tab, sums)
    spec_field, stats = lon_call(lon_field_kernel, "lon_field", 6, 1)(
        tokens, lon_tab, jnp.repeat(gain, RW).reshape(TILES, 1, 128),
        jnp.repeat(shift, RW).reshape(TILES, 1, 128), *terms, grad_mark
    )

    modes_field = exchange(spec_field)
    modes_grad = exchange(spec_grad)
    back_field, *saved = field_modes(modes_field, lat_tab, spread, w_in, b_in, w_out, b_out)
    gain_now, shift_now, saved[0] = lax.optimization_barrier((gain, shift, saved[0]))
    cubes = jnp.stack([gain_now, shift_now]).reshape(2, CH, 1, 1)
    cubes = jnp.broadcast_to(cubes, (2, CH, 1, 128))
    rows_field = exchange(back_field)
    grad_rows = grad_modes(modes_grad, lat_tab, spread)
    back_grad = pull_modes(grad_rows, saved, lat_tab, spread, w_in, w_out, cubes)
    back_grad, rows_field = lax.optimization_barrier((back_grad, rows_field))
    rows_grad = exchange(back_grad)
    part, back, grad_weights = inverse_call(
        pulled_kernel,
        "pulled",
        [VMEM, HBM, HBM, HBM, VMEM, VMEM],
        [VMEM] * 3,
        [
            jax.ShapeDtypeStruct((CH, RW, LON), f32),
            STATS_SHAPE,
            jax.ShapeDtypeStruct((1, 1152), f32),
        ],
        [pltpu.SemaphoreType.DMA((3,))],
    )(rows_grad, lon_high, tokens, cotangent, stats, cubes)
    back_terms = group_terms(back)
    mixed = inverse_call(
        mixed_kernel,
        "mixed",
        [VMEM, HBM, HBM, VMEM, VMEM, HBM],
        HBM,
        jax.ShapeDtypeStruct((CH, RW, LON), bf16),
        [pltpu.SemaphoreType.DMA((2,)), pltpu.SemaphoreType.DMA((CHUNKS,))],
    )(rows_field, lon_high, tokens, stats, cubes, back)
    grad_tokens = finish(part, tokens, stats, back_terms)
    return (mixed, grad_tokens, grad_weights)


def solution(mesh):
    in_specs = (
        P("grp", "lat", None),
        P("grp", "lat", None),
        P("grp"),
        P("grp"),
        P("grp", None, None, None),
        P("grp", None, None),
        P("grp", None, None, None),
        P("grp", None, None),
    )
    out_specs = (P("grp", "lat", None), P("grp", "lat", None), P("grp", "lat"))
    return jax.shard_map(
        per_device, mesh=mesh, in_specs=in_specs, out_specs=out_specs, check_vma=False
    )
```

```python
import functools
import math

import jax
import jax.numpy as jnp
import ml_dtypes
import numpy as np
from jax import lax
from jax.experimental import pallas as pl
from jax.experimental.pallas import tpu as pltpu
from jax.sharding import PartitionSpec as P

shrink_level = 0.01
norm_eps = 1e-05
f32 = jnp.float32
bf16 = jnp.bfloat16

CH = 96
RW = 8
LON = 1024
HALF = 512
PEERS = 32
LANES = RW * CH
QB = 4
KB = 128
STEPS = 4
TILES = LANES // 128
WIRE_SHAPE = jax.ShapeDtypeStruct((PEERS, TILES, 32, 128), jnp.float32)


def host_split(table):
    high = table.astype(ml_dtypes.bfloat16)
    low = (table - high.astype(np.float64)).astype(ml_dtypes.bfloat16)
    return np.stack([high, low])


def lon_table():
    parts = []
    n = np.arange(HALF)
    for parity in range(2):
        m = 2 * np.arange(256) + parity
        theta = 2.0 * np.pi * ((m[:, None] * n[None, :]) % LON) / LON
        table = np.stack([np.cos(theta), -np.sin(theta)], axis=1).reshape(HALF, HALF)
        parts.append(host_split(table / 32.0))
    return np.stack(parts)


def grad_table():
    parts = []
    n = np.arange(LON)
    for parity in range(2):
        m = 2 * np.arange(256) + parity
        theta = 2.0 * np.pi * ((m[:, None] * n[None, :]) % LON) / LON
        table = np.stack([np.cos(theta), -np.sin(theta)], axis=1)
        table = table * np.where(m == 0, 1.0, 2.0)[:, None, None]
        parts.append(host_split(table.reshape(HALF, LON) / 32.0)[0])
    return np.stack(parts)


def lat_table():
    parts = []
    row = np.arange(RW)[:, None]
    peer = np.arange(16)[None, :]
    place = (8 * peer + row).reshape(-1)
    for parity in range(2):
        k = 2 * np.arange(KB) + parity
        theta = 2.0 * np.pi * ((k[:, None] * place[None, :]) % 256) / 256
        c, s = np.cos(theta), np.sin(theta)
        table = np.concatenate(
            [np.concatenate([c, s], axis=1), np.concatenate([-s, c], axis=1)], axis=0
        )
        parts.append(host_split(table / 16.0))
    return np.stack(parts)


def spread_table():
    table = np.zeros((LANES, RW * 128), ml_dtypes.bfloat16)
    channel, row = np.divmod(np.arange(LANES), RW)
    table[np.arange(LANES), row * 128 + channel] = 1
    return table


def split(value):
    high = value.astype(bf16)
    low = (value - high.astype(f32)).astype(bf16)
    return high, low


def dot(left, right, dims=((1,), (0,))):
    return lax.dot_general(left, right, (dims, ((), ())), preferred_element_type=f32)


NT = ((1,), (1,))
TN = ((0,), (0,))


def dot3(left, right, dims=((1,), (0,))):
    return (
        dot(left[0], right[0], dims) + dot(left[0], right[1], dims) + dot(left[1], right[0], dims)
    )


def in_hbm(value):
    return pltpu.with_memory_space_constraint(value, pltpu.HBM)


CHUNKS = 4
GROUP = CH // CHUNKS


def bring(pairs, sems):
    copies = [pltpu.make_async_copy(src, dst, sems.at[i]) for i, (src, dst) in enumerate(pairs)]
    for copy in copies:
        copy.start()
    return copies


def lon_grad_kernel(
    x_hbm, tab_hbm, sums_ref,
    out_hbm, mark_ref,
    x_ref, tab_ref, wire_ref, in_sems, out_sems,
):
    copies = bring(
        [(x_hbm, x_ref)] + [(tab_hbm.at[p], tab_ref.at[p]) for p in range(2)], in_sems
    )
    mark_ref[...] = jnp.zeros((8, 128), f32)
    out_copies = []
    copies[0].wait()
    for parity in range(2):
        copies[1 + parity].wait()
        value = dot(tab_ref[parity], x_ref[...].reshape(LANES, LON), NT)
        own = pl.ds(parity * 16, 16)
        for tile in range(TILES):
            piece = value[:, tile * 128 : tile * 128 + 128]
            wire_ref[own, tile] = piece.reshape(16, 32, 128)
        copy = pltpu.make_async_copy(wire_ref.at[own], out_hbm.at[own], out_sems.at[parity])
        copy.start()
        out_copies.append(copy)
    for copy in out_copies:
        copy.wait()


def total(terms, at):
    return terms[0][at] + terms[1][at] + terms[2][at] + terms[3][at]


def lon_field_kernel(
    x_ref, tab_hbm, gain_ref, shift_ref, one_ref, two_ref, three_ref, four_ref, mark_ref,
    out_ref, stat_ref,
    tab_ref, halves_ref, tab_sems,
):
    tab_copies = bring([(tab_hbm.at[p], tab_ref.at[p]) for p in range(2)], tab_sems)
    terms = (one_ref, two_ref, three_ref, four_ref)
    count = 4.0 * CH
    mean = total(terms, 0) / count
    inv_std = lax.rsqrt(total(terms, 1) / count - mean * mean + norm_eps)
    stat_ref[0], stat_ref[1] = mean, inv_std
    for tile in range(4):
        pair = []
        for start in (tile * 128, HALF + tile * 128):
            lanes = slice(start, start + 128)
            value = x_ref[:, :, lanes].astype(f32)
            value = (value - mean[:, lanes][None]) * inv_std[:, lanes][None]
            pair.append(value.reshape(LANES, 128))
        for parity, value in enumerate((pair[0] + pair[1], pair[0] - pair[1])):
            high, low = split(value)
            halves_ref[parity, 0, :, tile * 128 : tile * 128 + 128] = high
            halves_ref[parity, 1, :, tile * 128 : tile * 128 + 128] = low
    for parity in range(2):
        tab_copies[parity].wait()
        both = dot(tab_ref[parity].reshape(2 * HALF, HALF), halves_ref[parity, 0], NT)
        value = both[:HALF] + both[HALF:] + dot(tab_ref[parity, 0], halves_ref[parity, 1], NT)
        for tile in range(TILES):
            piece = value[:, tile * 128 : tile * 128 + 128] * gain_ref[tile]
            out_ref[pl.ds(parity * 16, 16), tile] = piece.reshape(16, 32, 128)
    for tile in range(TILES):
        out_ref[0, tile, 0:1, :] = out_ref[0, tile, 0:1, :] + shift_ref[tile] * 32.0


VMEM = pl.BlockSpec(memory_space=pltpu.VMEM)
HBM = pl.BlockSpec(memory_space=pltpu.HBM)
STATS_SHAPE = jax.ShapeDtypeStruct((2, RW, LON), f32)
LON_COST = pl.CostEstimate(
    flops=6 * LANES * LON * LON, bytes_accessed=7 * 2**20, transcendentals=0
)


def lon_grad(cotangent, table, sums):
    return pl.pallas_call(
        lon_grad_kernel,
        name="lon_grad",
        in_specs=[HBM, HBM, VMEM],
        out_specs=[HBM, VMEM],
        out_shape=[
            pltpu.HBM(WIRE_SHAPE.shape, f32),
            jax.ShapeDtypeStruct((8, 128), f32),
        ],
        scratch_shapes=[
            pltpu.VMEM((CH, RW, LON), bf16),
            pltpu.VMEM((2, HALF, LON), bf16),
            pltpu.VMEM((PEERS, TILES, 32, 128), f32),
            pltpu.SemaphoreType.DMA((3,)),
            pltpu.SemaphoreType.DMA((2,)),
        ],
        compiler_params=pltpu.CompilerParams(vmem_limit_bytes=28 * 2**20),
        cost_estimate=LON_COST,
    )(in_hbm(cotangent), in_hbm(table), sums)


def lon_field(tokens, table, *small):
    return pl.pallas_call(
        lon_field_kernel,
        name="lon_field",
        in_specs=[VMEM, HBM] + [VMEM] * len(small),
        out_specs=[VMEM, VMEM],
        out_shape=[WIRE_SHAPE, STATS_SHAPE],
        scratch_shapes=[
            pltpu.VMEM((2, 2, HALF, HALF), bf16),
            pltpu.VMEM((2, 2, LANES, HALF), bf16),
            pltpu.SemaphoreType.DMA((2,)),
        ],
        compiler_params=pltpu.CompilerParams(vmem_limit_bytes=24 * 2**20),
        cost_estimate=LON_COST,
    )(tokens, in_hbm(table), *small)


def unpack_rows(block_ref, spread_ref, rows_ref, halves_ref, terms):
    left = jnp.concatenate([block_ref[:, t].reshape(PEERS * 8, 128) for t in range(TILES)], axis=1)
    value = None
    for _ in range(terms):
        part = left.astype(bf16)
        left = left - part.astype(f32)
        moved = dot(part, spread_ref[...])
        value = moved if value is None else value + moved
    for r in range(RW):
        rows_ref[r, 0 : PEERS * 8] = value[:, r * 128 : r * 128 + 128]
    for q in range(QB):
        for part in range(2):
            for r in range(RW):
                first = rows_ref[r, pl.ds(2 * q + part, 16, stride=8), :]
                second = rows_ref[r, pl.ds(128 + 2 * q + part, 16, stride=8), :]
                for parity, value in enumerate((first + second, first - second)):
                    high, low = split(value)
                    at = (pl.ds((part * RW + r) * 16, 16), pl.ds(q * 128, 128))
                    halves_ref[(parity, 0) + at] = high
                    halves_ref[(parity, 1) + at] = low


def pack_rows(even, odd, spread_ref, rows_ref):
    for q in range(QB):
        lanes = slice(q * 128, q * 128 + 128)
        for part in range(2):
            for r in range(RW):
                at = slice((part * RW + r) * 16, (part * RW + r + 1) * 16)
                first, second = even[at, lanes], odd[at, lanes]
                rows_ref[r, pl.ds(2 * q + part, 16, stride=8), :] = first + second
                rows_ref[r, pl.ds(128 + 2 * q + part, 16, stride=8), :] = first - second
    high, low = split(jnp.concatenate([rows_ref[r, 0 : PEERS * 8] for r in range(RW)], axis=1))
    return dot(high, spread_ref[...], NT) + dot(low, spread_ref[...], NT)


def by_frequency(even, odd):
    rows = []
    for q in range(QB):
        for value in (even, odd):
            lanes = slice(q * 128, q * 128 + 128)
            rows.append(jnp.concatenate([value[0:KB, lanes], value[KB : 2 * KB, lanes]], axis=1))
    return jnp.concatenate(rows, axis=0)


def by_part(rows):
    out = []
    for parity in range(2):
        parts = []
        for part in range(2):
            lanes = slice(part * 128, part * 128 + 128)
            parts.append(
                jnp.concatenate(
                    [rows[(2 * q + parity) * KB : (2 * q + parity + 1) * KB, lanes] for q in range(QB)],
                    axis=1,
                )
            )
        out.append(jnp.concatenate(parts, axis=0))
    return out


def lat_forward(block_ref, tab_ref, spread_ref, rows_ref, halves_ref, terms):
    unpack_rows(block_ref, spread_ref, rows_ref, halves_ref, terms)
    out = [
        dot3(
            (tab_ref[parity, 0], tab_ref[parity, 1]),
            (halves_ref[parity, 0], halves_ref[parity, 1]),
        )
        for parity in range(2)
    ]
    return by_frequency(out[0], out[1])


def lat_inverse(rows, tab_ref, spread_ref, rows_ref):
    high, low = by_part(rows[0]), by_part(rows[1])
    even, odd = [
        dot3((tab_ref[parity, 0], tab_ref[parity, 1]), (high[parity], low[parity]), TN)
        for parity in range(2)
    ]
    wire = pack_rows(even, odd, spread_ref, rows_ref)
    return [wire[:, t * 128 : t * 128 + 128].reshape(PEERS, 8, 128) for t in range(TILES)]


def fill_weight(w_ref, out_ref):
    full = jnp.zeros((256, 256), f32)
    out_ref[...] = full
    real, imag = w_ref[0, 0], w_ref[0, 1]
    out_ref[0:CH, 0:CH] = real
    out_ref[0:CH, 128 : 128 + CH] = imag
    out_ref[128 : 128 + CH, 0:CH] = -imag
    out_ref[128 : 128 + CH, 128 : 128 + CH] = real


def fill_bias(b_ref, out_ref):
    out_ref[...] = jnp.zeros((8, 256), f32)
    out_ref[0:1, 0:CH] = b_ref[0, 0:1, :]
    out_ref[0:1, 128 : 128 + CH] = b_ref[0, 1:2, :]


def grad_modes_kernel(block_ref, tab_ref, spread_ref, out_ref, rows_ref, halves_ref):
    out_ref[...] = lat_forward(block_ref, tab_ref, spread_ref, rows_ref, halves_ref, 2)


def field_modes_kernel(
    block_ref, tab_ref, spread_ref, w_in_ref, b_in_ref, w_out_ref, b_out_ref,
    back_ref, spec_ref, spec_low_ref, act_ref, act_low_ref, mask_ref,
    rows_ref, halves_ref, full_ref, weight_ref, bias_ref,
):
    @pl.when(pl.program_id(0) == 0)
    def _():
        for at, (w_ref, b_ref) in enumerate(((w_in_ref, b_in_ref), (w_out_ref, b_out_ref))):
            fill_weight(w_ref, full_ref)
            weight_ref[at, 0], weight_ref[at, 1] = split(full_ref[...])
            fill_bias(b_ref, bias_ref.at[at])

    spec = split(lat_forward(block_ref, tab_ref, spread_ref, rows_ref, halves_ref, 3))
    spec_ref[...], spec_low_ref[...] = spec
    act = dot3(spec, (weight_ref[0, 0], weight_ref[0, 1])) + bias_ref[0, 0:1, :]
    act = split(jnp.maximum(act, 0.0))
    act_ref[...], act_low_ref[...] = act
    post = dot3(act, (weight_ref[1, 0], weight_ref[1, 1])) + bias_ref[1, 0:1, :]
    mask_ref[...] = jnp.where(jnp.abs(post) > shrink_level, 1.0, 0.0).astype(bf16)
    shrunk = post - jnp.clip(post, -shrink_level, shrink_level)
    for tile, piece in enumerate(lat_inverse(split(shrunk), tab_ref, spread_ref, rows_ref)):
        back_ref[:, tile] = piece


def pull_modes_kernel(
    grad_ref, spec_ref, spec_low_ref, act_ref, act_low_ref, mask_ref, tab_ref, spread_ref,
    w_in_ref, w_out_ref, cubes_hbm,
    back_ref,
    rows_ref, full_ref, weight_ref, sum_ref,
):
    step = pl.program_id(0)

    @pl.when(step == 0)
    def _():
        for at, w_ref in enumerate((w_in_ref, w_out_ref)):
            fill_weight(w_ref, full_ref)
            weight_ref[at, 0], weight_ref[at, 1] = split(full_ref[...])
        sum_ref[...] = jnp.zeros_like(sum_ref)
        back_ref[:, PULL_ROWS - 16 :, :] = jnp.zeros((PEERS, 16, 128), f32)

    spec, act = (spec_ref[...], spec_low_ref[...]), (act_ref[...], act_low_ref[...])
    d_post = split(jnp.where(mask_ref[...].astype(f32) > 0.5, grad_ref[...], 0.0))
    sum_ref[1] += dot3(act, d_post, TN)
    d_act = dot3(d_post, (weight_ref[1, 0], weight_ref[1, 1]), NT)
    d_pre = split(jnp.where(act[0].astype(f32) > 0.0, d_act, 0.0))
    sum_ref[0] += dot3(spec, d_pre, TN)
    d_spec = dot3(d_pre, (weight_ref[0, 0], weight_ref[0, 1]), NT)
    for tile, piece in enumerate(lat_inverse(split(d_spec), tab_ref, spread_ref, rows_ref)):
        back_ref[:, pl.ds(pl.multiple_of(tile * 32 + step * 8, 8), 8), :] = piece

    @pl.when(step == STEPS - 1)
    def _():
        scale = 1.0 / math.sqrt(131072.0)
        for at in range(2):
            total = sum_ref[at] * scale
            rr, ri = total[0:CH, 0:CH], total[0:CH, 128 : 128 + CH]
            ir, ii = total[128 : 128 + CH, 0:CH], total[128 : 128 + CH, 128 : 128 + CH]
            for part, value in enumerate((rr + ii, ri - ir)):
                for k in range(8):
                    peer = (2 * at + part) * 8 + k
                    back_ref[peer, PULL_ROWS - 16 : PULL_ROWS - 4, 0:CH] = value[12 * k : 12 * k + 12]


PULL_ROWS = TILES * 32 + 16
WIRE = pl.BlockSpec((PEERS, TILES, 8, 128), lambda i: (0, 0, i, 0))
LAT_TAB = pl.BlockSpec((2, 2, 256, 256), lambda i: (0, 0, 0, 0))
MODES = pl.BlockSpec((1024, 256), lambda i: (i, 0))
SPREAD = pl.BlockSpec((LANES, RW * 128), lambda i: (0, 0))
ROWS = pltpu.VMEM((RW, PEERS * 8 + 8, 128), f32)
WEIGHT = pl.BlockSpec((1, 2, CH, CH), lambda i: (0, 0, 0, 0))
BIAS = pl.BlockSpec((1, 2, CH), lambda i: (0, 0, 0))


def modes_shape(dtype):
    return jax.ShapeDtypeStruct((4096, 256), dtype)


def grad_modes(block, table, spread):
    return pl.pallas_call(
        grad_modes_kernel,
        name="grad_modes",
        grid=(STEPS,),
        in_specs=[WIRE, LAT_TAB, SPREAD],
        out_specs=MODES,
        out_shape=modes_shape(f32),
        scratch_shapes=[ROWS, pltpu.VMEM((2, 2, 256, QB * 128), bf16)],
        compiler_params=pltpu.CompilerParams(vmem_limit_bytes=36 * 2**20),
        cost_estimate=pl.CostEstimate(
            flops=6 * 2**31, bytes_accessed=8 * 2**20, transcendentals=0
        ),
    )(block, table, spread)


def field_modes(block, table, spread, w_in, b_in, w_out, b_out):
    return pl.pallas_call(
        field_modes_kernel,
        name="field_modes",
        grid=(STEPS,),
        in_specs=[WIRE, LAT_TAB, SPREAD, WEIGHT, BIAS, WEIGHT, BIAS],
        out_specs=[WIRE] + [MODES] * 5,
        out_shape=[WIRE_SHAPE] + [modes_shape(bf16)] * 5,
        scratch_shapes=[
            ROWS,
            pltpu.VMEM((2, 2, 256, QB * 128), bf16),
            pltpu.VMEM((256, 256), f32),
            pltpu.VMEM((2, 2, 256, 256), bf16),
            pltpu.VMEM((2, 8, 256), f32),
        ],
        compiler_params=pltpu.CompilerParams(vmem_limit_bytes=36 * 2**20),
        cost_estimate=pl.CostEstimate(
            flops=12 * 2**31, bytes_accessed=14 * 2**20, transcendentals=0
        ),
    )(block, table, spread, w_in, b_in, w_out, b_out)


def pull_modes(grad, saved, table, spread, w_in, w_out, cubes):
    return pl.pallas_call(
        pull_modes_kernel,
        name="pull_modes",
        grid=(STEPS,),
        in_specs=[MODES] * 6 + [LAT_TAB, SPREAD, WEIGHT, WEIGHT, HBM],
        out_specs=pl.BlockSpec((PEERS, PULL_ROWS, 128), lambda i: (0, 0, 0)),
        out_shape=jax.ShapeDtypeStruct((PEERS, PULL_ROWS, 128), f32),
        scratch_shapes=[
            ROWS,
            pltpu.VMEM((256, 256), f32),
            pltpu.VMEM((2, 2, 256, 256), bf16),
            pltpu.VMEM((2, 256, 256), f32),
        ],
        compiler_params=pltpu.CompilerParams(vmem_limit_bytes=36 * 2**20),
        cost_estimate=pl.CostEstimate(
            flops=8 * 2**31, bytes_accessed=14 * 2**20, transcendentals=0
        ),
    )(grad, *saved, table, spread, w_in, w_out, cubes)


def lon_inverse(take, tab_ref, weighted):
    sides = []
    for parity in range(2):
        value = jnp.concatenate(
            [
                take(slice(parity * 16, parity * 16 + 16), tile).reshape(HALF, 128)
                for tile in range(TILES)
            ],
            axis=1,
        )
        if weighted:
            value = value * 2.0
            if parity == 0:
                row = lax.broadcasted_iota(jnp.int32, (HALF, 1), 0)
                value = value * jnp.where(row == 0, 0.5, 1.0)
        sides.append(dot(value.astype(bf16), tab_ref[parity], TN))
    sums, differences = sides[0] + sides[1], sides[0] - sides[1]
    return [v[:, t * 128 : t * 128 + 128] for v in (sums, differences) for t in range(4)]


def mixed_kernel(
    block_hbm, tab_hbm, tok_hbm, stat_ref, cubes_ref, back_hbm,
    out_hbm,
    tab_ref, tok_ref, mix_ref, block_ref, sems, out_sems,
):
    halves = [
        (block_hbm.at[pl.ds(p * 16, 16)], block_ref.at[pl.ds(p * 16, 16)]) for p in range(2)
    ]
    copies = bring([(tab_hbm, tab_ref)] + halves + [(tok_hbm, tok_ref)], sems)
    copies[0].wait()

    def take(peers, tile):
        if tile == 0:
            copies[1 if peers.start == 0 else 2].wait()
        return block_ref[peers, tile]

    tiles = lon_inverse(take, tab_ref, True)
    copies[3].wait()
    out_copies = []
    for g in range(CHUNKS):
        own = pl.ds(g * GROUP, GROUP)
        gain, shift = cubes_ref[0, own], cubes_ref[1, own]
        for tile in range(8):
            lanes = slice(tile * 128, tile * 128 + 128)
            tok = tok_ref[own, :, lanes].astype(f32)
            normed = (tok - stat_ref[0, :, lanes][None]) * stat_ref[1, :, lanes][None]
            filtered = tiles[tile][g * GROUP * RW : (g + 1) * GROUP * RW].reshape(GROUP, RW, 128)
            mix_ref[own, :, lanes] = (filtered + (normed * gain + shift) + tok).astype(bf16)
        copy = pltpu.make_async_copy(mix_ref.at[own], out_hbm.at[own], out_sems.at[g])
        copy.start()
        out_copies.append(copy)
    for copy in out_copies:
        copy.wait()


def pulled_kernel(
    block_ref, tab_hbm, tok_hbm, cot_hbm, stat_ref, cubes_ref,
    out_ref, sum_ref, weight_ref,
    tab_ref, tok_ref, cot_ref, sems,
):
    copies = bring(((tab_hbm, tab_ref), (tok_hbm, tok_ref), (cot_hbm, cot_ref)), sems)

    def take(peers, tile):
        return block_ref[peers, tile * 32 : tile * 32 + 32, :]

    copies[0].wait()
    tiles = lon_inverse(take, tab_ref, False)
    share = jnp.sum(block_ref[:, PULL_ROWS - 16 :, :], axis=0)
    for i in range(12):
        weight_ref[0:1, i * CH : i * CH + CH] = share[i : i + 1, 0:CH]
    copies[1].wait()
    copies[2].wait()
    for tile in range(8):
        lanes = slice(tile * 128, tile * 128 + 128)
        tok = tok_ref[:, :, lanes].astype(f32)
        inv_std = stat_ref[1, :, lanes]
        normed = (tok - stat_ref[0, :, lanes][None]) * inv_std[None]
        pulled = tiles[tile].reshape(CH, RW, 128)
        cot = cot_ref[:, :, lanes].astype(f32)
        dnorm = (pulled + cot) * cubes_ref[0]
        out_ref[:, :, lanes] = cot + inv_std[None] * dnorm
        sum_ref[0, :, lanes] = jnp.sum(dnorm, axis=0)
        sum_ref[1, :, lanes] = jnp.sum(dnorm * normed, axis=0)


def inverse_call(kernel, name, in_specs, out_specs, out_shape, scratch):
    return pl.pallas_call(
        kernel,
        name=name,
        in_specs=in_specs,
        out_specs=out_specs,
        out_shape=out_shape,
        scratch_shapes=[
            pltpu.VMEM((2, HALF, HALF), bf16),
            pltpu.VMEM((CH, RW, LON), bf16),
            pltpu.VMEM((CH, RW, LON), bf16),
        ]
        + scratch,
        compiler_params=pltpu.CompilerParams(vmem_limit_bytes=28 * 2**20),
        cost_estimate=pl.CostEstimate(
            flops=4 * LANES * LON * LON, bytes_accessed=10 * 2**20, transcendentals=0
        ),
    )


def finish_kernel(part_ref, tok_ref, stat_ref, one_ref, two_ref, three_ref, four_ref, out_ref):
    terms = (one_ref, two_ref, three_ref, four_ref)
    count = 4.0 * CH
    mean, inv_std = stat_ref[0], stat_ref[1]
    one, two = total(terms, 0) / count, total(terms, 1) / count
    normed = (tok_ref[...].astype(f32) - mean[None]) * inv_std[None]
    out_ref[...] = (part_ref[...] - (inv_std * one)[None] - normed * (inv_std * two)[None]).astype(bf16)


def finish(part, tokens, stats, terms):
    block = pl.BlockSpec((CH // 4, RW, LON), lambda i: (i, 0, 0))
    return pl.pallas_call(
        finish_kernel,
        name="finish",
        grid=(4,),
        in_specs=[block, block] + [pl.BlockSpec((2, RW, LON), lambda i: (0, 0, 0))] * 5,
        out_specs=block,
        out_shape=jax.ShapeDtypeStruct((CH, RW, LON), bf16),
        compiler_params=pltpu.CompilerParams(vmem_limit_bytes=24 * 2**20),
        cost_estimate=pl.CostEstimate(
            flops=8 * CH * RW * LON, bytes_accessed=6 * 2**20, transcendentals=0
        ),
    )(part, tokens, stats, *terms)


def exchange(value):
    return lax.all_to_all(value, "lat", split_axis=0, concat_axis=0, tiled=True)


def group_terms(value):
    return [value] + [
        lax.ppermute(value, "grp", [(j, j ^ step) for j in range(4)]) for step in (1, 2, 3)
    ]


def per_device(tokens, cotangent, gain, shift, w_in, b_in, w_out, b_out):
    lon_host = lon_table()
    lon_tab, lon_high = jnp.asarray(lon_host), jnp.asarray(lon_host[:, 0])
    lat_tab, spread = jnp.asarray(lat_table()), jnp.asarray(spread_table())
    tok_val = tokens.astype(f32)
    sums = jnp.stack([jnp.sum(tok_val, axis=0), jnp.sum(tok_val * tok_val, axis=0)])
    terms = group_terms(sums)
    spec_grad, grad_mark = lon_grad(cotangent, jnp.asarray(grad_table()), sums)
    spec_field, stats = lon_field(
        tokens,
        lon_tab,
        jnp.repeat(gain, RW).reshape(TILES, 1, 128),
        jnp.repeat(shift, RW).reshape(TILES, 1, 128),
        *terms,
        grad_mark,
    )

    modes_field = exchange(spec_field)
    modes_grad = exchange(spec_grad)
    back_field, *saved = field_modes(modes_field, lat_tab, spread, w_in, b_in, w_out, b_out)
    gain_now, shift_now, saved[0] = lax.optimization_barrier((gain, shift, saved[0]))
    cubes = jnp.stack([gain_now, shift_now]).reshape(2, CH, 1, 1)
    cubes = jnp.broadcast_to(cubes, (2, CH, 1, 128))
    rows_field = exchange(back_field)
    grad_rows = grad_modes(modes_grad, lat_tab, spread)
    back_grad = pull_modes(grad_rows, saved, lat_tab, spread, w_in, w_out, cubes)
    back_grad, rows_field = lax.optimization_barrier((back_grad, rows_field))
    rows_grad = exchange(back_grad)
    part, back, grad_weights = inverse_call(
        pulled_kernel,
        "pulled",
        [VMEM, HBM, HBM, HBM, VMEM, VMEM],
        [VMEM] * 3,
        [
            jax.ShapeDtypeStruct((CH, RW, LON), f32),
            STATS_SHAPE,
            jax.ShapeDtypeStruct((1, 1152), f32),
        ],
        [pltpu.SemaphoreType.DMA((3,))],
    )(rows_grad, lon_high, tokens, cotangent, stats, cubes)
    back_terms = group_terms(back)
    mixed = inverse_call(
        mixed_kernel,
        "mixed",
        [HBM, HBM, HBM, VMEM, VMEM, HBM],
        HBM,
        jax.ShapeDtypeStruct((CH, RW, LON), bf16),
        [
            pltpu.VMEM((PEERS, TILES, 32, 128), f32),
            pltpu.SemaphoreType.DMA((4,)),
            pltpu.SemaphoreType.DMA((CHUNKS,)),
        ],
    )(in_hbm(rows_field), lon_high, tokens, stats, cubes, back)
    grad_tokens = finish(part, tokens, stats, back_terms)
    return (mixed, grad_tokens, grad_weights)


def solution(mesh):
    in_specs = (
        P("grp", "lat", None),
        P("grp", "lat", None),
        P("grp"),
        P("grp"),
        P("grp", None, None, None),
        P("grp", None, None),
        P("grp", None, None, None),
        P("grp", None, None),
    )
    out_specs = (P("grp", "lat", None), P("grp", "lat", None), P("grp", "lat"))
    return jax.shard_map(
        per_device, mesh=mesh, in_specs=in_specs, out_specs=out_specs, check_vma=False
    )
```

```python
import functools
import math

import jax
import jax.numpy as jnp
import ml_dtypes
import numpy as np
from jax import lax
from jax.experimental import pallas as pl
from jax.experimental.pallas import tpu as pltpu
from jax.sharding import PartitionSpec as P

shrink_level = 0.01
norm_eps = 1e-05
f32 = jnp.float32
bf16 = jnp.bfloat16

CH = 96
RW = 8
LON = 1024
HALF = 512
PEERS = 32
LANES = RW * CH
QB = 4
KB = 128
STEPS = 4
TILES = LANES // 128
WIRE_SHAPE = jax.ShapeDtypeStruct((PEERS, TILES, 32, 128), jnp.float32)


def host_split(table):
    high = table.astype(ml_dtypes.bfloat16)
    low = (table - high.astype(np.float64)).astype(ml_dtypes.bfloat16)
    return np.stack([high, low])


def lon_table():
    parts = []
    n = np.arange(HALF)
    for parity in range(2):
        m = 2 * np.arange(256) + parity
        theta = 2.0 * np.pi * ((m[:, None] * n[None, :]) % LON) / LON
        table = np.stack([np.cos(theta), -np.sin(theta)], axis=1).reshape(HALF, HALF)
        parts.append(host_split(table / 32.0))
    return np.stack(parts)


def grad_table():
    parts = []
    n = np.arange(LON)
    for parity in range(2):
        m = 2 * np.arange(256) + parity
        theta = 2.0 * np.pi * ((m[:, None] * n[None, :]) % LON) / LON
        table = np.stack([np.cos(theta), -np.sin(theta)], axis=1)
        table = table * np.where(m == 0, 1.0, 2.0)[:, None, None]
        parts.append(host_split(table.reshape(HALF, LON) / 32.0)[0])
    return np.stack(parts)


def lat_table():
    parts = []
    row = np.arange(RW)[:, None]
    peer = np.arange(16)[None, :]
    place = (8 * peer + row).reshape(-1)
    for parity in range(2):
        k = 2 * np.arange(KB) + parity
        theta = 2.0 * np.pi * ((k[:, None] * place[None, :]) % 256) / 256
        c, s = np.cos(theta), np.sin(theta)
        table = np.concatenate(
            [np.concatenate([c, s], axis=1), np.concatenate([-s, c], axis=1)], axis=0
        )
        parts.append(host_split(table / 16.0))
    return np.stack(parts)


def spread_table():
    table = np.zeros((LANES, RW * 128), ml_dtypes.bfloat16)
    channel, row = np.divmod(np.arange(LANES), RW)
    table[np.arange(LANES), row * 128 + channel] = 1
    return table


def split(value):
    high = value.astype(bf16)
    low = (value - high.astype(f32)).astype(bf16)
    return high, low


def dot(left, right, dims=((1,), (0,))):
    return lax.dot_general(left, right, (dims, ((), ())), preferred_element_type=f32)


NT = ((1,), (1,))
TN = ((0,), (0,))


def dot3(left, right, dims=((1,), (0,))):
    return (
        dot(left[0], right[0], dims) + dot(left[0], right[1], dims) + dot(left[1], right[0], dims)
    )


def in_hbm(value):
    return pltpu.with_memory_space_constraint(value, pltpu.HBM)


CHUNKS = 4
GROUP = CH // CHUNKS


def bring(pairs, sems):
    copies = [pltpu.make_async_copy(src, dst, sems.at[i]) for i, (src, dst) in enumerate(pairs)]
    for copy in copies:
        copy.start()
    return copies


def lon_grad_kernel(
    x_hbm, tab_hbm, sums_ref,
    out_hbm, mark_ref,
    x_ref, tab_ref, wire_ref, in_sems, out_sems,
):
    copies = bring(
        [(x_hbm, x_ref)] + [(tab_hbm.at[p], tab_ref.at[p]) for p in range(2)], in_sems
    )
    mark_ref[...] = jnp.zeros((8, 128), f32)
    out_copies = []
    copies[0].wait()
    for parity in range(2):
        copies[1 + parity].wait()
        value = dot(tab_ref[parity], x_ref[...].reshape(LANES, LON), NT)
        own = pl.ds(parity * 16, 16)
        for tile in range(TILES):
            piece = value[:, tile * 128 : tile * 128 + 128]
            wire_ref[own, tile] = piece.reshape(16, 32, 128)
        copy = pltpu.make_async_copy(wire_ref.at[own], out_hbm.at[own], out_sems.at[parity])
        copy.start()
        out_copies.append(copy)
    for copy in out_copies:
        copy.wait()


def total(terms, at):
    return terms[0][at] + terms[1][at] + terms[2][at] + terms[3][at]


def lon_field_kernel(
    x_ref, tab_hbm, gain_ref, shift_ref, one_ref, two_ref, three_ref, four_ref, mark_ref,
    out_ref, stat_ref,
    tab_ref, halves_ref, tab_sems,
):
    tab_copies = bring([(tab_hbm.at[p], tab_ref.at[p]) for p in range(2)], tab_sems)
    terms = (one_ref, two_ref, three_ref, four_ref)
    count = 4.0 * CH
    mean = total(terms, 0) / count
    inv_std = lax.rsqrt(total(terms, 1) / count - mean * mean + norm_eps)
    stat_ref[0], stat_ref[1] = mean, inv_std
    for tile in range(4):
        pair = []
        for start in (tile * 128, HALF + tile * 128):
            lanes = slice(start, start + 128)
            value = x_ref[:, :, lanes].astype(f32)
            value = (value - mean[:, lanes][None]) * inv_std[:, lanes][None]
            pair.append(value.reshape(LANES, 128))
        for parity, value in enumerate((pair[0] + pair[1], pair[0] - pair[1])):
            high, low = split(value)
            halves_ref[parity, 0, :, tile * 128 : tile * 128 + 128] = high
            halves_ref[parity, 1, :, tile * 128 : tile * 128 + 128] = low
    for parity in range(2):
        tab_copies[parity].wait()
        both = dot(tab_ref[parity].reshape(2 * HALF, HALF), halves_ref[parity, 0], NT)
        value = both[:HALF] + both[HALF:] + dot(tab_ref[parity, 0], halves_ref[parity, 1], NT)
        for tile in range(TILES):
            piece = value[:, tile * 128 : tile * 128 + 128] * gain_ref[tile]
            out_ref[pl.ds(parity * 16, 16), tile] = piece.reshape(16, 32, 128)
    for tile in range(TILES):
        out_ref[0, tile, 0:1, :] = out_ref[0, tile, 0:1, :] + shift_ref[tile] * 32.0


VMEM = pl.BlockSpec(memory_space=pltpu.VMEM)
HBM = pl.BlockSpec(memory_space=pltpu.HBM)
STATS_SHAPE = jax.ShapeDtypeStruct((2, RW, LON), f32)
LON_COST = pl.CostEstimate(
    flops=6 * LANES * LON * LON, bytes_accessed=7 * 2**20, transcendentals=0
)


def lon_grad(cotangent, table, sums):
    return pl.pallas_call(
        lon_grad_kernel,
        name="lon_grad",
        in_specs=[HBM, HBM, VMEM],
        out_specs=[HBM, VMEM],
        out_shape=[
            pltpu.HBM(WIRE_SHAPE.shape, f32),
            jax.ShapeDtypeStruct((8, 128), f32),
        ],
        scratch_shapes=[
            pltpu.VMEM((CH, RW, LON), bf16),
            pltpu.VMEM((2, HALF, LON), bf16),
            pltpu.VMEM((PEERS, TILES, 32, 128), f32),
            pltpu.SemaphoreType.DMA((3,)),
            pltpu.SemaphoreType.DMA((2,)),
        ],
        compiler_params=pltpu.CompilerParams(vmem_limit_bytes=28 * 2**20),
        cost_estimate=LON_COST,
    )(in_hbm(cotangent), in_hbm(table), sums)


def lon_field(tokens, table, *small):
    return pl.pallas_call(
        lon_field_kernel,
        name="lon_field",
        in_specs=[VMEM, HBM] + [VMEM] * len(small),
        out_specs=[VMEM, VMEM],
        out_shape=[WIRE_SHAPE, STATS_SHAPE],
        scratch_shapes=[
            pltpu.VMEM((2, 2, HALF, HALF), bf16),
            pltpu.VMEM((2, 2, LANES, HALF), bf16),
            pltpu.SemaphoreType.DMA((2,)),
        ],
        compiler_params=pltpu.CompilerParams(vmem_limit_bytes=24 * 2**20),
        cost_estimate=LON_COST,
    )(tokens, in_hbm(table), *small)


def unpack_rows(block_ref, spread_ref, rows_ref, halves_ref, terms):
    left = jnp.concatenate([block_ref[:, t].reshape(PEERS * 8, 128) for t in range(TILES)], axis=1)
    value = None
    for _ in range(terms):
        part = left.astype(bf16)
        left = left - part.astype(f32)
        moved = dot(part, spread_ref[...])
        value = moved if value is None else value + moved
    for r in range(RW):
        rows_ref[r, 0 : PEERS * 8] = value[:, r * 128 : r * 128 + 128]
    for q in range(QB):
        for part in range(2):
            for r in range(RW):
                first = rows_ref[r, pl.ds(2 * q + part, 16, stride=8), :]
                second = rows_ref[r, pl.ds(128 + 2 * q + part, 16, stride=8), :]
                for parity, value in enumerate((first + second, first - second)):
                    high, low = split(value)
                    at = (pl.ds((part * RW + r) * 16, 16), pl.ds(q * 128, 128))
                    halves_ref[(parity, 0) + at] = high
                    halves_ref[(parity, 1) + at] = low


def pack_rows(even, odd, spread_ref, rows_ref):
    for q in range(QB):
        lanes = slice(q * 128, q * 128 + 128)
        for part in range(2):
            for r in range(RW):
                at = slice((part * RW + r) * 16, (part * RW + r + 1) * 16)
                first, second = even[at, lanes], odd[at, lanes]
                rows_ref[r, pl.ds(2 * q + part, 16, stride=8), :] = first + second
                rows_ref[r, pl.ds(128 + 2 * q + part, 16, stride=8), :] = first - second
    high, low = split(jnp.concatenate([rows_ref[r, 0 : PEERS * 8] for r in range(RW)], axis=1))
    return dot(high, spread_ref[...], NT) + dot(low, spread_ref[...], NT)


def by_frequency(even, odd):
    rows = []
    for q in range(QB):
        for value in (even, odd):
            lanes = slice(q * 128, q * 128 + 128)
            rows.append(jnp.concatenate([value[0:KB, lanes], value[KB : 2 * KB, lanes]], axis=1))
    return jnp.concatenate(rows, axis=0)


def by_part(rows):
    out = []
    for parity in range(2):
        parts = []
        for part in range(2):
            lanes = slice(part * 128, part * 128 + 128)
            parts.append(
                jnp.concatenate(
                    [rows[(2 * q + parity) * KB : (2 * q + parity + 1) * KB, lanes] for q in range(QB)],
                    axis=1,
                )
            )
        out.append(jnp.concatenate(parts, axis=0))
    return out


def lat_forward(block_ref, tab_ref, spread_ref, rows_ref, halves_ref, terms):
    unpack_rows(block_ref, spread_ref, rows_ref, halves_ref, terms)
    out = [
        dot3(
            (tab_ref[parity, 0], tab_ref[parity, 1]),
            (halves_ref[parity, 0], halves_ref[parity, 1]),
        )
        for parity in range(2)
    ]
    return by_frequency(out[0], out[1])


def lat_inverse(rows, tab_ref, spread_ref, rows_ref):
    high, low = by_part(rows[0]), by_part(rows[1])
    even, odd = [
        dot3((tab_ref[parity, 0], tab_ref[parity, 1]), (high[parity], low[parity]), TN)
        for parity in range(2)
    ]
    wire = pack_rows(even, odd, spread_ref, rows_ref)
    return [wire[:, t * 128 : t * 128 + 128].reshape(PEERS, 8, 128) for t in range(TILES)]


def fill_weight(w_ref, out_ref):
    full = jnp.zeros((256, 256), f32)
    out_ref[...] = full
    real, imag = w_ref[0, 0], w_ref[0, 1]
    out_ref[0:CH, 0:CH] = real
    out_ref[0:CH, 128 : 128 + CH] = imag
    out_ref[128 : 128 + CH, 0:CH] = -imag
    out_ref[128 : 128 + CH, 128 : 128 + CH] = real


def fill_bias(b_ref, out_ref):
    out_ref[...] = jnp.zeros((8, 256), f32)
    out_ref[0:1, 0:CH] = b_ref[0, 0:1, :]
    out_ref[0:1, 128 : 128 + CH] = b_ref[0, 1:2, :]


def grad_modes_kernel(block_ref, tab_ref, spread_ref, out_ref, rows_ref, halves_ref):
    out_ref[...] = lat_forward(block_ref, tab_ref, spread_ref, rows_ref, halves_ref, 2)


def field_modes_kernel(
    block_ref, tab_ref, spread_ref, w_in_ref, b_in_ref, w_out_ref, b_out_ref,
    back_ref, spec_ref, spec_low_ref, act_ref, act_low_ref, mask_ref,
    rows_ref, halves_ref, full_ref, weight_ref, bias_ref,
):
    @pl.when(pl.program_id(0) == 0)
    def _():
        for at, (w_ref, b_ref) in enumerate(((w_in_ref, b_in_ref), (w_out_ref, b_out_ref))):
            fill_weight(w_ref, full_ref)
            weight_ref[at, 0], weight_ref[at, 1] = split(full_ref[...])
            fill_bias(b_ref, bias_ref.at[at])

    spec = split(lat_forward(block_ref, tab_ref, spread_ref, rows_ref, halves_ref, 3))
    spec_ref[...], spec_low_ref[...] = spec
    act = dot3(spec, (weight_ref[0, 0], weight_ref[0, 1])) + bias_ref[0, 0:1, :]
    act = split(jnp.maximum(act, 0.0))
    act_ref[...], act_low_ref[...] = act
    post = dot3(act, (weight_ref[1, 0], weight_ref[1, 1])) + bias_ref[1, 0:1, :]
    mask_ref[...] = jnp.where(jnp.abs(post) > shrink_level, 1.0, 0.0).astype(bf16)
    shrunk = post - jnp.clip(post, -shrink_level, shrink_level)
    for tile, piece in enumerate(lat_inverse(split(shrunk), tab_ref, spread_ref, rows_ref)):
        back_ref[:, tile] = piece


def pull_modes_kernel(
    grad_ref, spec_ref, spec_low_ref, act_ref, act_low_ref, mask_ref, tab_ref, spread_ref,
    w_in_ref, w_out_ref, cubes_hbm,
    back_ref,
    rows_ref, full_ref, weight_ref, sum_ref,
):
    step = pl.program_id(0)

    @pl.when(step == 0)
    def _():
        for at, w_ref in enumerate((w_in_ref, w_out_ref)):
            fill_weight(w_ref, full_ref)
            weight_ref[at, 0], weight_ref[at, 1] = split(full_ref[...])
        sum_ref[...] = jnp.zeros_like(sum_ref)
        back_ref[:, PULL_ROWS - 16 :, :] = jnp.zeros((PEERS, 16, 128), f32)

    spec, act = (spec_ref[...], spec_low_ref[...]), (act_ref[...], act_low_ref[...])
    d_post = split(jnp.where(mask_ref[...].astype(f32) > 0.5, grad_ref[...], 0.0))
    sum_ref[1] += dot3(act, d_post, TN)
    d_act = dot3(d_post, (weight_ref[1, 0], weight_ref[1, 1]), NT)
    d_pre = split(jnp.where(act[0].astype(f32) > 0.0, d_act, 0.0))
    sum_ref[0] += dot3(spec, d_pre, TN)
    d_spec = dot3(d_pre, (weight_ref[0, 0], weight_ref[0, 1]), NT)
    for tile, piece in enumerate(lat_inverse(split(d_spec), tab_ref, spread_ref, rows_ref)):
        back_ref[:, pl.ds(pl.multiple_of(tile * 32 + step * 8, 8), 8), :] = piece

    @pl.when(step == STEPS - 1)
    def _():
        scale = 1.0 / math.sqrt(131072.0)
        for at in range(2):
            total = sum_ref[at] * scale
            rr, ri = total[0:CH, 0:CH], total[0:CH, 128 : 128 + CH]
            ir, ii = total[128 : 128 + CH, 0:CH], total[128 : 128 + CH, 128 : 128 + CH]
            for part, value in enumerate((rr + ii, ri - ir)):
                for k in range(8):
                    peer = (2 * at + part) * 8 + k
                    back_ref[peer, PULL_ROWS - 16 : PULL_ROWS - 4, 0:CH] = value[12 * k : 12 * k + 12]


PULL_ROWS = TILES * 32 + 16
WIRE = pl.BlockSpec((PEERS, TILES, 8, 128), lambda i: (0, 0, i, 0))
LAT_TAB = pl.BlockSpec((2, 2, 256, 256), lambda i: (0, 0, 0, 0))
MODES = pl.BlockSpec((1024, 256), lambda i: (i, 0))
SPREAD = pl.BlockSpec((LANES, RW * 128), lambda i: (0, 0))
ROWS = pltpu.VMEM((RW, PEERS * 8 + 8, 128), f32)
WEIGHT = pl.BlockSpec((1, 2, CH, CH), lambda i: (0, 0, 0, 0))
BIAS = pl.BlockSpec((1, 2, CH), lambda i: (0, 0, 0))


def modes_shape(dtype):
    return jax.ShapeDtypeStruct((4096, 256), dtype)


def grad_modes(block, table, spread):
    return pl.pallas_call(
        grad_modes_kernel,
        name="grad_modes",
        grid=(STEPS,),
        in_specs=[WIRE, LAT_TAB, SPREAD],
        out_specs=MODES,
        out_shape=modes_shape(f32),
        scratch_shapes=[ROWS, pltpu.VMEM((2, 2, 256, QB * 128), bf16)],
        compiler_params=pltpu.CompilerParams(vmem_limit_bytes=36 * 2**20),
        cost_estimate=pl.CostEstimate(
            flops=6 * 2**31, bytes_accessed=8 * 2**20, transcendentals=0
        ),
    )(block, table, spread)


def field_modes(block, table, spread, w_in, b_in, w_out, b_out):
    return pl.pallas_call(
        field_modes_kernel,
        name="field_modes",
        grid=(STEPS,),
        in_specs=[WIRE, LAT_TAB, SPREAD, WEIGHT, BIAS, WEIGHT, BIAS],
        out_specs=[WIRE] + [MODES] * 5,
        out_shape=[WIRE_SHAPE] + [modes_shape(bf16)] * 5,
        scratch_shapes=[
            ROWS,
            pltpu.VMEM((2, 2, 256, QB * 128), bf16),
            pltpu.VMEM((256, 256), f32),
            pltpu.VMEM((2, 2, 256, 256), bf16),
            pltpu.VMEM((2, 8, 256), f32),
        ],
        compiler_params=pltpu.CompilerParams(vmem_limit_bytes=36 * 2**20),
        cost_estimate=pl.CostEstimate(
            flops=12 * 2**31, bytes_accessed=14 * 2**20, transcendentals=0
        ),
    )(block, table, spread, w_in, b_in, w_out, b_out)


def pull_modes(grad, saved, table, spread, w_in, w_out, cubes):
    return pl.pallas_call(
        pull_modes_kernel,
        name="pull_modes",
        grid=(STEPS,),
        in_specs=[MODES] * 6 + [LAT_TAB, SPREAD, WEIGHT, WEIGHT, HBM],
        out_specs=pl.BlockSpec((PEERS, PULL_ROWS, 128), lambda i: (0, 0, 0)),
        out_shape=jax.ShapeDtypeStruct((PEERS, PULL_ROWS, 128), f32),
        scratch_shapes=[
            ROWS,
            pltpu.VMEM((256, 256), f32),
            pltpu.VMEM((2, 2, 256, 256), bf16),
            pltpu.VMEM((2, 256, 256), f32),
        ],
        compiler_params=pltpu.CompilerParams(vmem_limit_bytes=36 * 2**20),
        cost_estimate=pl.CostEstimate(
            flops=8 * 2**31, bytes_accessed=14 * 2**20, transcendentals=0
        ),
    )(grad, *saved, table, spread, w_in, w_out, cubes)


def lon_inverse(take, tab_ref, weighted):
    sides = []
    for parity in range(2):
        value = jnp.concatenate(
            [
                take(slice(parity * 16, parity * 16 + 16), tile).reshape(HALF, 128)
                for tile in range(TILES)
            ],
            axis=1,
        )
        if weighted:
            value = value * 2.0
            if parity == 0:
                row = lax.broadcasted_iota(jnp.int32, (HALF, 1), 0)
                value = value * jnp.where(row == 0, 0.5, 1.0)
        sides.append(dot(value.astype(bf16), tab_ref[parity], TN))
    sums, differences = sides[0] + sides[1], sides[0] - sides[1]
    return [v[:, t * 128 : t * 128 + 128] for v in (sums, differences) for t in range(4)]


def mixed_kernel(
    block_hbm, tab_ref, tok_ref, stat_ref, cubes_ref, back_hbm,
    out_hbm,
    mix_ref, block_ref, sems, out_sems,
):
    halves = [
        (block_hbm.at[pl.ds(p * 16, 16)], block_ref.at[pl.ds(p * 16, 16)]) for p in range(2)
    ]
    copies = bring(halves, sems)

    def take(peers, tile):
        if tile == 0:
            copies[0 if peers.start == 0 else 1].wait()
        return block_ref[peers, tile]

    tiles = lon_inverse(take, tab_ref, True)
    out_copies = []
    for g in range(CHUNKS):
        own = pl.ds(g * GROUP, GROUP)
        gain, shift = cubes_ref[0, own], cubes_ref[1, own]
        for tile in range(8):
            lanes = slice(tile * 128, tile * 128 + 128)
            tok = tok_ref[own, :, lanes].astype(f32)
            normed = (tok - stat_ref[0, :, lanes][None]) * stat_ref[1, :, lanes][None]
            filtered = tiles[tile][g * GROUP * RW : (g + 1) * GROUP * RW].reshape(GROUP, RW, 128)
            mix_ref[own, :, lanes] = (filtered + (normed * gain + shift) + tok).astype(bf16)
        copy = pltpu.make_async_copy(mix_ref.at[own], out_hbm.at[own], out_sems.at[g])
        copy.start()
        out_copies.append(copy)
    for copy in out_copies:
        copy.wait()


def pulled_kernel(
    block_ref, tab_ref, tok_ref, cot_ref, stat_ref, cubes_ref,
    out_ref, sum_ref, weight_ref,
):
    def take(peers, tile):
        return block_ref[peers, tile * 32 : tile * 32 + 32, :]

    tiles = lon_inverse(take, tab_ref, False)
    share = jnp.sum(block_ref[:, PULL_ROWS - 16 :, :], axis=0)
    for i in range(12):
        weight_ref[0:1, i * CH : i * CH + CH] = share[i : i + 1, 0:CH]
    for tile in range(8):
        lanes = slice(tile * 128, tile * 128 + 128)
        tok = tok_ref[:, :, lanes].astype(f32)
        inv_std = stat_ref[1, :, lanes]
        normed = (tok - stat_ref[0, :, lanes][None]) * inv_std[None]
        pulled = tiles[tile].reshape(CH, RW, 128)
        cot = cot_ref[:, :, lanes].astype(f32)
        dnorm = (pulled + cot) * cubes_ref[0]
        out_ref[:, :, lanes] = cot + inv_std[None] * dnorm
        sum_ref[0, :, lanes] = jnp.sum(dnorm, axis=0)
        sum_ref[1, :, lanes] = jnp.sum(dnorm * normed, axis=0)


def inverse_call(kernel, name, in_specs, out_specs, out_shape, scratch):
    return pl.pallas_call(
        kernel,
        name=name,
        in_specs=in_specs,
        out_specs=out_specs,
        out_shape=out_shape,
        scratch_shapes=scratch,
        compiler_params=pltpu.CompilerParams(vmem_limit_bytes=28 * 2**20),
        cost_estimate=pl.CostEstimate(
            flops=4 * LANES * LON * LON, bytes_accessed=10 * 2**20, transcendentals=0
        ),
    )


def finish_kernel(
    part_ref, tok_ref, stat_ref, one_ref, two_ref, three_ref, four_ref,
    out_hbm,
    own_ref, sems,
):
    terms = (one_ref, two_ref, three_ref, four_ref)
    count = 4.0 * CH
    mean, inv_std = stat_ref[0], stat_ref[1]
    one, two = inv_std * total(terms, 0) / count, inv_std * total(terms, 1) / count
    scale = inv_std * two
    level = one - mean * scale
    copies = []
    for g in range(CHUNKS):
        own = pl.ds(g * GROUP, GROUP)
        value = part_ref[own] - level[None] - tok_ref[own].astype(f32) * scale[None]
        own_ref[own] = value.astype(bf16)
        copy = pltpu.make_async_copy(own_ref.at[own], out_hbm.at[own], sems.at[g])
        copy.start()
        copies.append(copy)
    for copy in copies:
        copy.wait()


def finish(part, tokens, stats, terms):
    return pl.pallas_call(
        finish_kernel,
        name="finish",
        in_specs=[VMEM] * 7,
        out_specs=HBM,
        out_shape=jax.ShapeDtypeStruct((CH, RW, LON), bf16),
        scratch_shapes=[pltpu.VMEM((CH, RW, LON), bf16), pltpu.SemaphoreType.DMA((CHUNKS,))],
        compiler_params=pltpu.CompilerParams(vmem_limit_bytes=20 * 2**20),
        cost_estimate=pl.CostEstimate(
            flops=8 * CH * RW * LON, bytes_accessed=6 * 2**20, transcendentals=0
        ),
    )(part, tokens, stats, *terms)


def exchange(value):
    return lax.all_to_all(value, "lat", split_axis=0, concat_axis=0, tiled=True)


def group_terms(value):
    return [value] + [
        lax.ppermute(value, "grp", [(j, j ^ step) for j in range(4)]) for step in (1, 2, 3)
    ]


def per_device(tokens, cotangent, gain, shift, w_in, b_in, w_out, b_out):
    lon_host = lon_table()
    lon_tab, lon_high = jnp.asarray(lon_host), jnp.asarray(lon_host[:, 0])
    lat_tab, spread = jnp.asarray(lat_table()), jnp.asarray(spread_table())
    tok_val = tokens.astype(f32)
    sums = jnp.stack([jnp.sum(tok_val, axis=0), jnp.sum(tok_val * tok_val, axis=0)])
    terms = group_terms(sums)
    spec_grad, grad_mark = lon_grad(cotangent, jnp.asarray(grad_table()), sums)
    spec_field, stats = lon_field(
        tokens,
        lon_tab,
        jnp.repeat(gain, RW).reshape(TILES, 1, 128),
        jnp.repeat(shift, RW).reshape(TILES, 1, 128),
        *terms,
        grad_mark,
    )

    modes_field = exchange(spec_field)
    modes_grad = exchange(spec_grad)
    back_field, *saved = field_modes(modes_field, lat_tab, spread, w_in, b_in, w_out, b_out)
    gain_now, shift_now, saved[0] = lax.optimization_barrier((gain, shift, saved[0]))
    cubes = jnp.stack([gain_now, shift_now]).reshape(2, CH, 1, 1)
    cubes = jnp.broadcast_to(cubes, (2, CH, 1, 128))
    rows_field = exchange(back_field)
    grad_rows = grad_modes(modes_grad, lat_tab, spread)
    back_grad = pull_modes(grad_rows, saved, lat_tab, spread, w_in, w_out, cubes)
    back_grad, rows_field = lax.optimization_barrier((back_grad, rows_field))
    rows_grad = exchange(back_grad)
    part, back, grad_weights = inverse_call(
        pulled_kernel,
        "pulled",
        [VMEM] * 6,
        [VMEM] * 3,
        [
            jax.ShapeDtypeStruct((CH, RW, LON), f32),
            STATS_SHAPE,
            jax.ShapeDtypeStruct((1, 1152), f32),
        ],
        [],
    )(rows_grad, lon_high, tokens, cotangent, stats, cubes)
    back_terms = group_terms(back)
    mixed = inverse_call(
        mixed_kernel,
        "mixed",
        [HBM, VMEM, VMEM, VMEM, VMEM, HBM],
        HBM,
        jax.ShapeDtypeStruct((CH, RW, LON), bf16),
        [
            pltpu.VMEM((CH, RW, LON), bf16),
            pltpu.VMEM((PEERS, TILES, 32, 128), f32),
            pltpu.SemaphoreType.DMA((2,)),
            pltpu.SemaphoreType.DMA((CHUNKS,)),
        ],
    )(in_hbm(rows_field), lon_high, tokens, stats, cubes, back)
    grad_tokens = finish(part, tokens, stats, back_terms)
    return (mixed, grad_tokens, grad_weights)


def solution(mesh):
    in_specs = (
        P("grp", "lat", None),
        P("grp", "lat", None),
        P("grp"),
        P("grp"),
        P("grp", None, None, None),
        P("grp", None, None),
        P("grp", None, None, None),
        P("grp", None, None),
    )
    out_specs = (P("grp", "lat", None), P("grp", "lat", None), P("grp", "lat"))
    return jax.shard_map(
        per_device, mesh=mesh, in_specs=in_specs, out_specs=out_specs, check_vma=False
    )
```

```python
import functools
import math

import jax
import jax.numpy as jnp
import ml_dtypes
import numpy as np
from jax import lax
from jax.experimental import pallas as pl
from jax.experimental.pallas import tpu as pltpu
from jax.sharding import PartitionSpec as P

shrink_level = 0.01
norm_eps = 1e-05
f32 = jnp.float32
bf16 = jnp.bfloat16

CH = 96
RW = 8
LON = 1024
HALF = 512
PEERS = 32
LANES = RW * CH
QB = 4
KB = 128
STEPS = 4
TILES = LANES // 128
WIRE_SHAPE = jax.ShapeDtypeStruct((PEERS, TILES, 32, 128), jnp.float32)


def host_split(table):
    high = table.astype(ml_dtypes.bfloat16)
    low = (table - high.astype(np.float64)).astype(ml_dtypes.bfloat16)
    return np.stack([high, low])


def lon_table():
    parts = []
    n = np.arange(HALF)
    for parity in range(2):
        m = 2 * np.arange(256) + parity
        theta = 2.0 * np.pi * ((m[:, None] * n[None, :]) % LON) / LON
        table = np.stack([np.cos(theta), -np.sin(theta)], axis=1).reshape(HALF, HALF)
        parts.append(host_split(table / 32.0))
    return np.stack(parts)


def grad_table():
    parts = []
    n = np.arange(LON)
    for parity in range(2):
        m = 2 * np.arange(256) + parity
        theta = 2.0 * np.pi * ((m[:, None] * n[None, :]) % LON) / LON
        table = np.stack([np.cos(theta), -np.sin(theta)], axis=1)
        table = table * np.where(m == 0, 1.0, 2.0)[:, None, None]
        parts.append(host_split(table.reshape(HALF, LON) / 32.0)[0])
    return np.stack(parts)


def lat_table():
    parts = []
    row = np.arange(RW)[:, None]
    peer = np.arange(16)[None, :]
    place = (8 * peer + row).reshape(-1)
    for parity in range(2):
        k = 2 * np.arange(KB) + parity
        theta = 2.0 * np.pi * ((k[:, None] * place[None, :]) % 256) / 256
        c, s = np.cos(theta), np.sin(theta)
        table = np.concatenate(
            [np.concatenate([c, s], axis=1), np.concatenate([-s, c], axis=1)], axis=0
        )
        parts.append(host_split(table / 16.0))
    return np.stack(parts)


def spread_table():
    table = np.zeros((LANES, RW * 128), ml_dtypes.bfloat16)
    channel, row = np.divmod(np.arange(LANES), RW)
    table[np.arange(LANES), row * 128 + channel] = 1
    return table


def split(value):
    high = value.astype(bf16)
    low = (value - high.astype(f32)).astype(bf16)
    return high, low


def dot(left, right, dims=((1,), (0,))):
    return lax.dot_general(left, right, (dims, ((), ())), preferred_element_type=f32)


NT = ((1,), (1,))
TN = ((0,), (0,))


def dot3(left, right, dims=((1,), (0,))):
    return (
        dot(left[0], right[0], dims) + dot(left[0], right[1], dims) + dot(left[1], right[0], dims)
    )


def in_hbm(value):
    return pltpu.with_memory_space_constraint(value, pltpu.HBM)


CHUNKS = 4
GROUP = CH // CHUNKS


def bring(pairs, sems):
    copies = [pltpu.make_async_copy(src, dst, sems.at[i]) for i, (src, dst) in enumerate(pairs)]
    for copy in copies:
        copy.start()
    return copies


def sums_kernel(x_hbm, out_ref, x_ref, sems):
    parts = [pl.ds(g * GROUP, GROUP) for g in range(CHUNKS)]
    copies = bring([(x_hbm.at[own], x_ref.at[own]) for own in parts], sems)
    for g, own in enumerate(parts):
        copies[g].wait()
        for tile in range(8):
            lanes = slice(tile * 128, tile * 128 + 128)
            value = x_ref[own, :, lanes].astype(f32)
            for at, term in enumerate((value, value * value)):
                term = jnp.sum(term, axis=0)
                out_ref[at, :, lanes] = term if g == 0 else out_ref[at, :, lanes] + term


def lon_grad_kernel(
    x_hbm, tab_hbm, sums_ref,
    out_hbm, mark_ref,
    x_ref, tab_ref, wire_ref, in_sems, out_sems,
):
    copies = bring(
        [(x_hbm, x_ref)] + [(tab_hbm.at[p], tab_ref.at[p]) for p in range(2)], in_sems
    )
    mark_ref[...] = jnp.zeros((8, 128), f32)
    out_copies = []
    copies[0].wait()
    for parity in range(2):
        copies[1 + parity].wait()
        value = dot(tab_ref[parity], x_ref[...].reshape(LANES, LON), NT)
        own = pl.ds(parity * 16, 16)
        for tile in range(TILES):
            piece = value[:, tile * 128 : tile * 128 + 128]
            wire_ref[own, tile] = piece.reshape(16, 32, 128)
        copy = pltpu.make_async_copy(wire_ref.at[own], out_hbm.at[own], out_sems.at[parity])
        copy.start()
        out_copies.append(copy)
    for copy in out_copies:
        copy.wait()


def total(terms, at):
    return terms[0][at] + terms[1][at] + terms[2][at] + terms[3][at]


def lon_field_kernel(
    x_ref, tab_hbm, gain_ref, shift_ref, one_ref, two_ref, three_ref, four_ref, mark_ref,
    out_ref, stat_ref,
    tab_ref, halves_ref, tab_sems,
):
    tab_copies = bring([(tab_hbm.at[p], tab_ref.at[p]) for p in range(2)], tab_sems)
    terms = (one_ref, two_ref, three_ref, four_ref)
    count = 4.0 * CH
    mean = total(terms, 0) / count
    inv_std = lax.rsqrt(total(terms, 1) / count - mean * mean + norm_eps)
    stat_ref[0], stat_ref[1] = mean, inv_std
    for tile in range(4):
        pair = []
        for start in (tile * 128, HALF + tile * 128):
            lanes = slice(start, start + 128)
            value = x_ref[:, :, lanes].astype(f32)
            value = (value - mean[:, lanes][None]) * inv_std[:, lanes][None]
            pair.append(value.reshape(LANES, 128))
        for parity, value in enumerate((pair[0] + pair[1], pair[0] - pair[1])):
            high, low = split(value)
            halves_ref[parity, 0, :, tile * 128 : tile * 128 + 128] = high
            halves_ref[parity, 1, :, tile * 128 : tile * 128 + 128] = low
    for parity in range(2):
        tab_copies[parity].wait()
        both = dot(tab_ref[parity].reshape(2 * HALF, HALF), halves_ref[parity, 0], NT)
        value = both[:HALF] + both[HALF:] + dot(tab_ref[parity, 0], halves_ref[parity, 1], NT)
        for tile in range(TILES):
            piece = value[:, tile * 128 : tile * 128 + 128] * gain_ref[tile]
            out_ref[pl.ds(parity * 16, 16), tile] = piece.reshape(16, 32, 128)
    for tile in range(TILES):
        out_ref[0, tile, 0:1, :] = out_ref[0, tile, 0:1, :] + shift_ref[tile] * 32.0


VMEM = pl.BlockSpec(memory_space=pltpu.VMEM)
HBM = pl.BlockSpec(memory_space=pltpu.HBM)
STATS_SHAPE = jax.ShapeDtypeStruct((2, RW, LON), f32)
LON_COST = pl.CostEstimate(
    flops=6 * LANES * LON * LON, bytes_accessed=7 * 2**20, transcendentals=0
)


def token_sums(tokens):
    return pl.pallas_call(
        sums_kernel,
        name="token_sums",
        in_specs=[HBM],
        out_specs=VMEM,
        out_shape=STATS_SHAPE,
        scratch_shapes=[pltpu.VMEM((CH, RW, LON), bf16), pltpu.SemaphoreType.DMA((CHUNKS,))],
        compiler_params=pltpu.CompilerParams(vmem_limit_bytes=16 * 2**20),
        cost_estimate=pl.CostEstimate(
            flops=3 * CH * RW * LON, bytes_accessed=2 * CH * RW * LON, transcendentals=0
        ),
    )(in_hbm(tokens))


def lon_grad(cotangent, table, sums):
    return pl.pallas_call(
        lon_grad_kernel,
        name="lon_grad",
        in_specs=[HBM, HBM, VMEM],
        out_specs=[HBM, VMEM],
        out_shape=[
            pltpu.HBM(WIRE_SHAPE.shape, f32),
            jax.ShapeDtypeStruct((8, 128), f32),
        ],
        scratch_shapes=[
            pltpu.VMEM((CH, RW, LON), bf16),
            pltpu.VMEM((2, HALF, LON), bf16),
            pltpu.VMEM((PEERS, TILES, 32, 128), f32),
            pltpu.SemaphoreType.DMA((3,)),
            pltpu.SemaphoreType.DMA((2,)),
        ],
        compiler_params=pltpu.CompilerParams(vmem_limit_bytes=28 * 2**20),
        cost_estimate=LON_COST,
    )(in_hbm(cotangent), in_hbm(table), sums)


def lon_field(tokens, table, *small):
    return pl.pallas_call(
        lon_field_kernel,
        name="lon_field",
        in_specs=[VMEM, HBM] + [VMEM] * len(small),
        out_specs=[VMEM, VMEM],
        out_shape=[WIRE_SHAPE, STATS_SHAPE],
        scratch_shapes=[
            pltpu.VMEM((2, 2, HALF, HALF), bf16),
            pltpu.VMEM((2, 2, LANES, HALF), bf16),
            pltpu.SemaphoreType.DMA((2,)),
        ],
        compiler_params=pltpu.CompilerParams(vmem_limit_bytes=24 * 2**20),
        cost_estimate=LON_COST,
    )(tokens, in_hbm(table), *small)


def unpack_rows(block_ref, spread_ref, rows_ref, halves_ref, terms):
    left = jnp.concatenate([block_ref[:, t].reshape(PEERS * 8, 128) for t in range(TILES)], axis=1)
    value = None
    for _ in range(terms):
        part = left.astype(bf16)
        left = left - part.astype(f32)
        moved = dot(part, spread_ref[...])
        value = moved if value is None else value + moved
    for r in range(RW):
        rows_ref[r, 0 : PEERS * 8] = value[:, r * 128 : r * 128 + 128]
    for q in range(QB):
        for part in range(2):
            for r in range(RW):
                first = rows_ref[r, pl.ds(2 * q + part, 16, stride=8), :]
                second = rows_ref[r, pl.ds(128 + 2 * q + part, 16, stride=8), :]
                for parity, value in enumerate((first + second, first - second)):
                    high, low = split(value)
                    at = (pl.ds((part * RW + r) * 16, 16), pl.ds(q * 128, 128))
                    halves_ref[(parity, 0) + at] = high
                    halves_ref[(parity, 1) + at] = low


def pack_rows(even, odd, spread_ref, rows_ref):
    for q in range(QB):
        lanes = slice(q * 128, q * 128 + 128)
        for part in range(2):
            for r in range(RW):
                at = slice((part * RW + r) * 16, (part * RW + r + 1) * 16)
                first, second = even[at, lanes], odd[at, lanes]
                rows_ref[r, pl.ds(2 * q + part, 16, stride=8), :] = first + second
                rows_ref[r, pl.ds(128 + 2 * q + part, 16, stride=8), :] = first - second
    high, low = split(jnp.concatenate([rows_ref[r, 0 : PEERS * 8] for r in range(RW)], axis=1))
    return dot(high, spread_ref[...], NT) + dot(low, spread_ref[...], NT)


def by_frequency(even, odd):
    rows = []
    for q in range(QB):
        for value in (even, odd):
            lanes = slice(q * 128, q * 128 + 128)
            rows.append(jnp.concatenate([value[0:KB, lanes], value[KB : 2 * KB, lanes]], axis=1))
    return jnp.concatenate(rows, axis=0)


def by_part(rows):
    out = []
    for parity in range(2):
        parts = []
        for part in range(2):
            lanes = slice(part * 128, part * 128 + 128)
            parts.append(
                jnp.concatenate(
                    [rows[(2 * q + parity) * KB : (2 * q + parity + 1) * KB, lanes] for q in range(QB)],
                    axis=1,
                )
            )
        out.append(jnp.concatenate(parts, axis=0))
    return out


def lat_forward(block_ref, tab_ref, spread_ref, rows_ref, halves_ref, terms):
    unpack_rows(block_ref, spread_ref, rows_ref, halves_ref, terms)
    out = [
        dot3(
            (tab_ref[parity, 0], tab_ref[parity, 1]),
            (halves_ref[parity, 0], halves_ref[parity, 1]),
        )
        for parity in range(2)
    ]
    return by_frequency(out[0], out[1])


def lat_inverse(rows, tab_ref, spread_ref, rows_ref):
    high, low = by_part(rows[0]), by_part(rows[1])
    even, odd = [
        dot3((tab_ref[parity, 0], tab_ref[parity, 1]), (high[parity], low[parity]), TN)
        for parity in range(2)
    ]
    wire = pack_rows(even, odd, spread_ref, rows_ref)
    return [wire[:, t * 128 : t * 128 + 128].reshape(PEERS, 8, 128) for t in range(TILES)]


def fill_weight(w_ref, out_ref):
    full = jnp.zeros((256, 256), f32)
    out_ref[...] = full
    real, imag = w_ref[0, 0], w_ref[0, 1]
    out_ref[0:CH, 0:CH] = real
    out_ref[0:CH, 128 : 128 + CH] = imag
    out_ref[128 : 128 + CH, 0:CH] = -imag
    out_ref[128 : 128 + CH, 128 : 128 + CH] = real


def fill_bias(b_ref, out_ref):
    out_ref[...] = jnp.zeros((8, 256), f32)
    out_ref[0:1, 0:CH] = b_ref[0, 0:1, :]
    out_ref[0:1, 128 : 128 + CH] = b_ref[0, 1:2, :]


def grad_modes_kernel(block_ref, tab_ref, spread_ref, out_ref, rows_ref, halves_ref):
    out_ref[...] = lat_forward(block_ref, tab_ref, spread_ref, rows_ref, halves_ref, 2)


def field_modes_kernel(
    block_ref, tab_ref, spread_ref, w_in_ref, b_in_ref, w_out_ref, b_out_ref,
    back_ref, spec_ref, spec_low_ref, act_ref, act_low_ref, mask_ref,
    rows_ref, halves_ref, full_ref, weight_ref, bias_ref,
):
    @pl.when(pl.program_id(0) == 0)
    def _():
        for at, (w_ref, b_ref) in enumerate(((w_in_ref, b_in_ref), (w_out_ref, b_out_ref))):
            fill_weight(w_ref, full_ref)
            weight_ref[at, 0], weight_ref[at, 1] = split(full_ref[...])
            fill_bias(b_ref, bias_ref.at[at])

    spec = split(lat_forward(block_ref, tab_ref, spread_ref, rows_ref, halves_ref, 3))
    spec_ref[...], spec_low_ref[...] = spec
    act = dot3(spec, (weight_ref[0, 0], weight_ref[0, 1])) + bias_ref[0, 0:1, :]
    act = split(jnp.maximum(act, 0.0))
    act_ref[...], act_low_ref[...] = act
    post = dot3(act, (weight_ref[1, 0], weight_ref[1, 1])) + bias_ref[1, 0:1, :]
    mask_ref[...] = jnp.where(jnp.abs(post) > shrink_level, 1.0, 0.0).astype(bf16)
    shrunk = post - jnp.clip(post, -shrink_level, shrink_level)
    for tile, piece in enumerate(lat_inverse(split(shrunk), tab_ref, spread_ref, rows_ref)):
        back_ref[:, tile] = piece


def pull_modes_kernel(
    grad_ref, spec_ref, spec_low_ref, act_ref, act_low_ref, mask_ref, tab_ref, spread_ref,
    w_in_ref, w_out_ref, cubes_hbm,
    back_ref,
    rows_ref, full_ref, weight_ref, sum_ref,
):
    step = pl.program_id(0)

    @pl.when(step == 0)
    def _():
        for at, w_ref in enumerate((w_in_ref, w_out_ref)):
            fill_weight(w_ref, full_ref)
            weight_ref[at, 0], weight_ref[at, 1] = split(full_ref[...])
        sum_ref[...] = jnp.zeros_like(sum_ref)
        back_ref[:, PULL_ROWS - 16 :, :] = jnp.zeros((PEERS, 16, 128), f32)

    spec, act = (spec_ref[...], spec_low_ref[...]), (act_ref[...], act_low_ref[...])
    d_post = split(jnp.where(mask_ref[...].astype(f32) > 0.5, grad_ref[...], 0.0))
    sum_ref[1] += dot3(act, d_post, TN)
    d_act = dot3(d_post, (weight_ref[1, 0], weight_ref[1, 1]), NT)
    d_pre = split(jnp.where(act[0].astype(f32) > 0.0, d_act, 0.0))
    sum_ref[0] += dot3(spec, d_pre, TN)
    d_spec = dot3(d_pre, (weight_ref[0, 0], weight_ref[0, 1]), NT)
    for tile, piece in enumerate(lat_inverse(split(d_spec), tab_ref, spread_ref, rows_ref)):
        back_ref[:, pl.ds(pl.multiple_of(tile * 32 + step * 8, 8), 8), :] = piece

    @pl.when(step == STEPS - 1)
    def _():
        scale = 1.0 / math.sqrt(131072.0)
        for at in range(2):
            total = sum_ref[at] * scale
            rr, ri = total[0:CH, 0:CH], total[0:CH, 128 : 128 + CH]
            ir, ii = total[128 : 128 + CH, 0:CH], total[128 : 128 + CH, 128 : 128 + CH]
            for part, value in enumerate((rr + ii, ri - ir)):
                for k in range(8):
                    peer = (2 * at + part) * 8 + k
                    back_ref[peer, PULL_ROWS - 16 : PULL_ROWS - 4, 0:CH] = value[12 * k : 12 * k + 12]


PULL_ROWS = TILES * 32 + 16
WIRE = pl.BlockSpec((PEERS, TILES, 8, 128), lambda i: (0, 0, i, 0))
LAT_TAB = pl.BlockSpec((2, 2, 256, 256), lambda i: (0, 0, 0, 0))
MODES = pl.BlockSpec((1024, 256), lambda i: (i, 0))
SPREAD = pl.BlockSpec((LANES, RW * 128), lambda i: (0, 0))
ROWS = pltpu.VMEM((RW, PEERS * 8 + 8, 128), f32)
WEIGHT = pl.BlockSpec((1, 2, CH, CH), lambda i: (0, 0, 0, 0))
BIAS = pl.BlockSpec((1, 2, CH), lambda i: (0, 0, 0))


def modes_shape(dtype):
    return jax.ShapeDtypeStruct((4096, 256), dtype)


def grad_modes(block, table, spread):
    return pl.pallas_call(
        grad_modes_kernel,
        name="grad_modes",
        grid=(STEPS,),
        in_specs=[WIRE, LAT_TAB, SPREAD],
        out_specs=MODES,
        out_shape=modes_shape(f32),
        scratch_shapes=[ROWS, pltpu.VMEM((2, 2, 256, QB * 128), bf16)],
        compiler_params=pltpu.CompilerParams(vmem_limit_bytes=36 * 2**20),
        cost_estimate=pl.CostEstimate(
            flops=6 * 2**31, bytes_accessed=8 * 2**20, transcendentals=0
        ),
    )(block, table, spread)


def field_modes(block, table, spread, w_in, b_in, w_out, b_out):
    return pl.pallas_call(
        field_modes_kernel,
        name="field_modes",
        grid=(STEPS,),
        in_specs=[WIRE, LAT_TAB, SPREAD, WEIGHT, BIAS, WEIGHT, BIAS],
        out_specs=[WIRE] + [MODES] * 5,
        out_shape=[WIRE_SHAPE] + [modes_shape(bf16)] * 5,
        scratch_shapes=[
            ROWS,
            pltpu.VMEM((2, 2, 256, QB * 128), bf16),
            pltpu.VMEM((256, 256), f32),
            pltpu.VMEM((2, 2, 256, 256), bf16),
            pltpu.VMEM((2, 8, 256), f32),
        ],
        compiler_params=pltpu.CompilerParams(vmem_limit_bytes=36 * 2**20),
        cost_estimate=pl.CostEstimate(
            flops=12 * 2**31, bytes_accessed=14 * 2**20, transcendentals=0
        ),
    )(block, table, spread, w_in, b_in, w_out, b_out)


def pull_modes(grad, saved, table, spread, w_in, w_out, cubes):
    return pl.pallas_call(
        pull_modes_kernel,
        name="pull_modes",
        grid=(STEPS,),
        in_specs=[MODES] * 6 + [LAT_TAB, SPREAD, WEIGHT, WEIGHT, HBM],
        out_specs=pl.BlockSpec((PEERS, PULL_ROWS, 128), lambda i: (0, 0, 0)),
        out_shape=jax.ShapeDtypeStruct((PEERS, PULL_ROWS, 128), f32),
        scratch_shapes=[
            ROWS,
            pltpu.VMEM((256, 256), f32),
            pltpu.VMEM((2, 2, 256, 256), bf16),
            pltpu.VMEM((2, 256, 256), f32),
        ],
        compiler_params=pltpu.CompilerParams(vmem_limit_bytes=36 * 2**20),
        cost_estimate=pl.CostEstimate(
            flops=8 * 2**31, bytes_accessed=14 * 2**20, transcendentals=0
        ),
    )(grad, *saved, table, spread, w_in, w_out, cubes)


def lon_inverse(take, tab_ref, weighted):
    sides = []
    for parity in range(2):
        value = jnp.concatenate(
            [
                take(slice(parity * 16, parity * 16 + 16), tile).reshape(HALF, 128)
                for tile in range(TILES)
            ],
            axis=1,
        )
        if weighted:
            value = value * 2.0
            if parity == 0:
                row = lax.broadcasted_iota(jnp.int32, (HALF, 1), 0)
                value = value * jnp.where(row == 0, 0.5, 1.0)
        sides.append(dot(value.astype(bf16), tab_ref[parity], TN))
    sums, differences = sides[0] + sides[1], sides[0] - sides[1]
    return [v[:, t * 128 : t * 128 + 128] for v in (sums, differences) for t in range(4)]


def mixed_kernel(
    block_hbm, tab_ref, tok_ref, stat_ref, cubes_ref, back_hbm,
    out_hbm,
    mix_ref, block_ref, sems, out_sems,
):
    halves = [
        (block_hbm.at[pl.ds(p * 16, 16)], block_ref.at[pl.ds(p * 16, 16)]) for p in range(2)
    ]
    copies = bring(halves, sems)

    def take(peers, tile):
        if tile == 0:
            copies[0 if peers.start == 0 else 1].wait()
        return block_ref[peers, tile]

    tiles = lon_inverse(take, tab_ref, True)
    out_copies = []
    for g in range(CHUNKS):
        own = pl.ds(g * GROUP, GROUP)
        gain, shift = cubes_ref[0, own], cubes_ref[1, own]
        for tile in range(8):
            lanes = slice(tile * 128, tile * 128 + 128)
            tok = tok_ref[own, :, lanes].astype(f32)
            normed = (tok - stat_ref[0, :, lanes][None]) * stat_ref[1, :, lanes][None]
            filtered = tiles[tile][g * GROUP * RW : (g + 1) * GROUP * RW].reshape(GROUP, RW, 128)
            mix_ref[own, :, lanes] = (filtered + (normed * gain + shift) + tok).astype(bf16)
        copy = pltpu.make_async_copy(mix_ref.at[own], out_hbm.at[own], out_sems.at[g])
        copy.start()
        out_copies.append(copy)
    for copy in out_copies:
        copy.wait()


def pulled_kernel(
    block_ref, tab_ref, tok_ref, cot_ref, stat_ref, cubes_ref,
    out_ref, sum_ref, weight_ref,
):
    def take(peers, tile):
        return block_ref[peers, tile * 32 : tile * 32 + 32, :]

    tiles = lon_inverse(take, tab_ref, False)
    share = jnp.sum(block_ref[:, PULL_ROWS - 16 :, :], axis=0)
    for i in range(12):
        weight_ref[0:1, i * CH : i * CH + CH] = share[i : i + 1, 0:CH]
    for tile in range(8):
        lanes = slice(tile * 128, tile * 128 + 128)
        tok = tok_ref[:, :, lanes].astype(f32)
        inv_std = stat_ref[1, :, lanes]
        normed = (tok - stat_ref[0, :, lanes][None]) * inv_std[None]
        pulled = tiles[tile].reshape(CH, RW, 128)
        cot = cot_ref[:, :, lanes].astype(f32)
        dnorm = (pulled + cot) * cubes_ref[0]
        out_ref[:, :, lanes] = cot + inv_std[None] * dnorm
        sum_ref[0, :, lanes] = jnp.sum(dnorm, axis=0)
        sum_ref[1, :, lanes] = jnp.sum(dnorm * normed, axis=0)


def inverse_call(kernel, name, in_specs, out_specs, out_shape, scratch):
    return pl.pallas_call(
        kernel,
        name=name,
        in_specs=in_specs,
        out_specs=out_specs,
        out_shape=out_shape,
        scratch_shapes=scratch,
        compiler_params=pltpu.CompilerParams(vmem_limit_bytes=28 * 2**20),
        cost_estimate=pl.CostEstimate(
            flops=4 * LANES * LON * LON, bytes_accessed=10 * 2**20, transcendentals=0
        ),
    )


def finish_kernel(
    part_ref, tok_ref, stat_ref, one_ref, two_ref, three_ref, four_ref,
    out_hbm,
    own_ref, sems,
):
    terms = (one_ref, two_ref, three_ref, four_ref)
    count = 4.0 * CH
    mean, inv_std = stat_ref[0], stat_ref[1]
    one, two = inv_std * total(terms, 0) / count, inv_std * total(terms, 1) / count
    scale = inv_std * two
    level = one - mean * scale
    copies = []
    for g in range(CHUNKS):
        own = pl.ds(g * GROUP, GROUP)
        value = part_ref[own] - level[None] - tok_ref[own].astype(f32) * scale[None]
        own_ref[own] = value.astype(bf16)
        copy = pltpu.make_async_copy(own_ref.at[own], out_hbm.at[own], sems.at[g])
        copy.start()
        copies.append(copy)
    for copy in copies:
        copy.wait()


def finish(part, tokens, stats, terms):
    return pl.pallas_call(
        finish_kernel,
        name="finish",
        in_specs=[VMEM] * 7,
        out_specs=HBM,
        out_shape=jax.ShapeDtypeStruct((CH, RW, LON), bf16),
        scratch_shapes=[pltpu.VMEM((CH, RW, LON), bf16), pltpu.SemaphoreType.DMA((CHUNKS,))],
        compiler_params=pltpu.CompilerParams(vmem_limit_bytes=20 * 2**20),
        cost_estimate=pl.CostEstimate(
            flops=8 * CH * RW * LON, bytes_accessed=6 * 2**20, transcendentals=0
        ),
    )(part, tokens, stats, *terms)


def exchange(value):
    return lax.all_to_all(value, "lat", split_axis=0, concat_axis=0, tiled=True)


def group_terms(value):
    return [value] + [
        lax.ppermute(value, "grp", [(j, j ^ step) for j in range(4)]) for step in (1, 2, 3)
    ]


def per_device(tokens, cotangent, gain, shift, w_in, b_in, w_out, b_out):
    lon_host = lon_table()
    lon_tab, lon_high = jnp.asarray(lon_host), jnp.asarray(lon_host[:, 0])
    lat_tab, spread = jnp.asarray(lat_table()), jnp.asarray(spread_table())
    sums = token_sums(tokens)
    terms = group_terms(sums)
    spec_grad, grad_mark = lon_grad(cotangent, jnp.asarray(grad_table()), sums)
    spec_field, stats = lon_field(
        tokens,
        lon_tab,
        jnp.repeat(gain, RW).reshape(TILES, 1, 128),
        jnp.repeat(shift, RW).reshape(TILES, 1, 128),
        *terms,
        grad_mark,
    )

    modes_field = exchange(spec_field)
    modes_grad = exchange(spec_grad)
    back_field, *saved = field_modes(modes_field, lat_tab, spread, w_in, b_in, w_out, b_out)
    gain_now, shift_now, saved[0] = lax.optimization_barrier((gain, shift, saved[0]))
    cubes = jnp.stack([gain_now, shift_now]).reshape(2, CH, 1, 1)
    cubes = jnp.broadcast_to(cubes, (2, CH, 1, 128))
    rows_field = exchange(back_field)
    grad_rows = grad_modes(modes_grad, lat_tab, spread)
    back_grad = pull_modes(grad_rows, saved, lat_tab, spread, w_in, w_out, cubes)
    back_grad, rows_field = lax.optimization_barrier((back_grad, rows_field))
    rows_grad = exchange(back_grad)
    part, back, grad_weights = inverse_call(
        pulled_kernel,
        "pulled",
        [VMEM] * 6,
        [VMEM] * 3,
        [
            jax.ShapeDtypeStruct((CH, RW, LON), f32),
            STATS_SHAPE,
            jax.ShapeDtypeStruct((1, 1152), f32),
        ],
        [],
    )(rows_grad, lon_high, tokens, cotangent, stats, cubes)
    back_terms = group_terms(back)
    mixed = inverse_call(
        mixed_kernel,
        "mixed",
        [HBM, VMEM, VMEM, VMEM, VMEM, HBM],
        HBM,
        jax.ShapeDtypeStruct((CH, RW, LON), bf16),
        [
            pltpu.VMEM((CH, RW, LON), bf16),
            pltpu.VMEM((PEERS, TILES, 32, 128), f32),
            pltpu.SemaphoreType.DMA((2,)),
            pltpu.SemaphoreType.DMA((CHUNKS,)),
        ],
    )(in_hbm(rows_field), lon_high, tokens, stats, cubes, back)
    grad_tokens = finish(part, tokens, stats, back_terms)
    return (mixed, grad_tokens, grad_weights)


def solution(mesh):
    in_specs = (
        P("grp", "lat", None),
        P("grp", "lat", None),
        P("grp"),
        P("grp"),
        P("grp", None, None, None),
        P("grp", None, None),
        P("grp", None, None, None),
        P("grp", None, None),
    )
    out_specs = (P("grp", "lat", None), P("grp", "lat", None), P("grp", "lat"))
    return jax.shard_map(
        per_device, mesh=mesh, in_specs=in_specs, out_specs=out_specs, check_vma=False
    )
```

```python
import functools
import math

import jax
import jax.numpy as jnp
import ml_dtypes
import numpy as np
from jax import lax
from jax.experimental import pallas as pl
from jax.experimental.pallas import tpu as pltpu
from jax.sharding import PartitionSpec as P

shrink_level = 0.01
norm_eps = 1e-05
f32 = jnp.float32
bf16 = jnp.bfloat16

CH = 96
RW = 8
LON = 1024
HALF = 512
PEERS = 32
LANES = RW * CH
QB = 4
KB = 128
STEPS = 4
TILES = LANES // 128
WIRE_SHAPE = jax.ShapeDtypeStruct((PEERS, TILES, 32, 128), jnp.float32)


def host_split(table):
    high = table.astype(ml_dtypes.bfloat16)
    low = (table - high.astype(np.float64)).astype(ml_dtypes.bfloat16)
    return np.stack([high, low])


def lon_table():
    parts = []
    n = np.arange(HALF)
    for parity in range(2):
        m = 2 * np.arange(256) + parity
        theta = 2.0 * np.pi * ((m[:, None] * n[None, :]) % LON) / LON
        table = np.stack([np.cos(theta), -np.sin(theta)], axis=1).reshape(HALF, HALF)
        parts.append(host_split(table / 32.0))
    return np.stack(parts)


def grad_table():
    parts = []
    n = np.arange(LON)
    for parity in range(2):
        m = 2 * np.arange(256) + parity
        theta = 2.0 * np.pi * ((m[:, None] * n[None, :]) % LON) / LON
        table = np.stack([np.cos(theta), -np.sin(theta)], axis=1)
        table = table * np.where(m == 0, 1.0, 2.0)[:, None, None]
        parts.append(host_split(table.reshape(HALF, LON) / 32.0)[0])
    return np.stack(parts)


def lat_table():
    parts = []
    row = np.arange(RW)[:, None]
    peer = np.arange(16)[None, :]
    place = (8 * peer + row).reshape(-1)
    for parity in range(2):
        k = 2 * np.arange(KB) + parity
        theta = 2.0 * np.pi * ((k[:, None] * place[None, :]) % 256) / 256
        c, s = np.cos(theta), np.sin(theta)
        table = np.concatenate(
            [np.concatenate([c, s], axis=1), np.concatenate([-s, c], axis=1)], axis=0
        )
        parts.append(host_split(table / 16.0))
    return np.stack(parts)


def spread_table():
    table = np.zeros((LANES, RW * 128), ml_dtypes.bfloat16)
    channel, row = np.divmod(np.arange(LANES), RW)
    table[np.arange(LANES), row * 128 + channel] = 1
    return table


def split(value):
    high = value.astype(bf16)
    low = (value - high.astype(f32)).astype(bf16)
    return high, low


def dot(left, right, dims=((1,), (0,))):
    return lax.dot_general(left, right, (dims, ((), ())), preferred_element_type=f32)


NT = ((1,), (1,))
TN = ((0,), (0,))


def dot3(left, right, dims=((1,), (0,))):
    return (
        dot(left[0], right[0], dims) + dot(left[0], right[1], dims) + dot(left[1], right[0], dims)
    )


def in_hbm(value):
    return pltpu.with_memory_space_constraint(value, pltpu.HBM)


CHUNKS = 4
GROUP = CH // CHUNKS


def bring(pairs, sems):
    copies = [pltpu.make_async_copy(src, dst, sems.at[i]) for i, (src, dst) in enumerate(pairs)]
    for copy in copies:
        copy.start()
    return copies


def sums_kernel(x_hbm, out_ref, x_ref, sems):
    parts = [pl.ds(g * GROUP, GROUP) for g in range(CHUNKS)]
    copies = bring([(x_hbm.at[own], x_ref.at[own]) for own in parts], sems)
    for g, own in enumerate(parts):
        copies[g].wait()
        for tile in range(8):
            lanes = slice(tile * 128, tile * 128 + 128)
            value = x_ref[own, :, lanes].astype(f32)
            for at, term in enumerate((value, value * value)):
                term = jnp.sum(term, axis=0)
                out_ref[at, :, lanes] = term if g == 0 else out_ref[at, :, lanes] + term


def lon_grad_kernel(
    x_hbm, tab_hbm, sums_ref,
    out_hbm, mark_ref,
    x_ref, tab_ref, wire_ref, in_sems, out_sems,
):
    pairs = [(x_hbm, x_ref)] + [(tab_hbm.at[p], tab_ref.at[p]) for p in range(2)]
    copies = [pltpu.make_async_copy(src, dst, in_sems.at[i]) for i, (src, dst) in enumerate(pairs)]
    copies[0].start()
    copies[1].start()
    mark_ref[...] = jnp.zeros((8, 128), f32)
    out_copies = []
    copies[0].wait()
    copies[2].start()
    for parity in range(2):
        copies[1 + parity].wait()
        value = dot(tab_ref[parity], x_ref[...].reshape(LANES, LON), NT)
        own = pl.ds(parity * 16, 16)
        for tile in range(TILES):
            piece = value[:, tile * 128 : tile * 128 + 128]
            wire_ref[own, tile] = piece.reshape(16, 32, 128)
        copy = pltpu.make_async_copy(wire_ref.at[own], out_hbm.at[own], out_sems.at[parity])
        copy.start()
        out_copies.append(copy)
    for copy in out_copies:
        copy.wait()


def total(terms, at):
    return terms[0][at] + terms[1][at] + terms[2][at] + terms[3][at]


def lon_field_kernel(
    x_ref, tab_hbm, gain_ref, shift_ref, one_ref, two_ref, three_ref, four_ref, mark_ref,
    out_ref, stat_ref,
    tab_ref, halves_ref, tab_sems,
):
    tab_copies = bring([(tab_hbm.at[p], tab_ref.at[p]) for p in range(2)], tab_sems)
    terms = (one_ref, two_ref, three_ref, four_ref)
    count = 4.0 * CH
    mean = total(terms, 0) / count
    inv_std = lax.rsqrt(total(terms, 1) / count - mean * mean + norm_eps)
    stat_ref[0], stat_ref[1] = mean, inv_std
    for tile in range(4):
        pair = []
        for start in (tile * 128, HALF + tile * 128):
            lanes = slice(start, start + 128)
            value = x_ref[:, :, lanes].astype(f32)
            value = (value - mean[:, lanes][None]) * inv_std[:, lanes][None]
            pair.append(value.reshape(LANES, 128))
        for parity, value in enumerate((pair[0] + pair[1], pair[0] - pair[1])):
            high, low = split(value)
            halves_ref[parity, 0, :, tile * 128 : tile * 128 + 128] = high
            halves_ref[parity, 1, :, tile * 128 : tile * 128 + 128] = low
    for parity in range(2):
        tab_copies[parity].wait()
        both = dot(tab_ref[parity].reshape(2 * HALF, HALF), halves_ref[parity, 0], NT)
        value = both[:HALF] + both[HALF:] + dot(tab_ref[parity, 0], halves_ref[parity, 1], NT)
        for tile in range(TILES):
            piece = value[:, tile * 128 : tile * 128 + 128] * gain_ref[tile]
            out_ref[pl.ds(parity * 16, 16), tile] = piece.reshape(16, 32, 128)
    for tile in range(TILES):
        out_ref[0, tile, 0:1, :] = out_ref[0, tile, 0:1, :] + shift_ref[tile] * 32.0


VMEM = pl.BlockSpec(memory_space=pltpu.VMEM)
HBM = pl.BlockSpec(memory_space=pltpu.HBM)
STATS_SHAPE = jax.ShapeDtypeStruct((2, RW, LON), f32)
LON_COST = pl.CostEstimate(
    flops=6 * LANES * LON * LON, bytes_accessed=7 * 2**20, transcendentals=0
)


def token_sums(tokens):
    return pl.pallas_call(
        sums_kernel,
        name="token_sums",
        in_specs=[HBM],
        out_specs=VMEM,
        out_shape=STATS_SHAPE,
        scratch_shapes=[pltpu.VMEM((CH, RW, LON), bf16), pltpu.SemaphoreType.DMA((CHUNKS,))],
        compiler_params=pltpu.CompilerParams(vmem_limit_bytes=16 * 2**20),
        cost_estimate=pl.CostEstimate(
            flops=3 * CH * RW * LON, bytes_accessed=2 * CH * RW * LON, transcendentals=0
        ),
    )(in_hbm(tokens))


def lon_grad(cotangent, table, sums):
    return pl.pallas_call(
        lon_grad_kernel,
        name="lon_grad",
        in_specs=[HBM, HBM, VMEM],
        out_specs=[HBM, VMEM],
        out_shape=[
            pltpu.HBM(WIRE_SHAPE.shape, f32),
            jax.ShapeDtypeStruct((8, 128), f32),
        ],
        scratch_shapes=[
            pltpu.VMEM((CH, RW, LON), bf16),
            pltpu.VMEM((2, HALF, LON), bf16),
            pltpu.VMEM((PEERS, TILES, 32, 128), f32),
            pltpu.SemaphoreType.DMA((3,)),
            pltpu.SemaphoreType.DMA((2,)),
        ],
        compiler_params=pltpu.CompilerParams(vmem_limit_bytes=28 * 2**20),
        cost_estimate=LON_COST,
    )(in_hbm(cotangent), in_hbm(table), sums)


def lon_field(tokens, table, *small):
    return pl.pallas_call(
        lon_field_kernel,
        name="lon_field",
        in_specs=[VMEM, HBM] + [VMEM] * len(small),
        out_specs=[VMEM, VMEM],
        out_shape=[WIRE_SHAPE, STATS_SHAPE],
        scratch_shapes=[
            pltpu.VMEM((2, 2, HALF, HALF), bf16),
            pltpu.VMEM((2, 2, LANES, HALF), bf16),
            pltpu.SemaphoreType.DMA((2,)),
        ],
        compiler_params=pltpu.CompilerParams(vmem_limit_bytes=24 * 2**20),
        cost_estimate=LON_COST,
    )(tokens, in_hbm(table), *small)


def unpack_rows(block_ref, spread_ref, rows_ref, halves_ref, terms):
    left = jnp.concatenate([block_ref[:, t].reshape(PEERS * 8, 128) for t in range(TILES)], axis=1)
    value = None
    for _ in range(terms):
        part = left.astype(bf16)
        left = left - part.astype(f32)
        moved = dot(part, spread_ref[...])
        value = moved if value is None else value + moved
    for r in range(RW):
        rows_ref[r, 0 : PEERS * 8] = value[:, r * 128 : r * 128 + 128]
    for q in range(QB):
        for part in range(2):
            for r in range(RW):
                first = rows_ref[r, pl.ds(2 * q + part, 16, stride=8), :]
                second = rows_ref[r, pl.ds(128 + 2 * q + part, 16, stride=8), :]
                for parity, value in enumerate((first + second, first - second)):
                    high, low = split(value)
                    at = (pl.ds((part * RW + r) * 16, 16), pl.ds(q * 128, 128))
                    halves_ref[(parity, 0) + at] = high
                    halves_ref[(parity, 1) + at] = low


def pack_rows(even, odd, spread_ref, rows_ref):
    for q in range(QB):
        lanes = slice(q * 128, q * 128 + 128)
        for part in range(2):
            for r in range(RW):
                at = slice((part * RW + r) * 16, (part * RW + r + 1) * 16)
                first, second = even[at, lanes], odd[at, lanes]
                rows_ref[r, pl.ds(2 * q + part, 16, stride=8), :] = first + second
                rows_ref[r, pl.ds(128 + 2 * q + part, 16, stride=8), :] = first - second
    high, low = split(jnp.concatenate([rows_ref[r, 0 : PEERS * 8] for r in range(RW)], axis=1))
    return dot(high, spread_ref[...], NT) + dot(low, spread_ref[...], NT)


def by_frequency(even, odd):
    rows = []
    for q in range(QB):
        for value in (even, odd):
            lanes = slice(q * 128, q * 128 + 128)
            rows.append(jnp.concatenate([value[0:KB, lanes], value[KB : 2 * KB, lanes]], axis=1))
    return jnp.concatenate(rows, axis=0)


def by_part(rows):
    out = []
    for parity in range(2):
        parts = []
        for part in range(2):
            lanes = slice(part * 128, part * 128 + 128)
            parts.append(
                jnp.concatenate(
                    [rows[(2 * q + parity) * KB : (2 * q + parity + 1) * KB, lanes] for q in range(QB)],
                    axis=1,
                )
            )
        out.append(jnp.concatenate(parts, axis=0))
    return out


def lat_forward(block_ref, tab_ref, spread_ref, rows_ref, halves_ref, terms):
    unpack_rows(block_ref, spread_ref, rows_ref, halves_ref, terms)
    out = [
        dot3(
            (tab_ref[parity, 0], tab_ref[parity, 1]),
            (halves_ref[parity, 0], halves_ref[parity, 1]),
        )
        for parity in range(2)
    ]
    return by_frequency(out[0], out[1])


def lat_inverse(rows, tab_ref, spread_ref, rows_ref):
    high, low = by_part(rows[0]), by_part(rows[1])
    even, odd = [
        dot3((tab_ref[parity, 0], tab_ref[parity, 1]), (high[parity], low[parity]), TN)
        for parity in range(2)
    ]
    wire = pack_rows(even, odd, spread_ref, rows_ref)
    return [wire[:, t * 128 : t * 128 + 128].reshape(PEERS, 8, 128) for t in range(TILES)]


def fill_weight(w_ref, out_ref):
    full = jnp.zeros((256, 256), f32)
    out_ref[...] = full
    real, imag = w_ref[0, 0], w_ref[0, 1]
    out_ref[0:CH, 0:CH] = real
    out_ref[0:CH, 128 : 128 + CH] = imag
    out_ref[128 : 128 + CH, 0:CH] = -imag
    out_ref[128 : 128 + CH, 128 : 128 + CH] = real


def fill_bias(b_ref, out_ref):
    out_ref[...] = jnp.zeros((8, 256), f32)
    out_ref[0:1, 0:CH] = b_ref[0, 0:1, :]
    out_ref[0:1, 128 : 128 + CH] = b_ref[0, 1:2, :]


def grad_modes_kernel(block_ref, tab_ref, spread_ref, out_ref, rows_ref, halves_ref):
    out_ref[...] = lat_forward(block_ref, tab_ref, spread_ref, rows_ref, halves_ref, 2)


def field_modes_kernel(
    block_ref, tab_ref, spread_ref, w_in_ref, b_in_ref, w_out_ref, b_out_ref,
    back_ref, spec_ref, spec_low_ref, act_ref, act_low_ref, mask_ref,
    rows_ref, halves_ref, full_ref, weight_ref, bias_ref,
):
    @pl.when(pl.program_id(0) == 0)
    def _():
        for at, (w_ref, b_ref) in enumerate(((w_in_ref, b_in_ref), (w_out_ref, b_out_ref))):
            fill_weight(w_ref, full_ref)
            weight_ref[at, 0], weight_ref[at, 1] = split(full_ref[...])
            fill_bias(b_ref, bias_ref.at[at])

    spec = split(lat_forward(block_ref, tab_ref, spread_ref, rows_ref, halves_ref, 3))
    spec_ref[...], spec_low_ref[...] = spec
    act = dot3(spec, (weight_ref[0, 0], weight_ref[0, 1])) + bias_ref[0, 0:1, :]
    act = split(jnp.maximum(act, 0.0))
    act_ref[...], act_low_ref[...] = act
    post = dot3(act, (weight_ref[1, 0], weight_ref[1, 1])) + bias_ref[1, 0:1, :]
    mask_ref[...] = jnp.where(jnp.abs(post) > shrink_level, 1.0, 0.0).astype(bf16)
    shrunk = post - jnp.clip(post, -shrink_level, shrink_level)
    for tile, piece in enumerate(lat_inverse(split(shrunk), tab_ref, spread_ref, rows_ref)):
        back_ref[:, tile] = piece


def pull_modes_kernel(
    grad_ref, spec_ref, spec_low_ref, act_ref, act_low_ref, mask_ref, tab_ref, spread_ref,
    w_in_ref, w_out_ref, cubes_hbm,
    back_ref,
    rows_ref, full_ref, weight_ref, sum_ref,
):
    step = pl.program_id(0)

    @pl.when(step == 0)
    def _():
        for at, w_ref in enumerate((w_in_ref, w_out_ref)):
            fill_weight(w_ref, full_ref)
            weight_ref[at, 0], weight_ref[at, 1] = split(full_ref[...])
        sum_ref[...] = jnp.zeros_like(sum_ref)
        back_ref[:, PULL_ROWS - 16 :, :] = jnp.zeros((PEERS, 16, 128), f32)

    spec, act = (spec_ref[...], spec_low_ref[...]), (act_ref[...], act_low_ref[...])
    d_post = split(jnp.where(mask_ref[...].astype(f32) > 0.5, grad_ref[...], 0.0))
    sum_ref[1] += dot3(act, d_post, TN)
    d_act = dot3(d_post, (weight_ref[1, 0], weight_ref[1, 1]), NT)
    d_pre = split(jnp.where(act[0].astype(f32) > 0.0, d_act, 0.0))
    sum_ref[0] += dot3(spec, d_pre, TN)
    d_spec = dot3(d_pre, (weight_ref[0, 0], weight_ref[0, 1]), NT)
    for tile, piece in enumerate(lat_inverse(split(d_spec), tab_ref, spread_ref, rows_ref)):
        back_ref[:, pl.ds(pl.multiple_of(tile * 32 + step * 8, 8), 8), :] = piece

    @pl.when(step == STEPS - 1)
    def _():
        scale = 1.0 / math.sqrt(131072.0)
        for at in range(2):
            total = sum_ref[at] * scale
            rr, ri = total[0:CH, 0:CH], total[0:CH, 128 : 128 + CH]
            ir, ii = total[128 : 128 + CH, 0:CH], total[128 : 128 + CH, 128 : 128 + CH]
            for part, value in enumerate((rr + ii, ri - ir)):
                for k in range(8):
                    peer = (2 * at + part) * 8 + k
                    back_ref[peer, PULL_ROWS - 16 : PULL_ROWS - 4, 0:CH] = value[12 * k : 12 * k + 12]


PULL_ROWS = TILES * 32 + 16
WIRE = pl.BlockSpec((PEERS, TILES, 8, 128), lambda i: (0, 0, i, 0))
LAT_TAB = pl.BlockSpec((2, 2, 256, 256), lambda i: (0, 0, 0, 0))
MODES = pl.BlockSpec((1024, 256), lambda i: (i, 0))
SPREAD = pl.BlockSpec((LANES, RW * 128), lambda i: (0, 0))
ROWS = pltpu.VMEM((RW, PEERS * 8 + 8, 128), f32)
WEIGHT = pl.BlockSpec((1, 2, CH, CH), lambda i: (0, 0, 0, 0))
BIAS = pl.BlockSpec((1, 2, CH), lambda i: (0, 0, 0))


def modes_shape(dtype):
    return jax.ShapeDtypeStruct((4096, 256), dtype)


def grad_modes(block, table, spread):
    return pl.pallas_call(
        grad_modes_kernel,
        name="grad_modes",
        grid=(STEPS,),
        in_specs=[WIRE, LAT_TAB, SPREAD],
        out_specs=MODES,
        out_shape=modes_shape(f32),
        scratch_shapes=[ROWS, pltpu.VMEM((2, 2, 256, QB * 128), bf16)],
        compiler_params=pltpu.CompilerParams(vmem_limit_bytes=36 * 2**20),
        cost_estimate=pl.CostEstimate(
            flops=6 * 2**31, bytes_accessed=8 * 2**20, transcendentals=0
        ),
    )(block, table, spread)


def field_modes(block, table, spread, w_in, b_in, w_out, b_out):
    return pl.pallas_call(
        field_modes_kernel,
        name="field_modes",
        grid=(STEPS,),
        in_specs=[WIRE, LAT_TAB, SPREAD, WEIGHT, BIAS, WEIGHT, BIAS],
        out_specs=[WIRE] + [MODES] * 5,
        out_shape=[WIRE_SHAPE] + [modes_shape(bf16)] * 5,
        scratch_shapes=[
            ROWS,
            pltpu.VMEM((2, 2, 256, QB * 128), bf16),
            pltpu.VMEM((256, 256), f32),
            pltpu.VMEM((2, 2, 256, 256), bf16),
            pltpu.VMEM((2, 8, 256), f32),
        ],
        compiler_params=pltpu.CompilerParams(vmem_limit_bytes=36 * 2**20),
        cost_estimate=pl.CostEstimate(
            flops=12 * 2**31, bytes_accessed=14 * 2**20, transcendentals=0
        ),
    )(block, table, spread, w_in, b_in, w_out, b_out)


def pull_modes(grad, saved, table, spread, w_in, w_out, cubes):
    return pl.pallas_call(
        pull_modes_kernel,
        name="pull_modes",
        grid=(STEPS,),
        in_specs=[MODES] * 6 + [LAT_TAB, SPREAD, WEIGHT, WEIGHT, HBM],
        out_specs=pl.BlockSpec((PEERS, PULL_ROWS, 128), lambda i: (0, 0, 0)),
        out_shape=jax.ShapeDtypeStruct((PEERS, PULL_ROWS, 128), f32),
        scratch_shapes=[
            ROWS,
            pltpu.VMEM((256, 256), f32),
            pltpu.VMEM((2, 2, 256, 256), bf16),
            pltpu.VMEM((2, 256, 256), f32),
        ],
        compiler_params=pltpu.CompilerParams(vmem_limit_bytes=36 * 2**20),
        cost_estimate=pl.CostEstimate(
            flops=8 * 2**31, bytes_accessed=14 * 2**20, transcendentals=0
        ),
    )(grad, *saved, table, spread, w_in, w_out, cubes)


def lon_inverse(take, tab_ref, weighted):
    sides = []
    for parity in range(2):
        value = jnp.concatenate(
            [
                take(slice(parity * 16, parity * 16 + 16), tile).reshape(HALF, 128)
                for tile in range(TILES)
            ],
            axis=1,
        )
        if weighted:
            value = value * 2.0
            if parity == 0:
                row = lax.broadcasted_iota(jnp.int32, (HALF, 1), 0)
                value = value * jnp.where(row == 0, 0.5, 1.0)
        sides.append(dot(value.astype(bf16), tab_ref[parity], TN))
    sums, differences = sides[0] + sides[1], sides[0] - sides[1]
    return [v[:, t * 128 : t * 128 + 128] for v in (sums, differences) for t in range(4)]


def mixed_kernel(
    block_hbm, tab_ref, tok_ref, stat_ref, cubes_ref, back_hbm,
    out_hbm,
    mix_ref, block_ref, sems, out_sems,
):
    halves = [
        (block_hbm.at[pl.ds(p * 16, 16)], block_ref.at[pl.ds(p * 16, 16)]) for p in range(2)
    ]
    copies = bring(halves, sems)

    def take(peers, tile):
        if tile == 0:
            copies[0 if peers.start == 0 else 1].wait()
        return block_ref[peers, tile]

    tiles = lon_inverse(take, tab_ref, True)
    out_copies = []
    for g in range(CHUNKS):
        own = pl.ds(g * GROUP, GROUP)
        gain, shift = cubes_ref[0, own], cubes_ref[1, own]
        for tile in range(8):
            lanes = slice(tile * 128, tile * 128 + 128)
            tok = tok_ref[own, :, lanes].astype(f32)
            normed = (tok - stat_ref[0, :, lanes][None]) * stat_ref[1, :, lanes][None]
            filtered = tiles[tile][g * GROUP * RW : (g + 1) * GROUP * RW].reshape(GROUP, RW, 128)
            mix_ref[own, :, lanes] = (filtered + (normed * gain + shift) + tok).astype(bf16)
        copy = pltpu.make_async_copy(mix_ref.at[own], out_hbm.at[own], out_sems.at[g])
        copy.start()
        out_copies.append(copy)
    for copy in out_copies:
        copy.wait()


def pulled_kernel(
    block_ref, tab_ref, tok_ref, cot_ref, stat_ref, cubes_ref,
    out_ref, sum_ref, weight_ref,
):
    def take(peers, tile):
        return block_ref[peers, tile * 32 : tile * 32 + 32, :]

    tiles = lon_inverse(take, tab_ref, False)
    share = jnp.sum(block_ref[:, PULL_ROWS - 16 :, :], axis=0)
    for i in range(12):
        weight_ref[0:1, i * CH : i * CH + CH] = share[i : i + 1, 0:CH]
    for tile in range(8):
        lanes = slice(tile * 128, tile * 128 + 128)
        tok = tok_ref[:, :, lanes].astype(f32)
        inv_std = stat_ref[1, :, lanes]
        normed = (tok - stat_ref[0, :, lanes][None]) * inv_std[None]
        pulled = tiles[tile].reshape(CH, RW, 128)
        cot = cot_ref[:, :, lanes].astype(f32)
        dnorm = (pulled + cot) * cubes_ref[0]
        out_ref[:, :, lanes] = cot + inv_std[None] * dnorm
        sum_ref[0, :, lanes] = jnp.sum(dnorm, axis=0)
        sum_ref[1, :, lanes] = jnp.sum(dnorm * normed, axis=0)


def inverse_call(kernel, name, in_specs, out_specs, out_shape, scratch):
    return pl.pallas_call(
        kernel,
        name=name,
        in_specs=in_specs,
        out_specs=out_specs,
        out_shape=out_shape,
        scratch_shapes=scratch,
        compiler_params=pltpu.CompilerParams(vmem_limit_bytes=28 * 2**20),
        cost_estimate=pl.CostEstimate(
            flops=4 * LANES * LON * LON, bytes_accessed=10 * 2**20, transcendentals=0
        ),
    )


def finish_kernel(
    part_ref, tok_ref, stat_ref, one_ref, two_ref, three_ref, four_ref,
    out_hbm,
    own_ref, sems,
):
    terms = (one_ref, two_ref, three_ref, four_ref)
    count = 4.0 * CH
    mean, inv_std = stat_ref[0], stat_ref[1]
    one, two = inv_std * total(terms, 0) / count, inv_std * total(terms, 1) / count
    scale = inv_std * two
    level = one - mean * scale
    copies = []
    for g in range(CHUNKS):
        own = pl.ds(g * GROUP, GROUP)
        value = part_ref[own] - level[None] - tok_ref[own].astype(f32) * scale[None]
        own_ref[own] = value.astype(bf16)
        copy = pltpu.make_async_copy(own_ref.at[own], out_hbm.at[own], sems.at[g])
        copy.start()
        copies.append(copy)
    for copy in copies:
        copy.wait()


def finish(part, tokens, stats, terms):
    return pl.pallas_call(
        finish_kernel,
        name="finish",
        in_specs=[VMEM] * 7,
        out_specs=HBM,
        out_shape=jax.ShapeDtypeStruct((CH, RW, LON), bf16),
        scratch_shapes=[pltpu.VMEM((CH, RW, LON), bf16), pltpu.SemaphoreType.DMA((CHUNKS,))],
        compiler_params=pltpu.CompilerParams(vmem_limit_bytes=20 * 2**20),
        cost_estimate=pl.CostEstimate(
            flops=8 * CH * RW * LON, bytes_accessed=6 * 2**20, transcendentals=0
        ),
    )(part, tokens, stats, *terms)


def exchange(value):
    return lax.all_to_all(value, "lat", split_axis=0, concat_axis=0, tiled=True)


def group_terms(value):
    return [value] + [
        lax.ppermute(value, "grp", [(j, j ^ step) for j in range(4)]) for step in (1, 2, 3)
    ]


def per_device(tokens, cotangent, gain, shift, w_in, b_in, w_out, b_out):
    lon_host = lon_table()
    lon_tab, lon_high = jnp.asarray(lon_host), jnp.asarray(lon_host[:, 0])
    lat_tab, spread = jnp.asarray(lat_table()), jnp.asarray(spread_table())
    sums = token_sums(tokens)
    terms = group_terms(sums)
    spec_grad, grad_mark = lon_grad(cotangent, jnp.asarray(grad_table()), sums)
    spec_field, stats = lon_field(
        tokens,
        lon_tab,
        jnp.repeat(gain, RW).reshape(TILES, 1, 128),
        jnp.repeat(shift, RW).reshape(TILES, 1, 128),
        *terms,
        grad_mark,
    )

    modes_field = exchange(spec_field)
    modes_grad = exchange(spec_grad)
    back_field, *saved = field_modes(modes_field, lat_tab, spread, w_in, b_in, w_out, b_out)
    gain_now, shift_now, saved[0] = lax.optimization_barrier((gain, shift, saved[0]))
    cubes = jnp.stack([gain_now, shift_now]).reshape(2, CH, 1, 1)
    cubes = jnp.broadcast_to(cubes, (2, CH, 1, 128))
    rows_field = exchange(back_field)
    grad_rows = grad_modes(modes_grad, lat_tab, spread)
    back_grad = pull_modes(grad_rows, saved, lat_tab, spread, w_in, w_out, cubes)
    back_grad, rows_field = lax.optimization_barrier((back_grad, rows_field))
    rows_grad = exchange(back_grad)
    part, back, grad_weights = inverse_call(
        pulled_kernel,
        "pulled",
        [VMEM] * 6,
        [VMEM] * 3,
        [
            jax.ShapeDtypeStruct((CH, RW, LON), f32),
            STATS_SHAPE,
            jax.ShapeDtypeStruct((1, 1152), f32),
        ],
        [],
    )(rows_grad, lon_high, tokens, cotangent, stats, cubes)
    back_terms = group_terms(back)
    mixed = inverse_call(
        mixed_kernel,
        "mixed",
        [HBM, VMEM, VMEM, VMEM, VMEM, HBM],
        HBM,
        jax.ShapeDtypeStruct((CH, RW, LON), bf16),
        [
            pltpu.VMEM((CH, RW, LON), bf16),
            pltpu.VMEM((PEERS, TILES, 32, 128), f32),
            pltpu.SemaphoreType.DMA((2,)),
            pltpu.SemaphoreType.DMA((CHUNKS,)),
        ],
    )(in_hbm(rows_field), lon_high, tokens, stats, cubes, back)
    grad_tokens = finish(part, tokens, stats, back_terms)
    return (mixed, grad_tokens, grad_weights)


def solution(mesh):
    in_specs = (
        P("grp", "lat", None),
        P("grp", "lat", None),
        P("grp"),
        P("grp"),
        P("grp", None, None, None),
        P("grp", None, None),
        P("grp", None, None, None),
        P("grp", None, None),
    )
    out_specs = (P("grp", "lat", None), P("grp", "lat", None), P("grp", "lat"))
    return jax.shard_map(
        per_device, mesh=mesh, in_specs=in_specs, out_specs=out_specs, check_vma=False
    )
```
